32 devices in a mesh: dp: 8 (over y, x, core), tensor: 4 (over z).
Axes of the slice: x: 2, y: 2, z: 4, core: 2. Of those that a mesh axis runs over, the one named last changes fastest.
Arguments:
- tokens: bfloat16 [20480, 1024], P(('dp', 'tensor')), may hold values from -6 to 6
- lengths: int32 [8, 2], P('dp'), may hold values from 1024 to 1536, as said below
- row_order: int32 [8, 2560], P('dp'), may hold values from 0 to 2559, each once within a row
- attention_gain: bfloat16 [1024], P('dp'), may hold values from 0.099609375 to 1.8984375
- query_gain: bfloat16 [128], P('dp'), may hold values from 0.796875 to 1.796875
- key_gain: bfloat16 [128], P('dp'), may hold values from 0.796875 to 1.796875
- query_weight: bfloat16 [1024, 2048], P('dp', 'tensor'), may hold values from -0.1875 to 0.1875
- key_matrix: bfloat16 [1024, 1024], P('dp', 'tensor'), may hold values from -0.1875 to 0.1875
- value_matrix: bfloat16 [1024, 1024], P('dp', 'tensor'), may hold values from -0.1875 to 0.1875
- output_weight: bfloat16 [2048, 1024], P('tensor', 'dp'), may hold values from -1 to 1
- feedforward_gain: bfloat16 [1024], P('dp'), may hold values from 0.099609375 to 1.8984375
- gate_weight: bfloat16 [1024, 3072], P('dp', 'tensor'), may hold values from -0.1875 to 0.1875
- up_weight: bfloat16 [1024, 3072], P('dp', 'tensor'), may hold values from -0.1875 to 0.1875
- down_weight: bfloat16 [3072, 1024], P('tensor', 'dp'), may hold values from -0.109375 to 0.109375
- cotangent: bfloat16 [20480, 1024], P(('dp', 'tensor')), may hold values from -6 to 6
Outputs:
- layer_output: bfloat16 [20480, 1024], P(('dp', 'tensor'))
- input_grad: bfloat16 [20480, 1024], P(('dp', 'tensor'))
- attention_gain_grad: float32 [1024], P('dp')
- query_gain_grad: float32 [128], P('dp')
- key_gain_grad: float32 [128], P('dp')
- query_weight_grad: float32 [1024, 2048], P('dp', 'tensor')
- key_weight_grad: float32 [1024, 1024], P('dp', 'tensor')
- value_weight_grad: float32 [1024, 1024], P('dp', 'tensor')
- output_weight_grad: float32 [2048, 1024], P('tensor', 'dp')
- feedforward_gain_grad: float32 [1024], P('dp')
- gate_weight_grad: float32 [1024, 3072], P('dp', 'tensor')
- up_weight_grad: float32 [1024, 3072], P('dp', 'tensor')
- down_weight_grad: float32 [3072, 1024], P('tensor', 'dp')
The draws below stay inside these ranges and needn't reach their ends.
Inputs may be any that keep to these rules, and one draw needn't show every extreme that they name: Each row of lengths holds the lengths of the 2 sequences that fill one group's 2560 tokens. Each row of row_order holds every place of 0 to 2559 once.
All inputs are finite; a program needn't handle non-finite values.
Results may differ from the reference program's by a relative error of at most 0.025.
Values may be sent and summed in bfloat16 or wider, within the bound.
A program may use at most 256 MiB of HBM per device.

```python
import jax
import jax.numpy as jnp
from jax import lax

MODEL_WIDTH = 1024
QUERY_HEADS = 16
KEY_VALUE_HEADS = 8
HEAD_SIZE = 128
FF = 3072
GROUP_TOKENS = 2560
MIN_LEN = 1024
DOCS = 2
TOKENS = 20480
N_DP = 8


def draw_lengths(key, part):
    key = jax.random.fold_in(key, 11)
    extra = GROUP_TOKENS - DOCS * MIN_LEN
    cut_key, group_key, place_key = jax.random.split(key, 3)
    cuts = jnp.sort(jax.random.randint(cut_key, (N_DP, DOCS - 1), 0, extra + 1), axis=1)
    bounds = jnp.concatenate([jnp.zeros((N_DP, 1), jnp.int32), cuts.astype(jnp.int32), jnp.full((N_DP, 1), extra, jnp.int32)], axis=1)
    pieces = bounds[:, 1:] - bounds[:, :-1]
    chosen = jax.random.randint(group_key, (), 0, N_DP)
    which = jax.random.randint(place_key, (), 0, DOCS)
    filled = jnp.where(jnp.arange(DOCS, dtype=jnp.int32) == which, extra, 0).astype(jnp.int32)
    pieces = jnp.where((jnp.arange(N_DP, dtype=jnp.int32) == chosen)[:, None], filled[None, :], pieces)
    return (pieces + MIN_LEN).astype(jnp.int32)


def spiked(drawn, own_key, source, target, blocks, factor):
    def block_of(dim):
        return (jnp.arange(drawn.shape[dim]) // (drawn.shape[dim] // blocks)).reshape((-1,) + (1,) * (drawn.ndim - 1 - dim))

    first = jax.random.permutation(own_key, blocks)[block_of(target)]
    other_side = (block_of(target) + blocks // 2) % blocks
    return jnp.where((block_of(source) == first) | (block_of(source) == other_side), factor * drawn, drawn)


def block_levels(stream_key, dims, cuts, smallest, largest):
    level, own = 1.0, jax.random.fold_in(stream_key, 6)
    for axis_at, parts in cuts:
        steps = jnp.exp(jax.random.uniform(jax.random.fold_in(own, axis_at), (parts,), jnp.float32, smallest / len(cuts), largest / len(cuts)))
        level = level * jnp.repeat(steps, dims[axis_at] // parts).reshape([-1 if axis == axis_at else 1 for axis in range(len(dims))])
    return level


def gaussian(key, dims, spread, reach, cuts=(), kind=jnp.bfloat16):
    loudness = block_levels(key, dims, cuts, -0.22, 0.18) if cuts else 1.0
    entries = jax.random.normal(key, dims, jnp.float32) * spread * loudness
    return jnp.minimum(jnp.maximum(entries, -reach), reach).astype(kind)


def bell_draw_with(key, shape, scale, bound, cuts, heavy, kind=jnp.bfloat16):
    array = scale * jax.random.normal(key, shape, jnp.float32)
    if cuts:
        array = array * block_levels(key, shape, cuts, -0.22, 0.18)
    return jnp.clip(spiked(array, jax.random.fold_in(key, 3), *heavy), -bound, bound).astype(kind)


def setup_inputs(seed: int = 0) -> dict:
    arg_keys = jax.random.split(jax.random.key(seed), 16)
    return {
        "tokens": gaussian(arg_keys[0], (TOKENS, MODEL_WIDTH), 1.0, 6.0, ((0, 32),)),
        "lengths": draw_lengths(jax.random.fold_in(arg_keys[15], 71), 0),
        "row_order": jax.vmap(lambda own: jax.random.permutation(own, GROUP_TOKENS))(jax.random.split(arg_keys[2], N_DP)).reshape((N_DP, GROUP_TOKENS)).astype(jnp.int32),
        "attention_gain": jnp.clip(1.0 + 0.18 * jax.random.normal(arg_keys[3], (MODEL_WIDTH,), jnp.float32), 0.099609375, 1.8984375).astype(jnp.bfloat16),
        "query_gain": jnp.clip(0.796875 + 1.0 * jax.random.uniform(arg_keys[4], (HEAD_SIZE,), jnp.float32) ** block_levels(arg_keys[4], (HEAD_SIZE,), ((0, 8),), -0.2, 0.2), 0.796875, 1.796875).astype(jnp.bfloat16),
        "key_gain": jnp.clip(0.796875 + 1.0 * jax.random.uniform(arg_keys[5], (HEAD_SIZE,), jnp.float32) ** block_levels(arg_keys[5], (HEAD_SIZE,), ((0, 8),), -0.2, 0.2), 0.796875, 1.796875).astype(jnp.bfloat16),
        "query_weight": gaussian(arg_keys[6], (MODEL_WIDTH, QUERY_HEADS * HEAD_SIZE), MODEL_WIDTH ** -0.5, 0.1875, ((0, 8), (1, 4))),
        "key_matrix": gaussian(arg_keys[7], (MODEL_WIDTH, KEY_VALUE_HEADS * HEAD_SIZE), MODEL_WIDTH ** -0.5, 0.1875, ((0, 8), (1, 4))),
        "value_matrix": gaussian(arg_keys[8], (MODEL_WIDTH, KEY_VALUE_HEADS * HEAD_SIZE), MODEL_WIDTH ** -0.5, 0.1875, ((0, 8), (1, 4))),
        "output_weight": gaussian(arg_keys[9], (QUERY_HEADS * HEAD_SIZE, MODEL_WIDTH), (QUERY_HEADS * HEAD_SIZE // 64) ** -0.5, 1.0, ((0, 4), (1, 8))),
        "feedforward_gain": jnp.clip(1.0 + 0.18 * jax.random.normal(arg_keys[10], (MODEL_WIDTH,), jnp.float32), 0.099609375, 1.8984375).astype(jnp.bfloat16),
        "gate_weight": gaussian(arg_keys[11], (MODEL_WIDTH, FF), MODEL_WIDTH ** -0.5, 0.1875, ((0, 8), (1, 4))),
        "up_weight": gaussian(arg_keys[12], (MODEL_WIDTH, FF), MODEL_WIDTH ** -0.5, 0.1875, ((0, 8), (1, 4))),
        "down_weight": gaussian(arg_keys[13], (FF, MODEL_WIDTH), FF ** -0.5, 0.109375, ((0, 4), (1, 8))),
        "cotangent": bell_draw_with(arg_keys[14], (TOKENS, MODEL_WIDTH), 1.0, 6.0, ((0, 32),), (0, 1, 32, 2.75)),
    }


@jax.custom_vjp
def low_precise(v):
    return lax.optimization_barrier(v.astype(jnp.bfloat16)).astype(jnp.float32)

@jax.custom_vjp
def low_precise_back(v):
    return v

def low_keep(v):
    return (low_precise(v), None)

def low_pass(kept, grad):
    return (grad,)

def back_keep(v):
    return (v, None)

def back_low(kept, grad):
    return (low_precise(grad),)
low_precise.defvjp(low_keep, low_pass)
low_precise_back.defvjp(back_keep, back_low)
EPSILON = 1e-06
THETA = 1000000.0
HIGH_PRECISE = lax.Precision.HIGHEST

def rms_norm(value_rows, gain):
    scale = lax.rsqrt(lax.optimization_barrier(jnp.mean(value_rows * value_rows, axis=-1, keepdims=True)) + EPSILON)
    return value_rows * scale * gain

def rotate(value_rows, cosine, sine):
    half = value_rows.shape[-1] // 2
    first = value_rows[..., :half]
    second = value_rows[..., half:]
    return jnp.concatenate([first * cosine - second * sine, second * cosine + first * sine], axis=-1)

def layout(lengths_row, permuted_order_row):
    ends = jnp.cumsum(lengths_row).astype(jnp.int32)
    starts = (ends - lengths_row).astype(jnp.int32)
    document_ids = lax.optimization_barrier(jnp.sum((permuted_order_row[:, None] >= ends[None, :]).astype(jnp.int32), axis=1)).astype(jnp.int32)
    chosen = document_ids[:, None] == jnp.arange(lengths_row.shape[0], dtype=jnp.int32)[None, :]
    begin = lax.optimization_barrier(jnp.sum(jnp.where(chosen, starts[None, :], 0), axis=1)).astype(jnp.int32)
    return (document_ids, (permuted_order_row - begin).astype(jnp.int32))

def rotary_tables(position, width):
    half = width // 2
    inverse = THETA ** (-(jnp.arange(half, dtype=jnp.float32) * 2.0 / width))
    angle = position.astype(jnp.float32)[:, None] * inverse[None, :]
    return (jnp.cos(angle)[:, None, :], jnp.sin(angle)[:, None, :])

def group_layer(rows, lengths_row, permuted_order_row, params):
    gain_one, gain_query, gain_key, query_weight, key_matrix, value_matrix, output_weight, gain_two, gate_weight, up_weight, down_weight = params
    document_ids, position = layout(lengths_row, permuted_order_row)
    cosine, sine = rotary_tables(position, HEAD_SIZE)
    normed_input = low_precise(rms_norm(rows, gain_one))
    query_raw = low_precise_back(jnp.dot(normed_input, query_weight, precision=HIGH_PRECISE)).reshape(GROUP_TOKENS, QUERY_HEADS, HEAD_SIZE)
    key_unnormed = low_precise_back(jnp.dot(normed_input, key_matrix, precision=HIGH_PRECISE)).reshape(GROUP_TOKENS, KEY_VALUE_HEADS, HEAD_SIZE)
    value_rows = low_precise(low_precise_back(jnp.dot(normed_input, value_matrix, precision=HIGH_PRECISE))).reshape(GROUP_TOKENS, KEY_VALUE_HEADS, HEAD_SIZE)
    query_rows = low_precise(rotate(rms_norm(query_raw, gain_query), cosine, sine))
    keys = low_precise(rotate(rms_norm(key_unnormed, gain_key), cosine, sine))
    rows_per_block = min(512, GROUP_TOKENS)
    block_list = GROUP_TOKENS // rows_per_block

    def attend_heads(items):
        query_block, document_block, order_block = items
        scores = low_precise_back(jnp.einsum('qkgd,skd->kgqs', query_block, keys, precision=HIGH_PRECISE) * HEAD_SIZE ** (-0.5))
        allowed = (document_block[:, None] == document_ids[None, :]) & (order_block[:, None] >= permuted_order_row[None, :])
        weights = jax.nn.softmax(jnp.where(allowed, scores, -jnp.inf), axis=-1)
        return jnp.einsum('kgqs,skd->qkgd', low_precise(weights), value_rows, precision=HIGH_PRECISE)
    mixed_heads = lax.map(jax.checkpoint(attend_heads), (query_rows.reshape(block_list, rows_per_block, KEY_VALUE_HEADS, QUERY_HEADS // KEY_VALUE_HEADS, HEAD_SIZE), document_ids.reshape(block_list, rows_per_block), permuted_order_row.reshape(block_list, rows_per_block)))
    attended = low_precise(low_precise_back(mixed_heads.reshape(GROUP_TOKENS, QUERY_HEADS * HEAD_SIZE)))
    middle = rows + low_precise_back(jnp.dot(attended, output_weight, precision=HIGH_PRECISE))
    normed_two = low_precise(rms_norm(middle, gain_two))
    gate = low_precise_back(jnp.dot(normed_two, gate_weight, precision=HIGH_PRECISE))
    upward = low_precise_back(jnp.dot(normed_two, up_weight, precision=HIGH_PRECISE))
    activated = low_precise(jax.nn.silu(gate) * upward)
    return middle + low_precise_back(jnp.dot(activated, down_weight, precision=HIGH_PRECISE))

def reference(tokens, lengths, row_order, attention_gain, query_gain, key_gain, query_weight, key_matrix, value_matrix, output_weight, feedforward_gain, gate_weight, up_weight, down_weight, cotangent):
    params = tuple((item.astype(jnp.float32) for item in (attention_gain, query_gain, key_gain, query_weight, key_matrix, value_matrix, output_weight, feedforward_gain, gate_weight, up_weight, down_weight)))
    inputs = tokens.astype(jnp.float32).reshape(N_DP, GROUP_TOKENS, MODEL_WIDTH)

    def forward(inputs, params):

        def one_group(items):
            return group_layer(items[0], items[1], items[2], params)
        return lax.map(jax.checkpoint(one_group), (inputs, lengths, row_order))
    result, pullback = jax.vjp(forward, inputs, params)
    input_grad, grads = pullback(cotangent.astype(jnp.float32).reshape(N_DP, GROUP_TOKENS, MODEL_WIDTH))
    return (result.reshape(TOKENS, MODEL_WIDTH).astype(jnp.bfloat16), input_grad.reshape(TOKENS, MODEL_WIDTH).astype(jnp.bfloat16), grads[0], grads[1], grads[2], grads[3], grads[4], grads[5], grads[6], grads[7], grads[8], grads[9], grads[10])
```

```python
import functools

import jax
import jax.numpy as jnp
from jax import lax
from jax.experimental import pallas as pl
from jax.experimental.pallas import tpu as pltpu
from jax.sharding import PartitionSpec as P

HEAD_SIZE = 128
EPSILON = 1e-06
THETA = 1000000.0
AXES = ("dp", "tensor")
BLOCK = 256
HIDDEN_BLOCK = 512
SCALE = HEAD_SIZE ** (-0.5)
LOG2E = 1.4426950408889634
VMEM_LIMIT = 56 * 1024 * 1024
F32 = jnp.float32
BF16 = jnp.bfloat16


def dot_nn(left, right):
    return lax.dot_general(left, right, (((1,), (0,)), ((), ())), preferred_element_type=F32)


def dot_nt(left, right):
    return lax.dot_general(left, right, (((1,), (1,)), ((), ())), preferred_element_type=F32)


def dot_tn(left, right):
    return lax.dot_general(left, right, (((0,), (0,)), ((), ())), preferred_element_type=F32)


def row_scale(rows):
    return lax.rsqrt(jnp.mean(rows * rows, axis=-1, keepdims=True) + EPSILON)


def rotate(rows, cosine, sine):
    return rows * cosine + pltpu.roll(rows, HEAD_SIZE // 2, 1) * sine


def unrotate(rows, cosine, sine):
    return rows * cosine - pltpu.roll(rows, HEAD_SIZE // 2, 1) * sine


def project_kernel(
    query_heads, key_heads, x_ref, gain_ref, w_ref, gq_ref, gk_ref, cos_ref, sin_ref, normed_ref, qkv_ref, scale_ref
):
    x = x_ref[...].astype(F32)
    normed = (x * row_scale(x) * gain_ref[...]).astype(BF16)
    normed_ref[...] = normed
    raw = dot_nn(normed, w_ref[...])
    cosine, sine = cos_ref[...], sin_ref[...]
    lane = lax.broadcasted_iota(jnp.int32, (x.shape[0], HEAD_SIZE), 1)
    scales = jnp.zeros((x.shape[0], HEAD_SIZE), F32)
    for head in range(query_heads + key_heads):
        span = slice(head * HEAD_SIZE, (head + 1) * HEAD_SIZE)
        u = raw[:, span]
        r = row_scale(u)
        gain = gq_ref[...] if head < query_heads else gk_ref[...]
        qkv_ref[:, span] = rotate(u * r * gain, cosine, sine).astype(BF16)
        scales = jnp.where(lane == head, r, scales)
    span = slice((query_heads + key_heads) * HEAD_SIZE, None)
    qkv_ref[:, span] = raw[:, span].astype(BF16)
    scale_ref[...] = scales


def project(x, gain, weights, gain_query, gain_key, cosine, sine, query_heads, key_heads):
    rows, width = x.shape
    wide = weights.shape[1]
    whole = lambda shape: pl.BlockSpec(shape, lambda i: (0, 0))
    block = lambda cols: pl.BlockSpec((BLOCK, cols), lambda i: (i, 0))
    return pl.pallas_call(
        functools.partial(project_kernel, query_heads, key_heads),
        grid=(rows // BLOCK,),
        in_specs=[
            block(width),
            whole((1, width)),
            whole((width, wide)),
            whole((1, HEAD_SIZE)),
            whole((1, HEAD_SIZE)),
            block(HEAD_SIZE),
            block(HEAD_SIZE),
        ],
        out_specs=[block(width), block(wide), block(HEAD_SIZE)],
        out_shape=[
            jax.ShapeDtypeStruct((rows, width), BF16),
            jax.ShapeDtypeStruct((rows, wide), BF16),
            jax.ShapeDtypeStruct((rows, HEAD_SIZE), F32),
        ],
        compiler_params=pltpu.CompilerParams(vmem_limit_bytes=VMEM_LIMIT),
        cost_estimate=pl.CostEstimate(
            flops=2 * rows * width * wide, bytes_accessed=2 * rows * (2 * width + wide), transcendentals=0
        ),
        name="project",
    )(x, gain, weights, gain_query, gain_key, cosine, sine)


def first_place(info_ref, blocks, docs, places):
    start = jnp.zeros_like(places)
    for doc in range(docs):
        begin = info_ref[2 * blocks + doc]
        start = jnp.maximum(start, jnp.where(places >= begin, begin, 0))
    return start


def forward_kernel(group, blocks, docs, info_ref, q_ref, k_ref, v_ref, o_ref, lse_ref, wide_ref, acc_ref):
    i = pl.program_id(1)

    @pl.when(i == 0)
    def _():
        wide_ref[:, :HEAD_SIZE] = v_ref[...]
        wide_ref[:, HEAD_SIZE:] = jnp.ones_like(v_ref)

    queries = jnp.concatenate([q_ref[:, h * HEAD_SIZE : (h + 1) * HEAD_SIZE] for h in range(group)], axis=0)
    acc_ref[...] = jnp.zeros_like(acc_ref)
    shape = (group * BLOCK, BLOCK)

    def step(j, masked):
        rows = pl.ds(pl.multiple_of(j * BLOCK, BLOCK), BLOCK)
        weights = jnp.exp2(dot_nt(queries, k_ref[rows, :]) * (SCALE * LOG2E))
        if masked:
            places = i * BLOCK + lax.rem(lax.broadcasted_iota(jnp.int32, (group * BLOCK, 1), 0), BLOCK)
            start = first_place(info_ref, blocks, docs, places)
            other = j * BLOCK + lax.broadcasted_iota(jnp.int32, shape, 1)
            weights = jnp.where((other <= places) & (other >= start), weights, 0.0)
        acc_ref[...] += dot_nn(weights.astype(BF16), wide_ref[rows, :])

    low, clear = info_ref[i], info_ref[blocks + i]

    def masked_step(j, carry):
        step(j, True)
        return carry

    def clear_step(j, carry):
        step(j, False)
        return carry

    lax.fori_loop(low, jnp.minimum(clear, i), masked_step, 0)
    lax.fori_loop(jnp.minimum(clear, i), i, clear_step, 0)
    step(i, True)
    total = acc_ref[:, HEAD_SIZE:]
    out = (acc_ref[:, :HEAD_SIZE] / total).astype(BF16)
    for h in range(group):
        o_ref[:, h * HEAD_SIZE : (h + 1) * HEAD_SIZE] = out[h * BLOCK : (h + 1) * BLOCK]
    lse_ref[0, 0] = lax.dot_general(
        jnp.full((8, HEAD_SIZE), 1.0 / HEAD_SIZE, F32),
        jnp.log2(total),
        (((1,), (1,)), ((), ())),
        precision=lax.Precision.HIGHEST,
        preferred_element_type=F32,
    )


def attention_forward(info, qkv, query_heads, key_heads, docs):
    rows = qkv.shape[0]
    blocks = rows // BLOCK
    group = query_heads // key_heads
    wide = group * HEAD_SIZE
    return pl.pallas_call(
        functools.partial(forward_kernel, group, blocks, docs),
        grid_spec=pltpu.PrefetchScalarGridSpec(
            num_scalar_prefetch=1,
            grid=(key_heads, blocks),
            in_specs=[
                pl.BlockSpec((BLOCK, wide), lambda h, i, s: (i, h)),
                pl.BlockSpec((rows, HEAD_SIZE), lambda h, i, s: (0, query_heads + h)),
                pl.BlockSpec((rows, HEAD_SIZE), lambda h, i, s: (0, query_heads + key_heads + h)),
            ],
            out_specs=[
                pl.BlockSpec((BLOCK, wide), lambda h, i, s: (i, h)),
                pl.BlockSpec((1, 1, 8, group * BLOCK), lambda h, i, s: (h, i, 0, 0)),
            ],
            scratch_shapes=[
                pltpu.VMEM((rows, 2 * HEAD_SIZE), BF16),
                pltpu.VMEM((group * BLOCK, 2 * HEAD_SIZE), F32),
            ],
        ),
        out_shape=[
            jax.ShapeDtypeStruct((rows, query_heads * HEAD_SIZE), BF16),
            jax.ShapeDtypeStruct((key_heads, blocks, 8, group * BLOCK), F32),
        ],
        compiler_params=pltpu.CompilerParams(vmem_limit_bytes=VMEM_LIMIT),
        cost_estimate=pl.CostEstimate(
            flops=3 * rows * rows * HEAD_SIZE * query_heads // 2,
            bytes_accessed=4 * rows * query_heads * HEAD_SIZE,
            transcendentals=rows * rows * query_heads // 3,
        ),
        name="attention_forward",
    )(info, qkv, qkv, qkv)


def backward_kernel(
    group,
    query_heads,
    blocks,
    docs,
    info_ref,
    q_ref,
    k_ref,
    v_ref,
    o_ref,
    do_ref,
    lse_ref,
    cos_ref,
    sin_ref,
    scale_ref,
    gq_ref,
    gk_ref,
    dq_ref,
    dk_ref,
    dv_ref,
    dgain_ref,
    dk_acc,
    dv_acc,
    dq_acc,
):
    kv, i = pl.program_id(0), pl.program_id(1)

    @pl.when(i == 0)
    def _():
        dk_acc[...] = jnp.zeros_like(dk_acc)
        dv_acc[...] = jnp.zeros_like(dv_acc)

    @pl.when((i == 0) & (kv == 0))
    def _():
        dgain_ref[...] = jnp.zeros_like(dgain_ref)

    def stacked(ref):
        return jnp.concatenate([ref[:, h * HEAD_SIZE : (h + 1) * HEAD_SIZE] for h in range(group)], axis=0)

    queries, grads = stacked(q_ref), stacked(do_ref)
    product = stacked(o_ref).astype(F32) * grads.astype(F32)
    delta = lax.dot_general(
        jnp.ones((8, HEAD_SIZE), F32),
        product,
        (((1,), (1,)), ((), ())),
        precision=lax.Precision.HIGHEST,
        preferred_element_type=F32,
    )[:1]
    lse = lse_ref[0, 0, :1]
    dq_acc[...] = jnp.zeros_like(dq_acc)
    shape = (BLOCK, group * BLOCK)

    def step(j, masked):
        rows = pl.ds(pl.multiple_of(j * BLOCK, BLOCK), BLOCK)
        keys, values = k_ref[rows, :], v_ref[rows, :]
        probs = jnp.exp2(dot_nt(keys, queries) * (SCALE * LOG2E) - lse)
        if masked:
            places = i * BLOCK + lax.rem(lax.broadcasted_iota(jnp.int32, (1, group * BLOCK), 1), BLOCK)
            start = first_place(info_ref, blocks, docs, places)
            other = j * BLOCK + lax.broadcasted_iota(jnp.int32, shape, 0)
            probs = jnp.where((other <= places) & (other >= start), probs, 0.0)
        score_grad = (probs * (dot_nt(values, grads) - delta)).astype(BF16)
        dv_acc[rows, :] += dot_nn(probs.astype(BF16), grads)
        dk_acc[rows, :] += dot_nn(score_grad, queries)
        dq_acc[...] += dot_tn(score_grad, keys)

    low, clear = info_ref[i], info_ref[blocks + i]

    def masked_step(j, carry):
        step(j, True)
        return carry

    def clear_step(j, carry):
        step(j, False)
        return carry

    lax.fori_loop(low, jnp.minimum(clear, i), masked_step, 0)
    lax.fori_loop(jnp.minimum(clear, i), i, clear_step, 0)
    step(i, True)

    lane = lax.broadcasted_iota(jnp.int32, (BLOCK, HEAD_SIZE), 1)

    def raw_grad(grad, rotated, rows, head, gain):
        cosine, sine = cos_ref[rows, :], sin_ref[rows, :]
        r = jnp.sum(jnp.where(lane == head, scale_ref[rows, :], 0.0), axis=1, keepdims=True)
        unit = unrotate(rotated.astype(F32), cosine, sine) / gain
        back = unrotate(grad * SCALE, cosine, sine)
        scaled = back * gain
        raw = r * (scaled - unit * jnp.mean(scaled * unit, axis=1, keepdims=True))
        return raw.astype(BF16), jnp.sum(back * unit, axis=0, keepdims=True)

    here = pl.ds(pl.multiple_of(i * BLOCK, BLOCK), BLOCK)
    for h in range(group):
        span = slice(h * HEAD_SIZE, (h + 1) * HEAD_SIZE)
        raw, gain_grad = raw_grad(
            dq_acc[h * BLOCK : (h + 1) * BLOCK, :], q_ref[:, span], here, kv * group + h, gq_ref[...]
        )
        dq_ref[:, span] = raw
        dgain_ref[0:1, :] += gain_grad

    @pl.when(i == blocks - 1)
    def _():
        dv_ref[...] = dv_acc[...].astype(BF16)

        def finish(b, carry):
            rows = pl.ds(pl.multiple_of(b * BLOCK, BLOCK), BLOCK)
            raw, gain_grad = raw_grad(dk_acc[rows, :], k_ref[rows, :], rows, query_heads + kv, gk_ref[...])
            dk_ref[rows, :] = raw
            dgain_ref[1:2, :] += gain_grad
            return carry

        lax.fori_loop(0, blocks, finish, 0)


def attention_backward(
    info, qkv, attended, grads, lse, cosine, sine, scales, gain_query, gain_key, query_heads, key_heads, docs
):
    rows = qkv.shape[0]
    blocks = rows // BLOCK
    group = query_heads // key_heads
    wide = group * HEAD_SIZE
    per_block = pl.BlockSpec((BLOCK, wide), lambda h, i, s: (i, h))
    whole = lambda shape: pl.BlockSpec(shape, lambda h, i, s: (0, 0))
    return pl.pallas_call(
        functools.partial(backward_kernel, group, query_heads, blocks, docs),
        grid_spec=pltpu.PrefetchScalarGridSpec(
            num_scalar_prefetch=1,
            grid=(key_heads, blocks),
            in_specs=[
                per_block,
                pl.BlockSpec((rows, HEAD_SIZE), lambda h, i, s: (0, query_heads + h)),
                pl.BlockSpec((rows, HEAD_SIZE), lambda h, i, s: (0, query_heads + key_heads + h)),
                per_block,
                per_block,
                pl.BlockSpec((1, 1, 8, group * BLOCK), lambda h, i, s: (h, i, 0, 0)),
                whole((rows, HEAD_SIZE)),
                whole((rows, HEAD_SIZE)),
                whole((rows, HEAD_SIZE)),
                whole((1, HEAD_SIZE)),
                whole((1, HEAD_SIZE)),
            ],
            out_specs=[
                per_block,
                pl.BlockSpec((rows, HEAD_SIZE), lambda h, i, s: (0, h)),
                pl.BlockSpec((rows, HEAD_SIZE), lambda h, i, s: (0, h)),
                whole((8, HEAD_SIZE)),
            ],
            scratch_shapes=[
                pltpu.VMEM((rows, HEAD_SIZE), F32),
                pltpu.VMEM((rows, HEAD_SIZE), F32),
                pltpu.VMEM((group * BLOCK, HEAD_SIZE), F32),
            ],
        ),
        out_shape=[
            jax.ShapeDtypeStruct((rows, query_heads * HEAD_SIZE), BF16),
            jax.ShapeDtypeStruct((rows, key_heads * HEAD_SIZE), BF16),
            jax.ShapeDtypeStruct((rows, key_heads * HEAD_SIZE), BF16),
            jax.ShapeDtypeStruct((8, HEAD_SIZE), F32),
        ],
        compiler_params=pltpu.CompilerParams(vmem_limit_bytes=VMEM_LIMIT),
        cost_estimate=pl.CostEstimate(
            flops=10 * rows * rows * HEAD_SIZE * query_heads // 2,
            bytes_accessed=10 * rows * query_heads * HEAD_SIZE,
            transcendentals=rows * rows * query_heads // 3,
        ),
        name="attention_backward",
    )(info, qkv, qkv, qkv, attended, grads, lse, cosine, sine, scales, gain_query, gain_key)


def feed_kernel(
    x_ref, xt_ref, c_ref, ct_ref, g_ref, u_ref, d_ref, out_ref, ng_ref, dg_ref, du_ref, dd_ref, act_s, gg_s, ug_s
):
    j = pl.program_id(0)
    rows_all, width = x_ref.shape
    chunk = rows_all // 2

    @pl.when(j == 0)
    def _():
        out_ref[...] = jnp.zeros_like(out_ref)
        ng_ref[...] = jnp.zeros_like(ng_ref)

    def rows_step(m, carry):
        rows = pl.ds(pl.multiple_of(m * chunk, chunk), chunk)
        gate = dot_nn(x_ref[rows, :], g_ref[...])
        upward = dot_nn(x_ref[rows, :], u_ref[...])
        act_grad = dot_nn(c_ref[rows, :], d_ref[...])
        sig = 1.0 / (1.0 + jnp.exp(-gate))
        silu = gate * sig
        act = (silu * upward).astype(BF16)
        up_grad = (act_grad * silu).astype(BF16)
        gate_grad = (act_grad * upward * sig * (1.0 + gate * (1.0 - sig))).astype(BF16)
        act_s[rows, :] = act
        ug_s[rows, :] = up_grad
        gg_s[rows, :] = gate_grad
        out_ref[rows, :] += dot_nt(act, d_ref[...])
        ng_ref[rows, :] += dot_nt(gate_grad, g_ref[...]) + dot_nt(up_grad, u_ref[...])
        return carry

    lax.fori_loop(0, rows_all // chunk, rows_step, 0)

    def grad_step(m, carry):
        rows = pl.ds(pl.multiple_of(m * BLOCK, BLOCK), BLOCK)
        dg_ref[rows, :] = dot_nn(xt_ref[rows, :], gg_s[...]).astype(BF16)
        du_ref[rows, :] = dot_nn(xt_ref[rows, :], ug_s[...]).astype(BF16)
        dd_ref[rows, :] = dot_nn(ct_ref[rows, :], act_s[...]).astype(BF16)
        return carry

    lax.fori_loop(0, width // BLOCK, grad_step, 0)


def feed(x, xt, cot, cot_t, first, second, head_columns, hidden):
    rows, width = x.shape
    hb = HIDDEN_BLOCK
    whole = lambda shape: pl.BlockSpec(shape, lambda j: (0, 0))
    at = lambda base: pl.BlockSpec((width, hb), lambda j: (0, base + j))
    shift = head_columns // hb
    steps = hidden // hb
    return pl.pallas_call(
        feed_kernel,
        grid=(steps,),
        in_specs=[
            whole((rows, width)),
            whole((width, rows)),
            whole((rows, width)),
            whole((width, rows)),
            at(shift),
            at(0),
            at(steps),
        ],
        out_specs=[whole((rows, width)), whole((rows, width)), at(0), at(0), at(0)],
        out_shape=[
            jax.ShapeDtypeStruct((rows, width), F32),
            jax.ShapeDtypeStruct((rows, width), F32),
            jax.ShapeDtypeStruct((width, hidden), BF16),
            jax.ShapeDtypeStruct((width, hidden), BF16),
            jax.ShapeDtypeStruct((width, hidden), BF16),
        ],
        scratch_shapes=[pltpu.VMEM((rows, hb), BF16)] * 3,
        compiler_params=pltpu.CompilerParams(vmem_limit_bytes=VMEM_LIMIT),
        cost_estimate=pl.CostEstimate(
            flops=18 * rows * width * hidden,
            bytes_accessed=12 * width * hidden + 16 * rows * width,
            transcendentals=rows * hidden,
        ),
        name="feed_forward",
    )(x, xt, cot, cot_t, first, second, second)


def local(
    tokens,
    lengths,
    row_order,
    attention_gain,
    query_gain,
    key_gain,
    query_weight,
    key_matrix,
    value_matrix,
    output_weight,
    feedforward_gain,
    gate_weight,
    up_weight,
    down_weight,
    cotangent,
):
    span = lax.axis_size("tensor")
    pairs = lax.axis_size("dp") // 2
    half = span // 2
    rows, width = tokens.shape
    group_rows = rows * span
    blocks = group_rows // BLOCK
    docs = lengths.shape[1]
    query_heads = query_weight.shape[1] // HEAD_SIZE
    key_heads = key_matrix.shape[1] // HEAD_SIZE
    head_columns = query_weight.shape[1]
    hidden_columns = gate_weight.shape[1]
    shard = query_weight.shape[0]

    dp, t = lax.axis_index("dp"), lax.axis_index("tensor")
    p, c = dp // 2, lax.rem(dp, 2)
    q = t // half
    settled = c == q

    def send(x, route):
        moves = []
        for pp in range(pairs):
            for cc in range(2):
                for tt in range(span):
                    to = route(pp, cc, tt)
                    if to is not None:
                        moves.append(((pp * 2 + cc) * span + tt, (to[0] * 2 + to[1]) * span + to[2]))
        return lax.ppermute(x, AXES, moves)

    def sibling(x):
        return send(x, lambda pp, cc, tt: (pp, 1 - cc, tt))

    def swap(x):
        moved = send(x, lambda pp, cc, tt: (pp, 1 - cc, span - 1 - tt) if cc != tt // half else None)
        return jnp.where(settled, x, moved)

    def ordered(mine, other, first):
        return jnp.where(first, mine, other), jnp.where(first, other, mine)

    swapped = swap(tokens)
    stack = [swapped]
    bit = 1
    while bit < half:
        moved = send(jnp.concatenate(stack, axis=0), lambda pp, cc, tt: (pp, cc, tt ^ bit))
        stack += [moved[k * rows : (k + 1) * rows] for k in range(len(stack))]
        bit *= 2
    moved = sibling(jnp.concatenate(stack, axis=0))
    tokens_all = jnp.concatenate(stack + [moved], axis=0)
    cot_own = swap(cotangent)

    heads_local = jnp.concatenate([query_weight, key_matrix, value_matrix], axis=1)
    moved = send(heads_local, lambda pp, cc, tt: (pp, 1 - cc, tt) if cc != tt // half else None)
    pair = jnp.concatenate(ordered(heads_local, moved, c == 0), axis=0)
    moved = send(pair, lambda pp, cc, tt: (pp, cc, (tt + half) % span) if cc == tt // half else None)
    pair = jnp.where(settled, pair, moved)

    def gather_pairs(x):
        size = x.shape[0]
        out = jnp.zeros((pairs * size, x.shape[1]), x.dtype)
        put = lambda out, piece, at, shift: lax.dynamic_update_slice(out, piece, (at * size + shift, 0))
        if pairs == 4:
            cut = size // 2
            one = send(x, lambda pp, cc, tt: (pp ^ 1, cc, tt))
            two = send(x, lambda pp, cc, tt: (pp ^ 2, cc, tt))
            upper = send(two[:cut], lambda pp, cc, tt: (pp ^ 1, cc, tt))
            lower = send(one[cut:], lambda pp, cc, tt: (pp ^ 2, cc, tt))
            out = put(out, x, p, 0)
            out = put(out, one, p ^ 1, 0)
            out = put(out, two, p ^ 2, 0)
            out = put(out, upper, p ^ 3, 0)
            return put(out, lower, p ^ 3, cut)
        pieces, bit = [x], 1
        while bit < pairs:
            moved = send(jnp.concatenate(pieces, axis=0), lambda pp, cc, tt: (pp ^ bit, cc, tt))
            pieces += [moved[k * size : (k + 1) * size] for k in range(len(pieces))]
            bit *= 2
        for k, piece in enumerate(pieces):
            out = put(out, piece, p ^ k, 0)
        return out

    def scatter_pairs(x):
        size = x.shape[0] // pairs
        take = lambda at, shift, count: lax.dynamic_slice(x, (at * size + shift, 0), (count, x.shape[1]))
        if pairs == 4:
            cut = size // 2
            upper = send(take(p ^ 3, 0, cut), lambda pp, cc, tt: (pp ^ 1, cc, tt))
            lower = send(take(p ^ 3, cut, cut), lambda pp, cc, tt: (pp ^ 2, cc, tt))
            one = jnp.concatenate(
                [take(p ^ 1, 0, cut), (take(p ^ 1, cut, cut).astype(F32) + lower.astype(F32)).astype(BF16)], axis=0
            )
            two = jnp.concatenate(
                [(take(p ^ 2, 0, cut).astype(F32) + upper.astype(F32)).astype(BF16), take(p ^ 2, cut, cut)], axis=0
            )
            one = send(one, lambda pp, cc, tt: (pp ^ 1, cc, tt))
            two = send(two, lambda pp, cc, tt: (pp ^ 2, cc, tt))
            return (take(p, 0, size).astype(F32) + one.astype(F32) + two.astype(F32)).astype(BF16)
        pieces = [take(p ^ k, 0, size) for k in range(pairs)]
        while len(pieces) > 1:
            keep = len(pieces) // 2
            moved = send(jnp.concatenate(pieces[keep:], axis=0), lambda pp, cc, tt: (pp ^ keep, cc, tt))
            pieces = [
                (pieces[k].astype(F32) + moved[k * size : (k + 1) * size].astype(F32)).astype(BF16)
                for k in range(keep)
            ]
        return pieces[0]

    heads_weights = gather_pairs(pair)

    def halves(x):
        middle = x.shape[1] // 2
        return x[:, :middle], x[:, middle:]

    def wide_gather(parts):
        split = [halves(part) for part in parts]
        mine = jnp.concatenate([jnp.where(c == 0, a, b) for a, b in split], axis=1)
        theirs = jnp.concatenate([jnp.where(c == 0, b, a) for a, b in split], axis=1)
        moved = sibling(theirs)
        joined = jnp.concatenate(ordered(mine, moved, c == 0), axis=0)
        pieces = [joined] + [send(joined, lambda pp, cc, tt: (pp, cc, tt ^ r)) for r in range(1, span)]
        spread, at = [], 0
        for part in parts:
            wide = part.shape[1] // 2
            spread += [piece[:, at : at + wide] for piece in pieces]
            at += wide
        return gather_pairs(jnp.concatenate(spread, axis=1))

    first_own = wide_gather([output_weight.T, gate_weight])
    second_own = wide_gather([up_weight, down_weight.T])
    first_sib = sibling(first_own)
    second_sib = sibling(second_own)

    gains = jnp.concatenate([attention_gain, query_gain, key_gain, feedforward_gain])
    gains = lax.all_gather(gains, "dp", axis=0).astype(F32)
    small, tiny = attention_gain.shape[0], query_gain.shape[0]
    gain_one = gains[:, :small].reshape(1, width)
    gain_query = gains[:, small : small + tiny].reshape(1, HEAD_SIZE)
    gain_key = gains[:, small + tiny : small + 2 * tiny].reshape(1, HEAD_SIZE)
    gain_two = gains[:, small + 2 * tiny :].reshape(1, width)

    facts = jnp.concatenate([row_order[0], lengths[0]])
    facts = jnp.where(settled, facts, sibling(facts))
    order, length = facts[:group_rows].reshape(span, rows), facts[group_rows:]
    places = []
    for k in range(span):
        tt, cc = t ^ (k % half), c ^ (k // half)
        places.append(lax.dynamic_index_in_dim(order, jnp.where(cc == tt // half, tt, span - 1 - tt), 0, False))
    places = jnp.concatenate(places)
    inverse = jnp.argsort(places)
    before = jnp.arange(docs)[None, :] < jnp.arange(docs)[:, None]
    starts = jnp.sum(jnp.where(before, length[None, :], 0), axis=1).astype(jnp.int32)

    def start_of(place):
        return jnp.max(jnp.where(place[:, None] >= starts[None, :], starts[None, :], 0), axis=1)

    index = jnp.arange(blocks, dtype=jnp.int32) * BLOCK
    low = start_of(index) // BLOCK
    clear = (start_of(index + BLOCK - 1) + BLOCK - 1) // BLOCK
    info = jnp.concatenate([low, clear, starts]).astype(jnp.int32)
    index = jnp.arange(group_rows, dtype=jnp.int32)
    position = (index - start_of(index)).astype(F32)
    inverse_rate = THETA ** (-(jnp.arange(HEAD_SIZE // 2, dtype=F32) * 2.0 / HEAD_SIZE))
    angle = position[:, None] * inverse_rate[None, :]
    cosine, sine = jnp.cos(angle), jnp.sin(angle)
    cosine = jnp.concatenate([cosine, cosine], axis=1)
    sine = jnp.concatenate([-sine, sine], axis=1)

    tokens_sorted = jnp.take(tokens_all, inverse, axis=0, mode="clip")
    normed, qkv, scales = project(
        tokens_sorted, gain_one, heads_weights, gain_query, gain_key, cosine, sine, query_heads, key_heads
    )
    attended, lse = attention_forward(info, qkv, query_heads, key_heads, docs)
    attended_rows = jnp.take(attended, places, axis=0, mode="clip")

    def exchange(parts):
        out = [parts[0]]
        for k in range(1, span):
            out.append(send(parts[k], lambda pp, cc, tt: (pp, cc ^ (k // half), tt ^ (k % half))))
        return out

    arrived = exchange([attended_rows[k * rows : (k + 1) * rows] for k in range(span)])
    by_chunk = [
        jnp.where(settled, arrived[r], arrived[(1 - r // half) * half + r % half]) for r in range(span)
    ]
    split = [halves(piece) for piece in by_chunk]
    mixed_own = jnp.concatenate([jnp.where(c == 0, a, b) for a, b in split], axis=1)
    mixed_sib = jnp.concatenate([jnp.where(c == 0, b, a) for a, b in split], axis=1)
    columns = mixed_own.shape[1]
    inputs = swapped.astype(F32)
    middle = inputs + (dot_nt(mixed_own, first_own[:, :columns]) + dot_nt(mixed_sib, first_sib[:, :columns]))

    r_two = row_scale(middle)
    unit_two = middle * r_two
    normed_two = (unit_two * gain_two).astype(BF16)
    normed_two_t, cot_t = normed_two.T, cot_own.T
    hidden = span * (hidden_columns // 2)
    sib = feed(normed_two, normed_two_t, cot_own, cot_t, first_sib, second_sib, columns, hidden)
    own = feed(normed_two, normed_two_t, cot_own, cot_t, first_own, second_own, columns, hidden)
    layer_output = swap((middle + (own[0] + sib[0])).astype(BF16))
    normed_two_grad = own[1] + sib[1]
    gain_two_grad = jnp.sum(normed_two_grad * unit_two, axis=0)
    scaled = normed_two_grad * gain_two
    middle_grad = cot_own.astype(F32) + r_two * (
        scaled - unit_two * jnp.mean(scaled * unit_two, axis=-1, keepdims=True)
    )
    branch = middle_grad.astype(BF16)

    grad_own = dot_nn(branch, first_own[:, :columns]).astype(BF16)
    grad_sib = dot_nn(branch, first_sib[:, :columns]).astype(BF16)
    wide = columns // span
    by_chunk = []
    for r in range(span):
        a, b = ordered(grad_own[:, r * wide : (r + 1) * wide], grad_sib[:, r * wide : (r + 1) * wide], c == 0)
        by_chunk.append(jnp.concatenate([a, b], axis=1))
    arrived = exchange(
        [jnp.where(settled, by_chunk[k], by_chunk[(1 - k // half) * half + k % half]) for k in range(span)]
    )
    attended_grad = jnp.take(jnp.concatenate(arrived, axis=0), inverse, axis=0, mode="clip")
    query_grad, key_grad, value_grad, head_gains = attention_backward(
        info,
        qkv,
        attended,
        attended_grad,
        lse,
        cosine,
        sine,
        scales,
        gain_query,
        gain_key,
        query_heads,
        key_heads,
        docs,
    )
    qkv_grad = jnp.concatenate([query_grad, key_grad, value_grad], axis=1)
    partial = dot_nt(jnp.take(qkv_grad, places, axis=0, mode="clip"), heads_weights).astype(BF16)
    parts = [partial[k * rows : (k + 1) * rows] for k in range(span)]
    moved = sibling(jnp.concatenate(parts[half:], axis=0))
    parts = [
        (parts[k].astype(F32) + moved[k * rows : (k + 1) * rows].astype(F32)).astype(BF16) for k in range(half)
    ]
    while len(parts) > 1:
        keep = len(parts) // 2
        moved = send(jnp.concatenate(parts[keep:], axis=0), lambda pp, cc, tt: (pp, cc, tt ^ keep))
        parts = [
            (parts[k].astype(F32) + moved[k * rows : (k + 1) * rows].astype(F32)).astype(BF16) for k in range(keep)
        ]
    normed_grad = parts[0].astype(F32)
    r_one = row_scale(inputs)
    unit_one = inputs * r_one
    gain_one_grad = jnp.sum(normed_grad * unit_one, axis=0)
    scaled = normed_grad * gain_one
    input_grad = swap(
        (middle_grad + r_one * (scaled - unit_one * jnp.mean(scaled * unit_one, axis=-1, keepdims=True))).astype(BF16)
    )

    def wide_scatter(own_parts, sib_parts):
        moved = sibling(jnp.concatenate(sib_parts, axis=1))
        total = (jnp.concatenate(own_parts, axis=1).astype(F32) + moved.astype(F32)).astype(BF16)
        total = scatter_pairs(total)
        widths = [part.shape[1] // span for part in own_parts]
        pieces = []
        for r in range(span):
            at, cols = 0, []
            for w in widths:
                cols.append(total[:, at + r * w : at + (r + 1) * w])
                at += span * w
            pieces.append(jnp.concatenate(cols, axis=1))
        summed = pieces[0].astype(F32)
        for r in range(1, span):
            summed = summed + send(pieces[r], lambda pp, cc, tt: (pp, cc, tt ^ r)).astype(F32)
        top, bottom = summed[:shard], summed[shard:]
        mine, theirs = jnp.where(c == 0, top, bottom), jnp.where(c == 0, bottom, top)
        moved = sibling(theirs.astype(BF16)).astype(F32)
        low_half, high_half = ordered(mine, moved, c == 0)
        out, at = [], 0
        for w in widths:
            out.append(jnp.concatenate([low_half[:, at : at + w], high_half[:, at : at + w]], axis=1))
            at += w
        return out

    up_grad, down_grad = wide_scatter(own[3:5], sib[3:5])
    output_grads = [dot_tn(branch, mixed).astype(BF16) for mixed in (mixed_own, mixed_sib)]
    output_grad, gate_grad = wide_scatter([output_grads[0], own[2]], [output_grads[1], sib[2]])

    heads_grad = dot_tn(normed, qkv_grad).astype(BF16)
    mine = scatter_pairs(heads_grad)
    moved = send(mine, lambda pp, cc, tt: (pp, cc, (tt + half) % span) if cc != tt // half else None)
    summed = mine.astype(F32) + moved.astype(F32)
    top, bottom = summed[:shard], summed[shard:]
    theirs = jnp.where(c == 0, bottom, top).astype(BF16)
    moved = send(theirs, lambda pp, cc, tt: (pp, 1 - cc, tt) if cc == tt // half else None).astype(F32)
    summed = jnp.where(settled, jnp.where(c == 0, top, bottom), moved)
    key_columns = key_heads * HEAD_SIZE

    gain_sums = lax.psum(
        jnp.concatenate([gain_one_grad, head_gains[0], head_gains[1], gain_two_grad]), AXES
    )
    cut = lambda at, size: lax.dynamic_slice(gain_sums, (at + dp * size,), (size,))
    return (
        layer_output,
        input_grad,
        cut(0, small),
        cut(width, tiny),
        cut(width + HEAD_SIZE, tiny),
        summed[:, :head_columns],
        summed[:, head_columns : head_columns + key_columns],
        summed[:, head_columns + key_columns :],
        output_grad.T,
        cut(width + 2 * HEAD_SIZE, small),
        gate_grad,
        up_grad,
        down_grad.T,
    )


def solution(mesh):
    placed = (
        P(AXES, None),
        P("dp", None),
        P("dp", None),
        P("dp"),
        P("dp"),
        P("dp"),
        P("dp", "tensor"),
        P("dp", "tensor"),
        P("dp", "tensor"),
        P("tensor", "dp"),
        P("dp"),
        P("dp", "tensor"),
        P("dp", "tensor"),
        P("tensor", "dp"),
        P(AXES, None),
    )
    return jax.shard_map(
        local,
        mesh=mesh,
        in_specs=placed,
        out_specs=(
            P(AXES, None),
            P(AXES, None),
            P("dp"),
            P("dp"),
            P("dp"),
            P("dp", "tensor"),
            P("dp", "tensor"),
            P("dp", "tensor"),
            P("tensor", "dp"),
            P("dp"),
            P("dp", "tensor"),
            P("dp", "tensor"),
            P("tensor", "dp"),
        ),
        check_vma=False,
    )
```

```python
import functools

import jax
import jax.numpy as jnp
from jax import lax
from jax.experimental.layout import Layout, with_layout_constraint
from jax.experimental import pallas as pl
from jax.experimental.pallas import tpu as pltpu
from jax.sharding import PartitionSpec as P

HEAD_SIZE = 128
EPSILON = 1e-06
THETA = 1000000.0
AXES = ("dp", "tensor")
BLOCK = 256
SCALE = HEAD_SIZE ** (-0.5)
LOG2E = 1.4426950408889634
VMEM_LIMIT = 56 * 1024 * 1024
F32 = jnp.float32
BF16 = jnp.bfloat16


def dot_nn(left, right):
    return lax.dot_general(left, right, (((1,), (0,)), ((), ())), preferred_element_type=F32)


def dot_nt(left, right):
    return lax.dot_general(left, right, (((1,), (1,)), ((), ())), preferred_element_type=F32)


def dot_tn(left, right):
    return lax.dot_general(left, right, (((0,), (0,)), ((), ())), preferred_element_type=F32)


def by_rows(x):
    return with_layout_constraint(x, Layout(major_to_minor=tuple(range(x.ndim))))


def row_scale(rows):
    return lax.rsqrt(jnp.mean(rows * rows, axis=-1, keepdims=True) + EPSILON)


def rotate(rows, cosine, sine):
    return rows * cosine + pltpu.roll(rows, HEAD_SIZE // 2, 1) * sine


def unrotate(rows, cosine, sine):
    return rows * cosine - pltpu.roll(rows, HEAD_SIZE // 2, 1) * sine


CHUNKS = 4


def first_kernel(
    pairs,
    span,
    tokens_ref,
    heads_ref,
    output_ref,
    gains_ref,
    facts_ref,
    tokens_out,
    heads_out,
    output_out,
    gains_out,
    facts_out,
    send_sems,
    recv_sems,
    local_sems,
):
    half = span // 2
    dp, t = lax.axis_index("dp"), lax.axis_index("tensor")
    p, c = dp // 2, lax.rem(dp, 2)
    q = t // half
    settled = c == q
    rows = tokens_ref.shape[0]
    piece = rows // CHUNKS
    shard = heads_ref.shape[0]
    small = gains_ref.shape[0]
    place = lambda pp, cc, tt: (pp * 2 + cc, tt)

    barrier = pltpu.get_barrier_semaphore()
    greeted = 0
    for k in range(1, 2 * span):
        pl.semaphore_signal(
            barrier,
            device_id=place(p, c ^ (k // span), t ^ (k % span)),
            device_id_type=pl.DeviceIdType.MESH,
        )
        greeted += 1
    for k in range(1, pairs):
        for cc in range(2):
            pl.semaphore_signal(
                barrier, device_id=place(p ^ k, c ^ cc, t), device_id_type=pl.DeviceIdType.MESH
            )
            greeted += 1
    pl.semaphore_wait(barrier, greeted)

    used = [0]

    def number(count=1):
        used[0] += count
        return used[0] - count

    def remote(src, dst, sem, to, arrival=None):
        return pltpu.make_async_remote_copy(
            src_ref=src,
            dst_ref=dst,
            send_sem=send_sems.at[sem],
            recv_sem=recv_sems.at[sem if arrival is None else arrival],
            device_id=to,
            device_id_type=pl.DeviceIdType.MESH,
        )

    def rows_of(i):
        return pl.ds(i * piece, piece)

    swap_sem = number(CHUNKS)
    line_sems = [[number() for _ in range(CHUNKS)] for _ in range(half)]
    side_sems = [[number() for _ in range(CHUNKS)] for _ in range(half)]
    near_sem, far_sem = number(), number(2)
    pair_sems = [number() for _ in range(pairs)]
    output_sems = [number() for _ in range(span)]
    gain_sems = [number() for _ in range(2 * pairs)]
    fact_sem = number()

    sibling = place(p, 1 - c, t)
    partner = place(p, 1 - c, span - 1 - t)
    swaps = [
        remote(tokens_ref.at[rows_of(i)], tokens_out.at[0, rows_of(i)], swap_sem + i, partner) for i in range(CHUNKS)
    ]
    own_rows = pl.ds(dp * shard, shard)
    far = lax.rem(t + half, span)
    near_copy = remote(heads_ref, heads_out.at[own_rows], near_sem, sibling)
    far_copy = remote(heads_ref, heads_out.at[own_rows], far_sem + c, place(p, q, far))
    local_tokens = pltpu.make_async_copy(tokens_ref, tokens_out.at[0], local_sems.at[0])
    local_heads = pltpu.make_async_copy(heads_ref, heads_out.at[own_rows], local_sems.at[1])
    local_output = pltpu.make_async_copy(output_ref, output_out.at[0], local_sems.at[2])
    local_gains = pltpu.make_async_copy(gains_ref, gains_out.at[pl.ds(dp * small, small)], local_sems.at[3])

    fact_copy = remote(facts_ref, facts_out, fact_sem, sibling)
    fact_copy.start()
    far_copy.start()

    @pl.when(settled)
    def _():
        local_heads.start()
        local_tokens.start()

    @pl.when(jnp.logical_not(settled))
    def _():
        near_copy.start()
        for copy in swaps:
            copy.start()

    gain_copies = []
    for k in range(1, 2 * pairs):
        to = (p ^ (k // 2), c ^ (k % 2))
        gain_copies.append(
            remote(gains_ref, gains_out.at[pl.ds(dp * small, small)], gain_sems[k], place(to[0], to[1], t))
        )
    local_gains.start()
    local_output.start()
    for copy in gain_copies:
        copy.start()

    def spread(i, source):
        copies = [remote(source, tokens_out.at[half, rows_of(i)], side_sems[0][i], sibling)]
        for k in range(1, half):
            copies.append(remote(source, tokens_out.at[k, rows_of(i)], line_sems[k][i], place(p, c, t ^ k)))
        return copies

    @pl.when(settled)
    def _():
        for i in range(CHUNKS):
            for copy in spread(i, tokens_ref.at[rows_of(i)]):
                copy.start()

    output_copies = [
        remote(output_ref, output_out.at[r], output_sems[r], place(p, c, t ^ r)) for r in range(1, span)
    ]

    @pl.when(settled)
    def _():
        local_heads.wait()
        near_copy.wait_recv()

    @pl.when(jnp.logical_not(settled))
    def _():
        near_copy.wait_send()
        for cc in range(2):
            remote(heads_ref, heads_out.at[own_rows], far_sem, sibling, far_sem + cc).wait_recv()

    both = heads_out.at[pl.ds(p * 2 * shard, 2 * shard)]
    pair_copies = [remote(both, both, pair_sems[k], place(p ^ k, c, t)) for k in range(1, pairs)]
    for copy in pair_copies:
        copy.start()

    @pl.when(jnp.logical_not(settled))
    def _():
        for i in range(CHUNKS):
            swaps[i].wait_recv()
            for copy in spread(i, tokens_out.at[0, rows_of(i)]):
                copy.start()

    for copy in output_copies:
        copy.start()

    forwards = []
    for i in range(CHUNKS):
        for k in range(1, half):
            block = tokens_out.at[k, rows_of(i)]
            remote(block, block, line_sems[k][i], sibling).wait_recv()
            copy = remote(block, tokens_out.at[half + k, rows_of(i)], side_sems[k][i], sibling)
            copy.start()
            forwards.append(copy)

    far_copy.wait_send()
    fact_copy.wait()
    local_output.wait()
    local_gains.wait()

    @pl.when(settled)
    def _():
        local_tokens.wait()

    @pl.when(jnp.logical_not(settled))
    def _():
        for copy in swaps:
            copy.wait_send()

    for i in range(CHUNKS):
        for index, copy in enumerate(spread(i, tokens_out.at[0, rows_of(i)])):
            copy.wait_send()
            if index == 0:
                copy.wait_recv()
    for copy in forwards + pair_copies + output_copies + gain_copies:
        copy.wait()


def first_transfers(pairs, span, tokens, heads, output, gains, facts):
    rows, width = tokens.shape
    shard = heads.shape[0]
    half = span // 2
    copies = CHUNKS * (1 + 2 * half) + 3 + pairs + span + 2 * pairs + 1
    any_ref = pl.BlockSpec(memory_space=pl.ANY)
    return pl.pallas_call(
        functools.partial(first_kernel, pairs, span),
        in_specs=[any_ref] * 5,
        out_specs=[any_ref] * 5,
        out_shape=[
            jax.ShapeDtypeStruct((span, rows, width), tokens.dtype),
            jax.ShapeDtypeStruct((2 * pairs * shard, heads.shape[1]), heads.dtype),
            jax.ShapeDtypeStruct((span, *output.shape), output.dtype),
            jax.ShapeDtypeStruct((2 * pairs * gains.shape[0], gains.shape[1]), gains.dtype),
            jax.ShapeDtypeStruct(facts.shape, facts.dtype),
        ],
        scratch_shapes=[
            pltpu.SemaphoreType.DMA((copies,)),
            pltpu.SemaphoreType.DMA((copies,)),
            pltpu.SemaphoreType.DMA((4,)),
        ],
        compiler_params=pltpu.CompilerParams(collective_id=0, has_side_effects=True),
        name="first_transfers",
    )(tokens, heads, output, gains, facts)


def project_kernel(
    query_heads, key_heads, x_ref, gain_ref, w_ref, gq_ref, gk_ref, cos_ref, sin_ref, normed_ref, qkv_ref, scale_ref
):
    x = x_ref[...].astype(F32)
    normed = (x * row_scale(x) * gain_ref[...]).astype(BF16)
    normed_ref[...] = normed
    raw = dot_nn(normed, w_ref[...])
    cosine, sine = cos_ref[...], sin_ref[...]
    lane = lax.broadcasted_iota(jnp.int32, (x.shape[0], HEAD_SIZE), 1)
    scales = jnp.zeros((x.shape[0], HEAD_SIZE), F32)
    for head in range(query_heads + key_heads):
        span = slice(head * HEAD_SIZE, (head + 1) * HEAD_SIZE)
        u = raw[:, span]
        r = row_scale(u)
        gain = gq_ref[...] if head < query_heads else gk_ref[...]
        qkv_ref[:, span] = rotate(u * r * gain, cosine, sine).astype(BF16)
        scales = jnp.where(lane == head, r, scales)
    span = slice((query_heads + key_heads) * HEAD_SIZE, None)
    qkv_ref[:, span] = raw[:, span].astype(BF16)
    scale_ref[...] = scales


def project(x, gain, weights, gain_query, gain_key, cosine, sine, query_heads, key_heads):
    rows, width = x.shape
    wide = weights.shape[1]
    whole = lambda shape: pl.BlockSpec(shape, lambda i: (0, 0))
    block = lambda cols: pl.BlockSpec((BLOCK, cols), lambda i: (i, 0))
    return pl.pallas_call(
        functools.partial(project_kernel, query_heads, key_heads),
        grid=(rows // BLOCK,),
        in_specs=[
            block(width),
            whole((1, width)),
            whole((width, wide)),
            whole((1, HEAD_SIZE)),
            whole((1, HEAD_SIZE)),
            block(HEAD_SIZE),
            block(HEAD_SIZE),
        ],
        out_specs=[block(width), block(wide), block(HEAD_SIZE)],
        out_shape=[
            jax.ShapeDtypeStruct((rows, width), BF16),
            jax.ShapeDtypeStruct((rows, wide), BF16),
            jax.ShapeDtypeStruct((rows, HEAD_SIZE), F32),
        ],
        compiler_params=pltpu.CompilerParams(vmem_limit_bytes=VMEM_LIMIT),
        name="project",
    )(x, gain, weights, gain_query, gain_key, cosine, sine)


def first_place(info_ref, blocks, docs, places):
    start = jnp.zeros_like(places)
    for doc in range(docs):
        begin = info_ref[2 * blocks + doc]
        start = jnp.maximum(start, jnp.where(places >= begin, begin, 0))
    return start


def forward_kernel(group, blocks, docs, info_ref, q_ref, k_ref, v_ref, o_ref, lse_ref, wide_ref, acc_ref):
    i = pl.program_id(0)

    @pl.when(i == 0)
    def _():
        wide_ref[:, :HEAD_SIZE] = v_ref[...]
        wide_ref[:, HEAD_SIZE:] = jnp.ones_like(v_ref)

    queries = jnp.concatenate([q_ref[:, h * HEAD_SIZE : (h + 1) * HEAD_SIZE] for h in range(group)], axis=0)
    acc_ref[...] = jnp.zeros_like(acc_ref)
    shape = (group * BLOCK, BLOCK)

    def step(j, masked):
        rows = pl.ds(pl.multiple_of(j * BLOCK, BLOCK), BLOCK)
        weights = jnp.exp2(dot_nt(queries, k_ref[rows, :]) * (SCALE * LOG2E))
        if masked:
            places = i * BLOCK + lax.rem(lax.broadcasted_iota(jnp.int32, (group * BLOCK, 1), 0), BLOCK)
            start = first_place(info_ref, blocks, docs, places)
            other = j * BLOCK + lax.broadcasted_iota(jnp.int32, shape, 1)
            weights = jnp.where((other <= places) & (other >= start), weights, 0.0)
        acc_ref[...] += dot_nn(weights.astype(BF16), wide_ref[rows, :])

    low, clear = info_ref[i], info_ref[blocks + i]

    def masked_step(j, carry):
        step(j, True)
        return carry

    def clear_step(j, carry):
        step(j, False)
        return carry

    lax.fori_loop(low, jnp.minimum(clear, i), masked_step, 0)
    lax.fori_loop(jnp.minimum(clear, i), i, clear_step, 0)
    step(i, True)
    total = acc_ref[:, HEAD_SIZE:]
    out = (acc_ref[:, :HEAD_SIZE] / total).astype(BF16)
    for h in range(group):
        o_ref[:, h * HEAD_SIZE : (h + 1) * HEAD_SIZE] = out[h * BLOCK : (h + 1) * BLOCK]
    lse_ref[0] = lax.dot_general(
        jnp.full((8, HEAD_SIZE), 1.0 / HEAD_SIZE, F32),
        jnp.log2(total),
        (((1,), (1,)), ((), ())),
        precision=lax.Precision.HIGHEST,
        preferred_element_type=F32,
    )


def attention_forward(info, qkv, query_heads, key_heads, docs, kv):
    rows = qkv.shape[0]
    blocks = rows // BLOCK
    group = query_heads // key_heads
    wide = group * HEAD_SIZE
    return pl.pallas_call(
        functools.partial(forward_kernel, group, blocks, docs),
        grid_spec=pltpu.PrefetchScalarGridSpec(
            num_scalar_prefetch=1,
            grid=(blocks,),
            in_specs=[
                pl.BlockSpec((BLOCK, wide), lambda i, s: (i, kv)),
                pl.BlockSpec((rows, HEAD_SIZE), lambda i, s: (0, query_heads + kv)),
                pl.BlockSpec((rows, HEAD_SIZE), lambda i, s: (0, query_heads + key_heads + kv)),
            ],
            out_specs=[
                pl.BlockSpec((BLOCK, wide), lambda i, s: (i, 0)),
                pl.BlockSpec((1, 8, group * BLOCK), lambda i, s: (i, 0, 0)),
            ],
            scratch_shapes=[
                pltpu.VMEM((rows, 2 * HEAD_SIZE), BF16),
                pltpu.VMEM((group * BLOCK, 2 * HEAD_SIZE), F32),
            ],
        ),
        out_shape=[
            jax.ShapeDtypeStruct((rows, wide), BF16),
            jax.ShapeDtypeStruct((blocks, 8, group * BLOCK), F32),
        ],
        compiler_params=pltpu.CompilerParams(vmem_limit_bytes=VMEM_LIMIT),
        name="attention_forward",
    )(info, qkv, qkv, qkv)


def backward_kernel(
    group,
    query_heads,
    kv,
    blocks,
    docs,
    info_ref,
    q_ref,
    k_ref,
    v_ref,
    o_ref,
    do_ref,
    lse_ref,
    cos_ref,
    sin_ref,
    scale_ref,
    gq_ref,
    gk_ref,
    grad_ref,
    dgain_ref,
    dk_acc,
    dv_acc,
    dq_acc,
):
    i = pl.program_id(0)

    @pl.when(i == 0)
    def _():
        dk_acc[...] = jnp.zeros_like(dk_acc)
        dv_acc[...] = jnp.zeros_like(dv_acc)
        dgain_ref[...] = jnp.zeros_like(dgain_ref)

    def stacked(ref):
        return jnp.concatenate([ref[:, h * HEAD_SIZE : (h + 1) * HEAD_SIZE] for h in range(group)], axis=0)

    queries, grads = stacked(q_ref), stacked(do_ref)
    product = stacked(o_ref).astype(F32) * grads.astype(F32)
    delta = lax.dot_general(
        jnp.ones((8, HEAD_SIZE), F32),
        product,
        (((1,), (1,)), ((), ())),
        precision=lax.Precision.HIGHEST,
        preferred_element_type=F32,
    )[:1]
    lse = lse_ref[0, :1]
    dq_acc[...] = jnp.zeros_like(dq_acc)
    shape = (BLOCK, group * BLOCK)

    def step(j, masked):
        rows = pl.ds(pl.multiple_of(j * BLOCK, BLOCK), BLOCK)
        keys, values = k_ref[rows, :], v_ref[rows, :]
        probs = jnp.exp2(dot_nt(keys, queries) * (SCALE * LOG2E) - lse)
        if masked:
            places = i * BLOCK + lax.rem(lax.broadcasted_iota(jnp.int32, (1, group * BLOCK), 1), BLOCK)
            start = first_place(info_ref, blocks, docs, places)
            other = j * BLOCK + lax.broadcasted_iota(jnp.int32, shape, 0)
            probs = jnp.where((other <= places) & (other >= start), probs, 0.0)
        score_grad = (probs * (dot_nt(values, grads) - delta)).astype(BF16)
        dv_acc[rows, :] += dot_nn(probs.astype(BF16), grads)
        dk_acc[rows, :] += dot_nn(score_grad, queries)
        dq_acc[...] += dot_tn(score_grad, keys)

    low, clear = info_ref[i], info_ref[blocks + i]

    def masked_step(j, carry):
        step(j, True)
        return carry

    def clear_step(j, carry):
        step(j, False)
        return carry

    lax.fori_loop(low, jnp.minimum(clear, i), masked_step, 0)
    lax.fori_loop(jnp.minimum(clear, i), i, clear_step, 0)
    step(i, True)

    lane = lax.broadcasted_iota(jnp.int32, (BLOCK, HEAD_SIZE), 1)

    def raw_grad(grad, rotated, rows, head, gain):
        cosine, sine = cos_ref[rows, :], sin_ref[rows, :]
        r = jnp.sum(jnp.where(lane == head, scale_ref[rows, :], 0.0), axis=1, keepdims=True)
        unit = unrotate(rotated.astype(F32), cosine, sine) / gain
        back = unrotate(grad * SCALE, cosine, sine)
        scaled = back * gain
        raw = r * (scaled - unit * jnp.mean(scaled * unit, axis=1, keepdims=True))
        return raw.astype(BF16), jnp.sum(back * unit, axis=0, keepdims=True)

    here = pl.ds(pl.multiple_of(i * BLOCK, BLOCK), BLOCK)
    for h in range(group):
        span = slice(h * HEAD_SIZE, (h + 1) * HEAD_SIZE)
        raw, gain_grad = raw_grad(
            dq_acc[h * BLOCK : (h + 1) * BLOCK, :], q_ref[:, span], here, kv * group + h, gq_ref[...]
        )
        grad_ref[here, span] = raw
        dgain_ref[0:1, :] += gain_grad

    @pl.when(i == blocks - 1)
    def _():
        grad_ref[:, (group + 1) * HEAD_SIZE :] = dv_acc[...].astype(BF16)

        def finish(b, carry):
            rows = pl.ds(pl.multiple_of(b * BLOCK, BLOCK), BLOCK)
            raw, gain_grad = raw_grad(dk_acc[rows, :], k_ref[rows, :], rows, query_heads + kv, gk_ref[...])
            grad_ref[rows, group * HEAD_SIZE : (group + 1) * HEAD_SIZE] = raw
            dgain_ref[1:2, :] += gain_grad
            return carry

        lax.fori_loop(0, blocks, finish, 0)


def attention_backward(
    info, qkv, attended, grads, lse, cosine, sine, scales, gain_query, gain_key, query_heads, key_heads, docs, kv
):
    rows = qkv.shape[0]
    blocks = rows // BLOCK
    group = query_heads // key_heads
    wide = group * HEAD_SIZE
    own = pl.BlockSpec((BLOCK, wide), lambda i, s: (i, 0))
    whole = lambda shape: pl.BlockSpec(shape, lambda i, s: (0, 0))
    return pl.pallas_call(
        functools.partial(backward_kernel, group, query_heads, kv, blocks, docs),
        grid_spec=pltpu.PrefetchScalarGridSpec(
            num_scalar_prefetch=1,
            grid=(blocks,),
            in_specs=[
                pl.BlockSpec((BLOCK, wide), lambda i, s: (i, kv)),
                pl.BlockSpec((rows, HEAD_SIZE), lambda i, s: (0, query_heads + kv)),
                pl.BlockSpec((rows, HEAD_SIZE), lambda i, s: (0, query_heads + key_heads + kv)),
                own,
                own,
                pl.BlockSpec((1, 8, group * BLOCK), lambda i, s: (i, 0, 0)),
                whole((rows, HEAD_SIZE)),
                whole((rows, HEAD_SIZE)),
                whole((rows, HEAD_SIZE)),
                whole((1, HEAD_SIZE)),
                whole((1, HEAD_SIZE)),
            ],
            out_specs=[whole((rows, wide + 2 * HEAD_SIZE)), whole((8, HEAD_SIZE))],
            scratch_shapes=[
                pltpu.VMEM((rows, HEAD_SIZE), F32),
                pltpu.VMEM((rows, HEAD_SIZE), F32),
                pltpu.VMEM((group * BLOCK, HEAD_SIZE), F32),
            ],
        ),
        out_shape=[
            jax.ShapeDtypeStruct((rows, wide + 2 * HEAD_SIZE), BF16),
            jax.ShapeDtypeStruct((8, HEAD_SIZE), F32),
        ],
        compiler_params=pltpu.CompilerParams(vmem_limit_bytes=VMEM_LIMIT),
        name="attention_backward",
    )(info, qkv, qkv, qkv, attended, grads, lse, cosine, sine, scales, gain_query, gain_key)


def wide_block(ref):
    value = ref[...]
    return value.reshape(value.shape[0] * value.shape[2], value.shape[3])


def output_kernel(a_ref, w_ref, tokens_ref, gain_ref, middle_ref, normed_ref):
    r = pl.program_id(0)

    @pl.when(r == 0)
    def _():
        middle_ref[...] = tokens_ref[...].astype(F32)

    middle_ref[...] += dot_nt(a_ref[0], wide_block(w_ref))

    @pl.when(r == pl.num_programs(0) - 1)
    def _():
        middle = middle_ref[...]
        normed_ref[...] = (middle * row_scale(middle) * gain_ref[...]).astype(BF16)


def output_project(mixed, weights, tokens, gain):
    span, rows, cols = mixed.shape
    devices, _, shard, _ = weights.shape
    width = devices * shard
    whole = lambda shape: pl.BlockSpec(shape, lambda r: (0, 0), pipeline_mode=pl.Buffered(1))
    return pl.pallas_call(
        output_kernel,
        grid=(span,),
        in_specs=[
            pl.BlockSpec((1, rows, cols), lambda r: (r, 0, 0)),
            pl.BlockSpec((devices, 1, shard, cols), lambda r: (0, r, 0, 0)),
            whole((rows, width)),
            whole((1, width)),
        ],
        out_specs=[whole((rows, width)), whole((rows, width))],
        out_shape=[jax.ShapeDtypeStruct((rows, width), F32), jax.ShapeDtypeStruct((rows, width), BF16)],
        compiler_params=pltpu.CompilerParams(vmem_limit_bytes=VMEM_LIMIT),
        name="output_project",
    )(mixed, weights, tokens, gain)


def output_back_kernel(b_ref, a_ref, w_ref, da_ref, dw_ref, bt_ref):
    @pl.when(pl.program_id(0) == 0)
    def _():
        bt_ref[...] = b_ref[...].T

    da_ref[0] = dot_nn(b_ref[...], wide_block(w_ref)).astype(BF16)
    dw_ref[...] = dot_nn(bt_ref[...], a_ref[0]).astype(BF16).reshape(dw_ref.shape)


def output_back(branch, mixed, weights):
    span, rows, cols = mixed.shape
    devices, _, shard, _ = weights.shape
    width = devices * shard
    chunk = pl.BlockSpec((1, rows, cols), lambda r: (r, 0, 0))
    wide = pl.BlockSpec((devices, 1, shard, cols), lambda r: (0, r, 0, 0))
    return pl.pallas_call(
        output_back_kernel,
        grid=(span,),
        in_specs=[
            pl.BlockSpec((rows, width), lambda r: (0, 0), pipeline_mode=pl.Buffered(1)),
            chunk,
            wide,
        ],
        out_specs=[chunk, wide],
        scratch_shapes=[pltpu.VMEM((width, rows), BF16)],
        out_shape=[
            jax.ShapeDtypeStruct((span, rows, cols), BF16),
            jax.ShapeDtypeStruct((devices, span, shard, cols), BF16),
        ],
        compiler_params=pltpu.CompilerParams(vmem_limit_bytes=VMEM_LIMIT),
        name="output_back",
    )(branch, mixed, weights)


def feed_kernel(last, x_ref, c_ref, w_ref, *refs):
    if last:
        (out_in, ng_in, middle_ref, gain_ref, result_ref, grad_ref, branch_ref, dgain_ref, dw_ref, out_s, ng_s) = refs[:11]
        act_s, gg_s, ug_s, xt_s, ct_s = refs[11:]
    else:
        out_s, ng_s, dw_ref, act_s, gg_s, ug_s, xt_s, ct_s = refs
    j = pl.program_id(0)
    rows_all, width = x_ref.shape
    hidden = act_s.shape[1]
    devices, _, shard, _ = w_ref.shape
    chunk = rows_all // 2

    @pl.when(j == 0)
    def _():
        xt_s[...] = x_ref[...].T
        ct_s[...] = c_ref[...].T
        out_s[...] = out_in[...] if last else jnp.zeros_like(out_s)
        ng_s[...] = ng_in[...] if last else jnp.zeros_like(ng_s)

    def part(k):
        return w_ref[:, 0, :, k * hidden : (k + 1) * hidden].reshape(width, hidden)

    def rows_step(m, carry):
        rows = pl.ds(pl.multiple_of(m * chunk, chunk), chunk)
        gate = dot_nn(x_ref[rows, :], part(0))
        upward = dot_nn(x_ref[rows, :], part(1))
        act_grad = dot_nn(c_ref[rows, :], part(2))
        sig = 1.0 / (1.0 + jnp.exp(-gate))
        silu = gate * sig
        act = (silu * upward).astype(BF16)
        up_grad = (act_grad * silu).astype(BF16)
        gate_grad = (act_grad * upward * sig * (1.0 + gate * (1.0 - sig))).astype(BF16)
        act_s[rows, :] = act
        ug_s[rows, :] = up_grad
        gg_s[rows, :] = gate_grad
        out_s[rows, :] += dot_nt(act, part(2))
        ng_s[rows, :] += dot_nt(gate_grad, part(0)) + dot_nt(up_grad, part(1))
        return carry

    lax.fori_loop(0, rows_all // chunk, rows_step, 0)

    group = BLOCK // shard

    def grad_step(m, carry):
        rows = pl.ds(pl.multiple_of(m * BLOCK, BLOCK), BLOCK)
        to = pl.ds(m * group, group)
        for k, left, right in ((0, xt_s, gg_s), (1, xt_s, ug_s), (2, ct_s, act_s)):
            value = dot_nn(left[rows, :], right[...]).astype(BF16)
            dw_ref[to, 0, :, k * hidden : (k + 1) * hidden] = value.reshape(group, shard, hidden)
        return carry

    lax.fori_loop(0, width // BLOCK, grad_step, 0)

    if not last:
        return

    @pl.when(j == pl.num_programs(0) - 1)
    def _():
        middle = middle_ref[...]
        result_ref[...] = (middle + out_s[...]).astype(BF16)
        r = row_scale(middle)
        unit = middle * r
        dgain_ref[...] = jnp.broadcast_to(jnp.sum(ng_s[...] * unit, axis=0, keepdims=True), dgain_ref.shape)
        scaled = ng_s[...] * gain_ref[...]
        grad = c_ref[...].astype(F32) + r * (scaled - unit * jnp.mean(scaled * unit, axis=-1, keepdims=True))
        grad_ref[...] = grad
        branch_ref[...] = grad.astype(BF16)


def feed(x, cot, weights, *rest):
    rows, width = x.shape
    devices, span, shard, cols = weights.shape
    hidden = cols // 3
    last = len(rest) > 0
    whole = lambda shape: pl.BlockSpec(shape, lambda j: (0, 0), pipeline_mode=pl.Buffered(1))
    chunk = pl.BlockSpec((devices, 1, shard, cols), lambda j: (0, j, 0, 0))
    full = whole((rows, width))
    grads = jax.ShapeDtypeStruct((devices, span, shard, cols), BF16)
    shape = lambda kind: jax.ShapeDtypeStruct((rows, width), kind)
    sums = [pltpu.VMEM((rows, width), F32)] * 2 if last else []
    return pl.pallas_call(
        functools.partial(feed_kernel, last),
        grid=(span,),
        in_specs=[full, full, chunk] + ([full, full, full, whole((1, width))] if last else []),
        out_specs=[full, full, full, whole((8, width)), chunk] if last else [full, full, chunk],
        out_shape=[shape(BF16), shape(F32), shape(BF16), jax.ShapeDtypeStruct((8, width), F32), grads]
        if last
        else [shape(F32), shape(F32), grads],
        scratch_shapes=sums + [pltpu.VMEM((rows, hidden), BF16)] * 3 + [pltpu.VMEM((width, rows), BF16)] * 2,
        compiler_params=pltpu.CompilerParams(vmem_limit_bytes=VMEM_LIMIT),
        name="feed_forward",
    )(x, cot, weights, *rest)


def local(
    tokens,
    lengths,
    row_order,
    attention_gain,
    query_gain,
    key_gain,
    query_weight,
    key_matrix,
    value_matrix,
    output_weight,
    feedforward_gain,
    gate_weight,
    up_weight,
    down_weight,
    cotangent,
):
    span = lax.axis_size("tensor")
    pairs = lax.axis_size("dp") // 2
    half = span // 2
    rows, width = tokens.shape
    group_rows = rows * span
    blocks = group_rows // BLOCK
    docs = lengths.shape[1]
    query_heads = query_weight.shape[1] // HEAD_SIZE
    key_heads = key_matrix.shape[1] // HEAD_SIZE
    head_columns = query_weight.shape[1]
    hidden_columns = gate_weight.shape[1]
    shard = query_weight.shape[0]

    dp, t = lax.axis_index("dp"), lax.axis_index("tensor")
    p, c = dp // 2, lax.rem(dp, 2)
    q = t // half
    settled = c == q

    def send(x, route):
        moves = []
        for pp in range(pairs):
            for cc in range(2):
                for tt in range(span):
                    to = route(pp, cc, tt)
                    if to is not None:
                        moves.append(((pp * 2 + cc) * span + tt, (to[0] * 2 + to[1]) * span + to[2]))
        return lax.ppermute(x, AXES, moves)

    def sibling(x):
        return send(x, lambda pp, cc, tt: (pp, 1 - cc, tt))

    def swap(x):
        moved = send(x, lambda pp, cc, tt: (pp, 1 - cc, span - 1 - tt) if cc != tt // half else None)
        return jnp.where(settled, x, moved)

    def ordered(mine, other, first):
        return jnp.where(first, mine, other), jnp.where(first, other, mine)

    def add(*terms):
        total = terms[0].astype(F32)
        for term in terms[1:]:
            total = total + term.astype(F32)
        return total.astype(BF16)

    one_off = lambda pp, cc, tt: (pp ^ 1, cc, tt)
    two_off = lambda pp, cc, tt: (pp ^ 2, cc, tt)

    def scatter_start(take):
        if pairs != 4:
            return ()
        cut = shard
        return send(take(p ^ 3, 0, cut), one_off), send(take(p ^ 3, cut, cut), two_off)

    def scatter_next(take, arrived):
        if pairs != 4:
            return ()
        cut = shard
        one = jnp.concatenate([take(p ^ 1, 0, cut), add(take(p ^ 1, cut, cut), arrived[1])], axis=0)
        two = jnp.concatenate([add(take(p ^ 2, 0, cut), arrived[0]), take(p ^ 2, cut, cut)], axis=0)
        return send(one, one_off), send(two, two_off)

    def scatter_end(take, later):
        size = 2 * shard
        if pairs == 4:
            return add(take(p, 0, size), *later)
        pieces = [take(p ^ k, 0, size) for k in range(pairs)]
        while len(pieces) > 1:
            keep = len(pieces) // 2
            moved = send(jnp.concatenate(pieces[keep:], axis=0), lambda pp, cc, tt: (pp ^ keep, cc, tt))
            pieces = [add(pieces[k], moved[k * size : (k + 1) * size]) for k in range(keep)]
        return pieces[0]

    def taker(parts):
        def take(at, shift, count):
            rows_of = lambda x: lax.dynamic_slice(x, (at * 2 * shard + shift, 0), (count, x.shape[1]))
            cols = [add(*[rows_of(x) for x in terms]) if len(terms) > 1 else rows_of(terms[0]) for terms in parts]
            return jnp.concatenate(cols, axis=1) if len(cols) > 1 else cols[0]

        return take

    never = row_order[0, 0] < 0

    def behind(x, other):
        return jnp.where(never, other[0, 0].astype(x.dtype), x)

    def line(x, steps):
        return [send(x, lambda pp, cc, tt: (pp, cc, tt ^ r)) for r in steps]

    def gather_wide(pieces):
        cols = pieces[0].shape[1]
        out = by_rows(lax.all_gather(by_rows(jnp.concatenate(pieces, axis=0)), "dp", axis=0, tiled=True))
        return out.reshape(2 * pairs, len(pieces), shard, cols)

    def scatter_wide(grads):
        devices, count, _, cols = grads.shape
        out = by_rows(grads.reshape(devices * count * shard, cols))
        out = by_rows(lax.psum_scatter(out, "dp", scatter_dimension=0, tiled=True))
        return [out[r * shard : (r + 1) * shard] for r in range(count)]

    def line_back(pieces, first):
        return [
            piece if r == 0 else send(piece, lambda pp, cc, tt: (pp, cc, tt ^ r))
            for r, piece in enumerate(pieces, start=first)
        ]

    heads_local = by_rows(jnp.concatenate([query_weight, key_matrix, value_matrix], axis=1))
    feed_local = by_rows(jnp.concatenate([gate_weight, up_weight, down_weight.T], axis=1))
    gains = jnp.concatenate([attention_gain, query_gain, key_gain, feedforward_gain])
    small, tiny = attention_gain.shape[0], query_gain.shape[0]
    few, lanes = gains.shape[0], -(-gains.shape[0] // 128) * 128
    gains = jnp.broadcast_to(jnp.pad(gains, (0, lanes - few))[None], (16, lanes))
    facts = jnp.concatenate([row_order[0], lengths[0]])
    fact_rows = -(-facts.shape[0] // 1024) * 8
    facts = jnp.pad(facts, (0, fact_rows * 128 - facts.shape[0])).reshape(fact_rows, 128)
    tokens_all, heads_weights, output_line, gains, facts_moved = first_transfers(
        pairs, span, tokens, heads_local, by_rows(output_weight.T), gains, facts
    )
    swapped = tokens_all[0]
    tokens_all = tokens_all.reshape(group_rows, width)
    feed_weights = [gather_wide([feed_local])]
    output_weights = gather_wide([output_line[r] for r in range(span)])
    feed_weights.append(gather_wide(line(behind(feed_local, swapped), range(1, span))))

    gains = gains.reshape(2 * pairs, 16, lanes)[:, 0, :few].astype(F32)
    gain_one = gains[:, :small].reshape(1, width)
    gain_query = gains[:, small : small + tiny].reshape(1, HEAD_SIZE)
    gain_key = gains[:, small + tiny : small + 2 * tiny].reshape(1, HEAD_SIZE)
    gain_two = gains[:, small + 2 * tiny : small + 2 * tiny + small].reshape(1, width)
    facts = jnp.where(settled, facts, facts_moved).reshape(-1)[: group_rows + docs]
    order, length = facts[:group_rows].reshape(span, rows), facts[group_rows:]
    places = []
    for k in range(span):
        tt, cc = t ^ (k % half), c ^ (k // half)
        places.append(lax.dynamic_index_in_dim(order, jnp.where(cc == tt // half, tt, span - 1 - tt), 0, False))
    places = jnp.concatenate(places)
    inverse = jnp.argsort(places)
    before = jnp.arange(docs)[None, :] < jnp.arange(docs)[:, None]
    starts = jnp.sum(jnp.where(before, length[None, :], 0), axis=1).astype(jnp.int32)

    def start_of(place):
        return jnp.max(jnp.where(place[:, None] >= starts[None, :], starts[None, :], 0), axis=1)

    index = jnp.arange(blocks, dtype=jnp.int32) * BLOCK
    low = start_of(index) // BLOCK
    clear = (start_of(index + BLOCK - 1) + BLOCK - 1) // BLOCK
    info = jnp.concatenate([low, clear, starts]).astype(jnp.int32)
    index = jnp.arange(group_rows, dtype=jnp.int32)
    position = (index - start_of(index)).astype(F32)
    inverse_rate = THETA ** (-(jnp.arange(HEAD_SIZE // 2, dtype=F32) * 2.0 / HEAD_SIZE))
    angle = position[:, None] * inverse_rate[None, :]
    cosine, sine = jnp.cos(angle), jnp.sin(angle)
    cosine = jnp.concatenate([cosine, cosine], axis=1)
    sine = jnp.concatenate([-sine, sine], axis=1)

    tokens_sorted = jnp.take(tokens_all, inverse, axis=0, mode="clip")
    cot_own = swap(cotangent)
    normed, qkv, scales = project(
        tokens_sorted, gain_one, heads_weights, gain_query, gain_key, cosine, sine, query_heads, key_heads
    )

    def exchange(parts):
        out = [parts[0]]
        for k in range(1, span):
            out.append(send(parts[k], lambda pp, cc, tt: (pp, cc ^ (k // half), tt ^ (k % half))))
        return out

    def by_chunk(parts):
        return [jnp.where(settled, parts[r], parts[(1 - r // half) * half + r % half]) for r in range(span)]

    attended, lse, chunks = [], [], []
    for kv in range(key_heads):
        out, total = attention_forward(info, qkv, query_heads, key_heads, docs, kv)
        attended.append(out)
        lse.append(total)
        out = jnp.take(out, places, axis=0, mode="clip")
        chunks.append(by_chunk(exchange([out[k * rows : (k + 1) * rows] for k in range(span)])))
    mixed = jnp.stack([jnp.concatenate([chunk[r] for chunk in chunks], axis=1) for r in range(span)])

    hidden = gate_weight.shape[1]
    middle, normed_two = output_project(mixed, output_weights, swapped, gain_two)
    out, normed_grad, first_grad = feed(normed_two, cot_own, feed_weights[0])
    result, middle_grad, branch, gain_two_grad, second_grad = feed(
        normed_two, cot_own, feed_weights[1], out, normed_grad, middle, gain_two
    )
    feed_back = line_back(scatter_wide(first_grad), 0) + line_back(scatter_wide(second_grad), 1)

    mixed_grad, output_grad = output_back(branch, mixed, output_weights)
    merged = by_chunk([mixed_grad[r] for r in range(span)])
    per_head = head_columns // key_heads
    grad_chunks = [exchange([x[:, kv * per_head : (kv + 1) * per_head] for x in merged]) for kv in range(key_heads)]
    output_sum = line_back(scatter_wide(output_grad), 0)
    layer_output = swap(result)

    head_grads, head_gains = [], 0.0
    for kv in range(key_heads):
        attended_grad = jnp.take(jnp.concatenate(grad_chunks[kv], axis=0), inverse, axis=0, mode="clip")
        grads, gains_of = attention_backward(
            info,
            qkv,
            attended[kv],
            attended_grad,
            lse[kv],
            cosine,
            sine,
            scales,
            gain_query,
            gain_key,
            query_heads,
            key_heads,
            docs,
            kv,
        )
        head_grads.append(grads)
        head_gains = head_gains + gains_of
    wide_q, wide_k = head_columns // key_heads, HEAD_SIZE
    qkv_grad = jnp.concatenate(
        [g[:, :wide_q] for g in head_grads]
        + [g[:, wide_q : wide_q + wide_k] for g in head_grads]
        + [g[:, wide_q + wide_k :] for g in head_grads],
        axis=1,
    )
    partial = dot_nt(jnp.take(qkv_grad, places, axis=0, mode="clip"), heads_weights).astype(BF16)
    parts = [partial[k * rows : (k + 1) * rows] for k in range(span)]
    moved = sibling(jnp.concatenate(parts[half:], axis=0))
    heads_grad = dot_tn(normed, qkv_grad).astype(BF16)
    heads = taker([(heads_grad,)])
    parts = [add(parts[k], moved[k * rows : (k + 1) * rows]) for k in range(half)]
    heads_arrived = scatter_start(heads)
    while len(parts) > 1:
        keep = len(parts) // 2
        moved = send(jnp.concatenate(parts[keep:], axis=0), lambda pp, cc, tt: (pp, cc, tt ^ keep))
        parts = [add(parts[k], moved[k * rows : (k + 1) * rows]) for k in range(keep)]
    heads_later = scatter_next(heads, heads_arrived)
    mine = scatter_end(heads, heads_later)
    moved = send(mine, lambda pp, cc, tt: (pp, cc, (tt + half) % span) if cc != tt // half else None)

    normed_grad = parts[0].astype(F32)
    inputs = swapped.astype(F32)
    r_one = row_scale(inputs)
    unit_one = inputs * r_one
    gain_one_grad = jnp.sum(normed_grad * unit_one, axis=0)
    scaled = normed_grad * gain_one
    input_grad = swap(
        (middle_grad + r_one * (scaled - unit_one * jnp.mean(scaled * unit_one, axis=-1, keepdims=True))).astype(BF16)
    )

    summed = mine.astype(F32) + moved.astype(F32)
    top, bottom = summed[:shard], summed[shard:]
    other = jnp.where(c == 0, bottom, top).astype(BF16)
    moved = send(other, lambda pp, cc, tt: (pp, 1 - cc, tt) if cc == tt // half else None).astype(F32)
    summed = jnp.where(settled, jnp.where(c == 0, top, bottom), moved)
    key_columns = key_heads * HEAD_SIZE

    def total(pieces):
        out = pieces[0].astype(F32)
        for piece in pieces[1:]:
            out = out + piece.astype(F32)
        return out

    wide_sum, output_sum = total(feed_back), total(output_sum)
    gain_sums = lax.psum(jnp.concatenate([gain_one_grad, head_gains[0], head_gains[1], gain_two_grad[0]]), AXES)
    cut = lambda at, size: lax.dynamic_slice(gain_sums, (at + dp * size,), (size,))
    return (
        layer_output,
        input_grad,
        cut(0, small),
        cut(width, tiny),
        cut(width + HEAD_SIZE, tiny),
        summed[:, :head_columns],
        summed[:, head_columns : head_columns + key_columns],
        summed[:, head_columns + key_columns :],
        output_sum.T,
        cut(width + 2 * HEAD_SIZE, small),
        wide_sum[:, :hidden],
        wide_sum[:, hidden : 2 * hidden],
        wide_sum[:, 2 * hidden :].T,
    )


def solution(mesh):
    placed = (
        P(AXES, None),
        P("dp", None),
        P("dp", None),
        P("dp"),
        P("dp"),
        P("dp"),
        P("dp", "tensor"),
        P("dp", "tensor"),
        P("dp", "tensor"),
        P("tensor", "dp"),
        P("dp"),
        P("dp", "tensor"),
        P("dp", "tensor"),
        P("tensor", "dp"),
        P(AXES, None),
    )
    return jax.shard_map(
        local,
        mesh=mesh,
        in_specs=placed,
        out_specs=(
            P(AXES, None),
            P(AXES, None),
            P("dp"),
            P("dp"),
            P("dp"),
            P("dp", "tensor"),
            P("dp", "tensor"),
            P("dp", "tensor"),
            P("tensor", "dp"),
            P("dp"),
            P("dp", "tensor"),
            P("dp", "tensor"),
            P("tensor", "dp"),
        ),
        check_vma=False,
    )
```

```python
import functools

import jax
import jax.numpy as jnp
from jax import lax
from jax.experimental.layout import Layout, with_layout_constraint
from jax.experimental import pallas as pl
from jax.experimental.pallas import tpu as pltpu
from jax.sharding import PartitionSpec as P

HEAD_SIZE = 128
EPSILON = 1e-06
THETA = 1000000.0
AXES = ("dp", "tensor")
ROWS = 256
BLOCK = 512
STEP = 512
SCALE = HEAD_SIZE ** (-0.5)
LOG2E = 1.4426950408889634
VMEM_LIMIT = 56 * 1024 * 1024
F32 = jnp.float32
BF16 = jnp.bfloat16


def dot_nn(left, right):
    return lax.dot_general(left, right, (((1,), (0,)), ((), ())), preferred_element_type=F32)


def dot_nt(left, right):
    return lax.dot_general(left, right, (((1,), (1,)), ((), ())), preferred_element_type=F32)


def dot_tn(left, right):
    return lax.dot_general(left, right, (((0,), (0,)), ((), ())), preferred_element_type=F32)


def by_rows(x):
    return with_layout_constraint(x, Layout(major_to_minor=tuple(range(x.ndim))))


def row_scale(rows):
    return lax.rsqrt(jnp.mean(rows * rows, axis=-1, keepdims=True) + EPSILON)


def rotate(rows, cosine, sine):
    return rows * cosine + pltpu.roll(rows, HEAD_SIZE // 2, 1) * sine


def unrotate(rows, cosine, sine):
    return rows * cosine - pltpu.roll(rows, HEAD_SIZE // 2, 1) * sine


CHUNKS = 4


def first_kernel(
    pairs,
    span,
    tokens_ref,
    heads_ref,
    output_ref,
    gains_ref,
    facts_ref,
    tokens_out,
    heads_out,
    output_out,
    gains_out,
    facts_out,
    send_sems,
    recv_sems,
    local_sems,
):
    half = span // 2
    dp, t = lax.axis_index("dp"), lax.axis_index("tensor")
    p, c = dp // 2, lax.rem(dp, 2)
    q = t // half
    settled = c == q
    rows = tokens_ref.shape[0]
    piece = rows // CHUNKS
    shard = heads_ref.shape[0]
    small = gains_ref.shape[0]
    place = lambda pp, cc, tt: (pp * 2 + cc, tt)

    barrier = pltpu.get_barrier_semaphore()
    greeted = 0
    for k in range(1, 2 * span):
        pl.semaphore_signal(
            barrier,
            device_id=place(p, c ^ (k // span), t ^ (k % span)),
            device_id_type=pl.DeviceIdType.MESH,
        )
        greeted += 1
    for k in range(1, pairs):
        for cc in range(2):
            pl.semaphore_signal(
                barrier, device_id=place(p ^ k, c ^ cc, t), device_id_type=pl.DeviceIdType.MESH
            )
            greeted += 1
    pl.semaphore_wait(barrier, greeted)

    used = [0]

    def number(count=1):
        used[0] += count
        return used[0] - count

    def remote(src, dst, sem, to, arrival=None):
        return pltpu.make_async_remote_copy(
            src_ref=src,
            dst_ref=dst,
            send_sem=send_sems.at[sem],
            recv_sem=recv_sems.at[sem if arrival is None else arrival],
            device_id=to,
            device_id_type=pl.DeviceIdType.MESH,
        )

    def rows_of(i):
        return pl.ds(i * piece, piece)

    swap_sem = number(CHUNKS)
    line_sems = [[number() for _ in range(CHUNKS)] for _ in range(half)]
    side_sems = [[number() for _ in range(CHUNKS)] for _ in range(half)]
    near_sem, far_sem = number(), number(2)
    pair_sems = [number() for _ in range(pairs)]
    output_sems = [number() for _ in range(span)]
    gain_sems = [number() for _ in range(2 * pairs)]
    fact_sem = number()

    sibling = place(p, 1 - c, t)
    partner = place(p, 1 - c, span - 1 - t)
    swaps = [
        remote(tokens_ref.at[rows_of(i)], tokens_out.at[0, rows_of(i)], swap_sem + i, partner) for i in range(CHUNKS)
    ]
    own_rows = pl.ds(dp * shard, shard)
    far = lax.rem(t + half, span)
    near_copy = remote(heads_ref, heads_out.at[own_rows], near_sem, sibling)
    far_copy = remote(heads_ref, heads_out.at[own_rows], far_sem + c, place(p, q, far))
    local_tokens = pltpu.make_async_copy(tokens_ref, tokens_out.at[0], local_sems.at[0])
    local_heads = pltpu.make_async_copy(heads_ref, heads_out.at[own_rows], local_sems.at[1])
    local_output = pltpu.make_async_copy(output_ref, output_out.at[0], local_sems.at[2])
    local_gains = pltpu.make_async_copy(gains_ref, gains_out.at[pl.ds(dp * small, small)], local_sems.at[3])

    fact_copy = remote(facts_ref, facts_out, fact_sem, sibling)
    fact_copy.start()
    far_copy.start()

    @pl.when(settled)
    def _():
        local_heads.start()
        local_tokens.start()

    @pl.when(jnp.logical_not(settled))
    def _():
        near_copy.start()
        for copy in swaps:
            copy.start()

    gain_copies = []
    for k in range(1, 2 * pairs):
        to = (p ^ (k // 2), c ^ (k % 2))
        gain_copies.append(
            remote(gains_ref, gains_out.at[pl.ds(dp * small, small)], gain_sems[k], place(to[0], to[1], t))
        )
    local_gains.start()
    local_output.start()
    for copy in gain_copies:
        copy.start()

    def spread(i, source):
        copies = [remote(source, tokens_out.at[half, rows_of(i)], side_sems[0][i], sibling)]
        for k in range(1, half):
            copies.append(remote(source, tokens_out.at[k, rows_of(i)], line_sems[k][i], place(p, c, t ^ k)))
        return copies

    @pl.when(settled)
    def _():
        for i in range(CHUNKS):
            for copy in spread(i, tokens_ref.at[rows_of(i)]):
                copy.start()

    output_copies = [
        remote(output_ref, output_out.at[r], output_sems[r], place(p, c, t ^ r)) for r in range(1, span)
    ]

    @pl.when(settled)
    def _():
        local_heads.wait()
        near_copy.wait_recv()

    @pl.when(jnp.logical_not(settled))
    def _():
        near_copy.wait_send()
        for cc in range(2):
            remote(heads_ref, heads_out.at[own_rows], far_sem, sibling, far_sem + cc).wait_recv()

    both = heads_out.at[pl.ds(p * 2 * shard, 2 * shard)]
    pair_copies = [remote(both, both, pair_sems[k], place(p ^ k, c, t)) for k in range(1, pairs)]
    for copy in pair_copies:
        copy.start()

    @pl.when(jnp.logical_not(settled))
    def _():
        for i in range(CHUNKS):
            swaps[i].wait_recv()
            for copy in spread(i, tokens_out.at[0, rows_of(i)]):
                copy.start()

    for copy in output_copies:
        copy.start()

    forwards = []
    for i in range(CHUNKS):
        for k in range(1, half):
            block = tokens_out.at[k, rows_of(i)]
            remote(block, block, line_sems[k][i], sibling).wait_recv()
            copy = remote(block, tokens_out.at[half + k, rows_of(i)], side_sems[k][i], sibling)
            copy.start()
            forwards.append(copy)

    far_copy.wait_send()
    fact_copy.wait()
    local_output.wait()
    local_gains.wait()

    @pl.when(settled)
    def _():
        local_tokens.wait()

    @pl.when(jnp.logical_not(settled))
    def _():
        for copy in swaps:
            copy.wait_send()

    for i in range(CHUNKS):
        for index, copy in enumerate(spread(i, tokens_out.at[0, rows_of(i)])):
            copy.wait_send()
            if index == 0:
                copy.wait_recv()
    for copy in forwards + pair_copies + output_copies + gain_copies:
        copy.wait()


def first_transfers(pairs, span, tokens, heads, output, gains, facts):
    rows, width = tokens.shape
    shard = heads.shape[0]
    half = span // 2
    copies = CHUNKS * (1 + 2 * half) + 3 + pairs + span + 2 * pairs + 1
    any_ref = pl.BlockSpec(memory_space=pl.ANY)
    return pl.pallas_call(
        functools.partial(first_kernel, pairs, span),
        in_specs=[any_ref] * 5,
        out_specs=[any_ref] * 5,
        out_shape=[
            jax.ShapeDtypeStruct((span, rows, width), tokens.dtype),
            jax.ShapeDtypeStruct((2 * pairs * shard, heads.shape[1]), heads.dtype),
            jax.ShapeDtypeStruct((span, *output.shape), output.dtype),
            jax.ShapeDtypeStruct((2 * pairs * gains.shape[0], gains.shape[1]), gains.dtype),
            jax.ShapeDtypeStruct(facts.shape, facts.dtype),
        ],
        scratch_shapes=[
            pltpu.SemaphoreType.DMA((copies,)),
            pltpu.SemaphoreType.DMA((copies,)),
            pltpu.SemaphoreType.DMA((4,)),
        ],
        compiler_params=pltpu.CompilerParams(collective_id=0, has_side_effects=True),
        cost_estimate=pl.CostEstimate(flops=0, bytes_accessed=150_000_000, transcendentals=0),
        name="first_transfers",
    )(tokens, heads, output, gains, facts)


def project_kernel(
    query_heads, key_heads, x_ref, gain_ref, w_ref, gq_ref, gk_ref, cos_ref, sin_ref, normed_ref, qkv_ref, scale_ref
):
    x = x_ref[...].astype(F32)
    normed = (x * row_scale(x) * gain_ref[...]).astype(BF16)
    normed_ref[...] = normed
    raw = dot_nn(normed, w_ref[...])
    cosine, sine = cos_ref[...], sin_ref[...]
    lane = lax.broadcasted_iota(jnp.int32, (x.shape[0], HEAD_SIZE), 1)
    scales = jnp.zeros((x.shape[0], HEAD_SIZE), F32)
    group = query_heads // key_heads
    for at in range(query_heads + 2 * key_heads):
        kv, kind = at // (group + 2), at % (group + 2)
        span = slice(at * HEAD_SIZE, (at + 1) * HEAD_SIZE)
        u = raw[:, span]
        if kind == group + 1:
            qkv_ref[:, span] = u.astype(BF16)
            continue
        r = row_scale(u)
        gain = gq_ref[...] if kind < group else gk_ref[...]
        qkv_ref[:, span] = rotate(u * r * gain, cosine, sine).astype(BF16)
        scales = jnp.where(lane == kind, r, scales) if kind else jnp.broadcast_to(r, scales.shape)
        if kind == group:
            scale_ref[kv] = scales


def project(x, gain, weights, gain_query, gain_key, cosine, sine, query_heads, key_heads):
    rows, width = x.shape
    wide = weights.shape[1]
    whole = lambda shape: pl.BlockSpec(shape, lambda i: (0, 0))
    block = lambda cols: pl.BlockSpec((ROWS, cols), lambda i: (i, 0))
    return pl.pallas_call(
        functools.partial(project_kernel, query_heads, key_heads),
        grid=(rows // ROWS,),
        in_specs=[
            block(width),
            whole((1, width)),
            whole((width, wide)),
            whole((1, HEAD_SIZE)),
            whole((1, HEAD_SIZE)),
            block(HEAD_SIZE),
            block(HEAD_SIZE),
        ],
        out_specs=[block(width), block(wide), pl.BlockSpec((key_heads, ROWS, HEAD_SIZE), lambda i: (0, i, 0))],
        out_shape=[
            jax.ShapeDtypeStruct((rows, width), BF16),
            jax.ShapeDtypeStruct((rows, wide), BF16),
            jax.ShapeDtypeStruct((key_heads, rows, HEAD_SIZE), F32),
        ],
        compiler_params=pltpu.CompilerParams(vmem_limit_bytes=VMEM_LIMIT),
        name="project",
    )(x, gain, weights, gain_query, gain_key, cosine, sine)


def first_place(info_ref, blocks, docs, places):
    start = jnp.zeros_like(places)
    for doc in range(docs):
        begin = info_ref[2 * blocks + doc]
        start = jnp.maximum(start, jnp.where(places >= begin, begin, 0))
    return start


def across(values, terms):
    ones = jnp.ones((8, HEAD_SIZE), BF16)
    total = None
    for _ in range(terms):
        part = values.astype(BF16)
        values = values - part.astype(F32)
        total = dot_nt(ones, part) if total is None else total + dot_nt(ones, part)
    return total


def keep_padded(pairs):
    for ref, kept in pairs:
        rows = ref.shape[0]
        kept[:rows, : ref.shape[1]] = ref[...]
        kept[rows:, : ref.shape[1]] = jnp.zeros((kept.shape[0] - rows, ref.shape[1]), BF16)


def forward_kernel(group, blocks, docs, info_ref, q_ref, k_ref, v_ref, o_ref, lse_ref, keys_s, wide_s, acc_ref):
    i = pl.program_id(1)

    @pl.when(i == 0)
    def _():
        keep_padded(((k_ref, keys_s), (v_ref, wide_s)))
        wide_s[:, HEAD_SIZE:] = jnp.ones((wide_s.shape[0], HEAD_SIZE), BF16)

    acc_ref[...] = jnp.zeros_like(acc_ref)
    places = i * BLOCK + lax.broadcasted_iota(jnp.int32, (BLOCK, 1), 0)
    start = first_place(info_ref, blocks, docs, places)
    low = info_ref[i]

    def step(m, carry):
        base = (low + m * (STEP // BLOCK)) * BLOCK
        rows = pl.ds(pl.multiple_of(base, BLOCK), STEP)
        keys, values = keys_s[rows, :], wide_s[rows, :]
        other = base + lax.broadcasted_iota(jnp.int32, (BLOCK, STEP), 1)
        keep = (other <= places) & (other >= start)
        scores = [dot_nt(q_ref[:, h * HEAD_SIZE : (h + 1) * HEAD_SIZE], keys) for h in range(group)]
        for h in range(group):
            weights = jnp.where(keep, jnp.exp2(scores[h] * (SCALE * LOG2E)), 0.0)
            acc_ref[h * BLOCK : (h + 1) * BLOCK, :] += dot_nn(weights.astype(BF16), values)
        return carry

    lax.fori_loop(0, (i - low) // (STEP // BLOCK) + 1, step, 0)
    total = acc_ref[:, HEAD_SIZE:]
    out = (acc_ref[:, :HEAD_SIZE] / total).astype(BF16)
    for h in range(group):
        o_ref[0, :, h * HEAD_SIZE : (h + 1) * HEAD_SIZE] = out[h * BLOCK : (h + 1) * BLOCK]
    lse_ref[0, 0] = across(jnp.log2(total) * (1.0 / HEAD_SIZE), 3)


def head_specs(rows, group, first):
    wide = group * HEAD_SIZE
    return [
        pl.BlockSpec((BLOCK, wide), lambda h, i, s: (i, (first + h) * (group + 2) // group)),
        pl.BlockSpec((rows, HEAD_SIZE), lambda h, i, s: (0, (first + h) * (group + 2) + group)),
        pl.BlockSpec((rows, HEAD_SIZE), lambda h, i, s: (0, (first + h) * (group + 2) + group + 1)),
    ]


def attention_forward(info, qkv, query_heads, key_heads, docs):
    rows = qkv.shape[0]
    blocks = rows // BLOCK
    group = query_heads // key_heads
    wide = group * HEAD_SIZE
    return pl.pallas_call(
        functools.partial(forward_kernel, group, blocks, docs),
        grid_spec=pltpu.PrefetchScalarGridSpec(
            num_scalar_prefetch=1,
            grid=(key_heads, blocks),
            in_specs=head_specs(rows, group, 0),
            out_specs=[
                pl.BlockSpec((1, BLOCK, wide), lambda h, i, s: (h, i, 0)),
                pl.BlockSpec((1, 1, 8, group * BLOCK), lambda h, i, s: (h, i, 0, 0)),
            ],
            scratch_shapes=[
                pltpu.VMEM((rows + STEP, HEAD_SIZE), BF16),
                pltpu.VMEM((rows + STEP, 2 * HEAD_SIZE), BF16),
                pltpu.VMEM((group * BLOCK, 2 * HEAD_SIZE), F32),
            ],
        ),
        out_shape=[
            jax.ShapeDtypeStruct((key_heads, rows, wide), BF16),
            jax.ShapeDtypeStruct((key_heads, blocks, 8, group * BLOCK), F32),
        ],
        compiler_params=pltpu.CompilerParams(vmem_limit_bytes=VMEM_LIMIT),
        cost_estimate=pl.CostEstimate(flops=0, bytes_accessed=100_000_000, transcendentals=0),
        name="attention_forward",
    )(info, qkv, qkv, qkv)


def backward_kernel(
    group,
    blocks,
    docs,
    info_ref,
    q_ref,
    k_ref,
    v_ref,
    o_ref,
    do_ref,
    lse_ref,
    cos_ref,
    sin_ref,
    scale_ref,
    gq_ref,
    gk_ref,
    grad_ref,
    dgain_ref,
    dk_acc,
    dv_acc,
    dq_acc,
    keys_s,
    values_s,
):
    i = pl.program_id(1)
    rows_all = k_ref.shape[0]

    @pl.when(i == 0)
    def _():
        dk_acc[...] = jnp.zeros_like(dk_acc)
        dv_acc[...] = jnp.zeros_like(dv_acc)
        keep_padded(((k_ref, keys_s), (v_ref, values_s)))

    @pl.when(i == 0)
    def _():
        dgain_ref[...] = jnp.zeros_like(dgain_ref)

    def stacked(value):
        return jnp.concatenate([value[:, h * HEAD_SIZE : (h + 1) * HEAD_SIZE] for h in range(group)], axis=0)

    queries, grads = stacked(q_ref[...]), stacked(do_ref[...])
    delta = across(stacked(o_ref[0]).astype(F32) * grads.astype(F32), 2)[:1]
    lse = lse_ref[0, 0, :1]
    dq_acc[...] = jnp.zeros_like(dq_acc)
    places = i * BLOCK + lax.rem(lax.broadcasted_iota(jnp.int32, (1, group * BLOCK), 1), BLOCK)
    start = first_place(info_ref, blocks, docs, places)
    low = info_ref[i]

    def step(m, carry):
        base = (low + m * (STEP // BLOCK)) * BLOCK
        rows = pl.ds(pl.multiple_of(base, BLOCK), STEP)
        keys, values = keys_s[rows, :], values_s[rows, :]
        other = base + lax.broadcasted_iota(jnp.int32, (STEP, group * BLOCK), 0)
        keep = (other <= places) & (other >= start)
        probs = jnp.where(keep, jnp.exp2(dot_nt(keys, queries) * (SCALE * LOG2E) - lse), 0.0)
        score_grad = (probs * (dot_nt(values, grads) - delta)).astype(BF16)
        dv_acc[rows, :] += dot_nn(probs.astype(BF16), grads)
        dk_acc[rows, :] += dot_nn(score_grad, queries)
        dq_acc[...] += dot_tn(score_grad, keys)
        return carry

    lax.fori_loop(0, (i - low) // (STEP // BLOCK) + 1, step, 0)

    def raw_grad(grad, rotated, rows, kind, gain):
        cosine, sine = cos_ref[rows, :], sin_ref[rows, :]
        r = scale_ref[0, rows, kind : kind + 1]
        unit = unrotate(rotated.astype(F32), cosine, sine) * (1.0 / gain)
        back = unrotate(grad * SCALE, cosine, sine)
        scaled = back * gain
        raw = r * (scaled - unit * jnp.mean(scaled * unit, axis=1, keepdims=True))
        return raw.astype(BF16), jnp.sum(back * unit, axis=0, keepdims=True)

    here = pl.ds(pl.multiple_of(i * BLOCK, BLOCK), BLOCK)
    for h in range(group):
        span = slice(h * HEAD_SIZE, (h + 1) * HEAD_SIZE)
        raw, gain_grad = raw_grad(dq_acc[h * BLOCK : (h + 1) * BLOCK, :], q_ref[:, span], here, h, gq_ref[...])
        grad_ref[here, span] = raw
        dgain_ref[0:1, :] += gain_grad

    @pl.when(i == blocks - 1)
    def _():
        grad_ref[:, (group + 1) * HEAD_SIZE :] = dv_acc[:rows_all, :].astype(BF16)

        def finish(b, carry):
            rows = pl.ds(pl.multiple_of(b * BLOCK, BLOCK), BLOCK)
            raw, gain_grad = raw_grad(dk_acc[rows, :], k_ref[rows, :], rows, group, gk_ref[...])
            grad_ref[rows, group * HEAD_SIZE : (group + 1) * HEAD_SIZE] = raw
            dgain_ref[1:2, :] += gain_grad
            return carry

        lax.fori_loop(0, blocks, finish, 0)


def attention_backward(
    info, qkv, attended, grads, lse, cosine, sine, scales, gain_query, gain_key, query_heads, key_heads, docs, kv
):
    rows = qkv.shape[0]
    blocks = rows // BLOCK
    group = query_heads // key_heads
    wide = group * HEAD_SIZE
    own = pl.BlockSpec((1, BLOCK, wide), lambda h, i, s: (kv, i, 0))
    whole = lambda shape: pl.BlockSpec(shape, lambda h, i, s: (0, 0), pipeline_mode=pl.Buffered(1))
    return pl.pallas_call(
        functools.partial(backward_kernel, group, blocks, docs),
        grid_spec=pltpu.PrefetchScalarGridSpec(
            num_scalar_prefetch=1,
            grid=(1, blocks),
            in_specs=[
                *head_specs(rows, group, kv),
                own,
                pl.BlockSpec((BLOCK, wide), lambda h, i, s: (i, 0)),
                pl.BlockSpec((1, 1, 8, group * BLOCK), lambda h, i, s: (kv, i, 0, 0)),
                whole((rows, HEAD_SIZE)),
                whole((rows, HEAD_SIZE)),
                pl.BlockSpec((1, rows, HEAD_SIZE), lambda h, i, s: (kv, 0, 0), pipeline_mode=pl.Buffered(1)),
                whole((1, HEAD_SIZE)),
                whole((1, HEAD_SIZE)),
            ],
            out_specs=[
                whole((rows, wide + 2 * HEAD_SIZE)),
                pl.BlockSpec((8, HEAD_SIZE), lambda h, i, s: (0, 0)),
            ],
            scratch_shapes=[
                pltpu.VMEM((rows + STEP, HEAD_SIZE), F32),
                pltpu.VMEM((rows + STEP, HEAD_SIZE), F32),
                pltpu.VMEM((group * BLOCK, HEAD_SIZE), F32),
                pltpu.VMEM((rows + STEP, HEAD_SIZE), BF16),
                pltpu.VMEM((rows + STEP, HEAD_SIZE), BF16),
            ],
        ),
        out_shape=[
            jax.ShapeDtypeStruct((rows, wide + 2 * HEAD_SIZE), BF16),
            jax.ShapeDtypeStruct((8, HEAD_SIZE), F32),
        ],
        compiler_params=pltpu.CompilerParams(vmem_limit_bytes=VMEM_LIMIT),
        cost_estimate=pl.CostEstimate(flops=0, bytes_accessed=100_000_000, transcendentals=0),
        name="attention_backward",
    )(info, qkv, qkv, qkv, attended, grads, lse, cosine, sine, scales, gain_query, gain_key)


def wide_block(ref):
    value = ref[...]
    return value.reshape(value.shape[0] * value.shape[2], value.shape[3])


def group_places(span):
    half = span // 2
    dp, t = lax.axis_index("dp"), lax.axis_index("tensor")
    p, c = dp // 2, lax.rem(dp, 2)
    aside = jnp.where(c == t // half, 0, 1)

    def place(k):
        return (p * 2 + (c ^ (k // half)), t ^ (k % half))

    def chunk(k):
        return ((k // half) ^ aside) * half + k % half

    return place, chunk


def group_barrier(span, place):
    barrier = pltpu.get_barrier_semaphore()
    for k in range(1, span):
        pl.semaphore_signal(barrier, device_id=place(k), device_id_type=pl.DeviceIdType.MESH)
    pl.semaphore_wait(barrier, span - 1)


def remote_copy(src, dst, send_sem, recv_sem, to):
    return pltpu.make_async_remote_copy(
        src_ref=src,
        dst_ref=dst,
        send_sem=send_sem,
        recv_sem=recv_sem,
        device_id=to,
        device_id_type=pl.DeviceIdType.MESH,
    )


def arrival_order(span):
    half = span // 2
    return [0, half] + [k for k in range(1, span) if k != half]


def output_kernel(span, count, *refs):
    heads = refs[:count]
    w_hbm, tokens_ref, gain_ref, middle_ref, normed_ref, mixed_ref, w_ref, send_sems, recv_sems, local_sems = refs[count:]
    place, chunk = group_places(span)
    rows, width = tokens_ref.shape
    wide = heads[0].shape[1]
    load = pltpu.make_async_copy(w_hbm, w_ref, local_sems.at[count])
    load.start()
    group_barrier(span, place)
    copies = {}
    for h, ref in enumerate(heads):
        to = pl.ds(h * wide, wide)
        for k in range(1, span):
            at = h * span + k
            copies[h, k] = remote_copy(
                ref.at[pl.ds(k * rows, rows)], mixed_ref.at[k, :, to], send_sems.at[at], recv_sems.at[at], place(k)
            )
            copies[h, k].start()
        copies[h, 0] = pltpu.make_async_copy(ref.at[pl.ds(0, rows)], mixed_ref.at[0, :, to], local_sems.at[h])
        copies[h, 0].start()
    middle_ref[...] = tokens_ref[...].astype(F32)
    load.wait()
    piece = rows // 2
    for k in arrival_order(span):
        for h in range(count):
            if k:
                copies[h, k].wait_recv()
            else:
                copies[h, k].wait()
        weights = w_ref[:, chunk(k)].reshape(width, w_ref.shape[3])

        def step(m, carry, k=k, weights=weights):
            at = pl.ds(pl.multiple_of(m * piece, piece), piece)
            middle_ref[at, :] += dot_nt(mixed_ref[k, at, :], weights)
            return carry

        lax.fori_loop(0, rows // piece, step, 0)
    middle = middle_ref[...]
    normed_ref[...] = (middle * row_scale(middle) * gain_ref[...]).astype(BF16)
    for k in range(1, span):
        for h in range(count):
            copies[h, k].wait_send()


def output_project(heads, weights, tokens, gain):
    devices, span, shard, cols = weights.shape
    rows, width = tokens.shape
    count = len(heads)
    any_ref = pl.BlockSpec(memory_space=pl.ANY)
    local_ref = pl.BlockSpec(memory_space=pltpu.VMEM)
    return pl.pallas_call(
        functools.partial(output_kernel, span, count),
        in_specs=[any_ref] * (count + 1) + [local_ref] * 2,
        out_specs=[local_ref] * 3,
        out_shape=[
            jax.ShapeDtypeStruct((rows, width), F32),
            jax.ShapeDtypeStruct((rows, width), BF16),
            jax.ShapeDtypeStruct((span, rows, cols), BF16),
        ],
        scratch_shapes=[
            pltpu.VMEM(weights.shape, BF16),
            pltpu.SemaphoreType.DMA((span * count,)),
            pltpu.SemaphoreType.DMA((span * count,)),
            pltpu.SemaphoreType.DMA((count + 1,)),
        ],
        compiler_params=pltpu.CompilerParams(
            collective_id=1, has_side_effects=True, vmem_limit_bytes=VMEM_LIMIT
        ),
        cost_estimate=pl.CostEstimate(flops=0, bytes_accessed=100_000_000, transcendentals=0),
        name="output_project",
    )(*heads, weights, tokens, gain)


def output_back_kernel(span, count, b_ref, mixed_ref, w_hbm, *refs):
    outs = refs[:count]
    dw_hbm, w_ref, grad_ref, dw_ref, bt_ref, send_sems, recv_sems, local_sems = refs[count:]
    place, chunk = group_places(span)
    rows, width = b_ref.shape
    wide = outs[0].shape[1]
    cols = w_ref.shape[3]
    load = pltpu.make_async_copy(w_hbm, w_ref, local_sems.at[0])
    load.start()
    group_barrier(span, place)
    load.wait()
    piece = rows // 2
    copies = {}
    for k in reversed(arrival_order(span)):
        weights = w_ref[:, chunk(k)].reshape(width, cols)

        def step(m, carry, k=k, weights=weights):
            at = pl.ds(pl.multiple_of(m * piece, piece), piece)
            grad_ref[k, at, :] = dot_nn(b_ref[at, :], weights).astype(BF16)
            return carry

        lax.fori_loop(0, rows // piece, step, 0)
        for h, ref in enumerate(outs):
            src, dst = grad_ref.at[k, :, pl.ds(h * wide, wide)], ref.at[pl.ds(k * rows, rows)]
            at = h * span + k
            if k:
                copies[h, k] = remote_copy(src, dst, send_sems.at[at], recv_sems.at[at], place(k))
            else:
                copies[h, k] = pltpu.make_async_copy(src, dst, local_sems.at[1 + h])
            copies[h, k].start()
    bt_ref[...] = b_ref[...].T
    stores = []
    shard = w_ref.shape[2]
    for k in range(span):
        dw_ref[k] = dot_nn(bt_ref[...], mixed_ref[k]).astype(BF16).reshape(dw_ref.shape[1:])
        stores.append(pltpu.make_async_copy(dw_ref.at[k], dw_hbm.at[:, chunk(k)], local_sems.at[1 + count + k]))
        stores[-1].start()
    for copy in stores:
        copy.wait()
    for key, copy in copies.items():
        copy.wait()


def output_back(branch, mixed, weights, count):
    devices, span, shard, cols = weights.shape
    rows, width = branch.shape
    any_ref = pl.BlockSpec(memory_space=pl.ANY)
    local_ref = pl.BlockSpec(memory_space=pltpu.VMEM)
    return pl.pallas_call(
        functools.partial(output_back_kernel, span, count),
        in_specs=[local_ref, local_ref, any_ref],
        out_specs=[any_ref] * (count + 1),
        out_shape=[jax.ShapeDtypeStruct((span * rows, cols // count), BF16)] * count
        + [jax.ShapeDtypeStruct(weights.shape, BF16)],
        scratch_shapes=[
            pltpu.VMEM(weights.shape, BF16),
            pltpu.VMEM((span, rows, cols), BF16),
            pltpu.VMEM((span, devices, shard, cols), BF16),
            pltpu.VMEM((width, rows), BF16),
            pltpu.SemaphoreType.DMA((span * count,)),
            pltpu.SemaphoreType.DMA((span * count,)),
            pltpu.SemaphoreType.DMA((1 + count + span,)),
        ],
        compiler_params=pltpu.CompilerParams(
            collective_id=2, has_side_effects=True, vmem_limit_bytes=VMEM_LIMIT
        ),
        cost_estimate=pl.CostEstimate(flops=0, bytes_accessed=100_000_000, transcendentals=0),
        name="output_back",
    )(branch, mixed, weights)


def feed_kernel(last, x_ref, c_ref, w_ref, *refs):
    if last:
        (out_in, ng_in, middle_ref, gain_ref, result_ref, grad_ref, branch_ref, dgain_ref, dw_ref, out_s, ng_s) = refs[:11]
        act_s, gg_s, ug_s, xt_s, ct_s = refs[11:]
    else:
        out_s, ng_s, dw_ref, act_s, gg_s, ug_s, xt_s, ct_s = refs
    j = pl.program_id(0)
    rows_all, width = x_ref.shape
    hidden = act_s.shape[1]
    devices, _, shard, _ = w_ref.shape
    chunk = rows_all // 2

    @pl.when(j == 0)
    def _():
        xt_s[...] = x_ref[...].T
        ct_s[...] = c_ref[...].T
        out_s[...] = out_in[...] if last else jnp.zeros_like(out_s)
        ng_s[...] = ng_in[...] if last else jnp.zeros_like(ng_s)

    def part(k):
        return w_ref[:, 0, :, k * hidden : (k + 1) * hidden].reshape(width, hidden)

    def rows_step(m, carry):
        rows = pl.ds(pl.multiple_of(m * chunk, chunk), chunk)
        gate = dot_nn(x_ref[rows, :], part(0))
        upward = dot_nn(x_ref[rows, :], part(1))
        act_grad = dot_nn(c_ref[rows, :], part(2))
        sig = 1.0 / (1.0 + jnp.exp(-gate))
        silu = gate * sig
        act = (silu * upward).astype(BF16)
        up_grad = (act_grad * silu).astype(BF16)
        gate_grad = (act_grad * upward * sig * (1.0 + gate * (1.0 - sig))).astype(BF16)
        act_s[rows, :] = act
        ug_s[rows, :] = up_grad
        gg_s[rows, :] = gate_grad
        out_s[rows, :] += dot_nt(act, part(2))
        ng_s[rows, :] += dot_nt(gate_grad, part(0)) + dot_nt(up_grad, part(1))
        return carry

    lax.fori_loop(0, rows_all // chunk, rows_step, 0)

    group = ROWS // shard

    def grad_step(m, carry):
        rows = pl.ds(pl.multiple_of(m * ROWS, ROWS), ROWS)
        to = pl.ds(m * group, group)
        for k, left, right in ((0, xt_s, gg_s), (1, xt_s, ug_s), (2, ct_s, act_s)):
            value = dot_nn(left[rows, :], right[...]).astype(BF16)
            dw_ref[to, 0, :, k * hidden : (k + 1) * hidden] = value.reshape(group, shard, hidden)
        return carry

    lax.fori_loop(0, width // ROWS, grad_step, 0)

    if not last:
        return

    @pl.when(j == pl.num_programs(0) - 1)
    def _():
        middle = middle_ref[...]
        result_ref[...] = (middle + out_s[...]).astype(BF16)
        r = row_scale(middle)
        unit = middle * r
        dgain_ref[...] = jnp.broadcast_to(jnp.sum(ng_s[...] * unit, axis=0, keepdims=True), dgain_ref.shape)
        scaled = ng_s[...] * gain_ref[...]
        grad = c_ref[...].astype(F32) + r * (scaled - unit * jnp.mean(scaled * unit, axis=-1, keepdims=True))
        grad_ref[...] = grad
        branch_ref[...] = grad.astype(BF16)


def feed(x, cot, weights, *rest):
    rows, width = x.shape
    devices, span, shard, cols = weights.shape
    hidden = cols // 3
    last = len(rest) > 0
    whole = lambda shape: pl.BlockSpec(shape, lambda j: (0, 0), pipeline_mode=pl.Buffered(1))
    chunk = pl.BlockSpec((devices, 1, shard, cols), lambda j: (0, j, 0, 0))
    full = whole((rows, width))
    grads = jax.ShapeDtypeStruct((devices, span, shard, cols), BF16)
    shape = lambda kind: jax.ShapeDtypeStruct((rows, width), kind)
    sums = [pltpu.VMEM((rows, width), F32)] * 2 if last else []
    return pl.pallas_call(
        functools.partial(feed_kernel, last),
        grid=(span,),
        in_specs=[full, full, chunk] + ([full, full, full, whole((1, width))] if last else []),
        out_specs=[full, full, full, whole((8, width)), chunk] if last else [full, full, chunk],
        out_shape=[shape(BF16), shape(F32), shape(BF16), jax.ShapeDtypeStruct((8, width), F32), grads]
        if last
        else [shape(F32), shape(F32), grads],
        scratch_shapes=sums + [pltpu.VMEM((rows, hidden), BF16)] * 3 + [pltpu.VMEM((width, rows), BF16)] * 2,
        compiler_params=pltpu.CompilerParams(vmem_limit_bytes=VMEM_LIMIT),
        name="feed_forward",
    )(x, cot, weights, *rest)


def last_kernel(
    pairs,
    span,
    count,
    *refs,
):
    grads_hbm, sorted_hbm = refs[:count], refs[count : 2 * count]
    last_body(pairs, span, grads_hbm, sorted_hbm, *refs[2 * count :])


def last_body(
    pairs,
    span,
    grads_hbm,
    sorted_hbm,
    normed_hbm,
    w_ref,
    middle_ref,
    tokens_ref,
    gain_ref,
    gains_ref,
    output_ref,
    rows_out,
    heads_out,
    gains_out,
    output_out,
    grads,
    sorted_s,
    normed_s,
    turned,
    mine,
    theirs,
    from_sibling,
    from_line,
    heads_s,
    heads_in,
    far_in,
    far_s,
    near_in,
    near_s,
    final_s,
    pass_s,
    far_pass,
    gains_one,
    gains_two,
    gains_s,
    send_sems,
    recv_sems,
    local_sems,
):
    half = span // 2
    dp, t = lax.axis_index("dp"), lax.axis_index("tensor")
    p, c = dp // 2, lax.rem(dp, 2)
    settled = c == t // half
    rows, width = middle_ref.shape
    shard = output_ref.shape[1]
    place = lambda pp, cc, tt: (pp * 2 + cc, tt)
    sibling = place(p, 1 - c, t)
    used = [0]

    def copy_to(src, dst, to):
        used[0] += 1
        at = used[0] - 1
        return remote_copy(src, dst, send_sems.at[at], recv_sems.at[at], to)

    count = len(grads_hbm)
    wide = grads_hbm[0].shape[1]

    def side_by_side(sources, rows_of, dst, sem):
        return [
            pltpu.make_async_copy(src.at[rows_of], dst.at[:, pl.ds(h * wide, wide)], local_sems.at[sem + h])
            for h, src in enumerate(sources)
        ]

    loads = [side_by_side(grads_hbm, pl.ds(k * rows, rows), grads.at[k], k * count) for k in range(span)]
    order = list(range(half, span)) + list(range(1, half)) + [0]
    for k in order:
        for load in loads[k]:
            load.start()
    more = [pltpu.make_async_copy(normed_hbm, normed_s, local_sems.at[span * count])]
    more += side_by_side(sorted_hbm, pl.ds(0, span * rows), sorted_s, span * count + 1)
    for load in more:
        load.start()

    barrier = pltpu.get_barrier_semaphore()
    greeted = 0
    for k in range(1, 2 * span):
        pl.semaphore_signal(
            barrier, device_id=place(p, c ^ (k // span), t ^ (k % span)), device_id_type=pl.DeviceIdType.MESH
        )
        greeted += 1
    for k in range(1, pairs):
        pl.semaphore_signal(barrier, device_id=place(p ^ k, c, t), device_id_type=pl.DeviceIdType.MESH)
        greeted += 1
    pl.semaphore_wait(barrier, greeted)

    outputs = [copy_to(output_ref.at[r], output_out.at[r - 1], place(p, c, t ^ r)) for r in range(1, span)]

    piece = rows // 2

    def multiply(k, dst, slot):
        def step(m, carry):
            at = pl.ds(pl.multiple_of(m * piece, piece), piece)
            dst[slot, at, :] = dot_nt(grads[k, at, :], w_ref[...]).astype(BF16)
            return carry

        lax.fori_loop(0, 2, step, 0)

    sides = []
    for k in range(half, span):
        for load in loads[k]:
            load.wait()
        multiply(k, theirs, k - half)
        sides.append(copy_to(theirs.at[k - half], from_sibling.at[k - half], sibling))
        sides[-1].start()
    for load in more:
        load.wait()
    turned[...] = normed_s[...].T
    block = 2 * shard

    def weights_step(m, carry):
        at = pl.ds(pl.multiple_of(m * block, block), block)
        heads_s[at, :] = dot_nn(turned[at, :], sorted_s[...]).astype(BF16)
        return carry

    lax.fori_loop(0, pairs, weights_step, 0)
    heads_copies = []
    for k in range(1, pairs):
        there = pl.ds((p ^ k) * block, block)
        heads_copies.append(copy_to(heads_s.at[there], heads_in.at[k - 1], place(p ^ k, c, t)))
        heads_copies[-1].start()

    hops = {}
    for k in list(range(1, half)) + [0]:
        for load in loads[k]:
            load.wait()
        multiply(k, mine, k)
        sides[k].wait_recv()
        mine[k] = (mine[k].astype(F32) + from_sibling[k].astype(F32)).astype(BF16)
        if k:
            for m in range(2):
                at = pl.ds(m * piece, piece)
                hops[k, m] = copy_to(mine.at[k, at], from_line.at[k - 1, at], place(p, c, t ^ k))
                hops[k, m].start()
    for copy in outputs:
        copy.start()

    for copy in heads_copies:
        copy.wait_recv()
    summed = heads_s[pl.ds(p * block, block), :].astype(F32)
    for k in range(1, pairs):
        summed = summed + heads_in[k - 1].astype(F32)
    far_s[...] = summed.astype(BF16)
    side = copy_to(far_s, far_pass, sibling)
    far = copy_to(far_pass, far_in, place(p, 1 - c, lax.rem(t + half, span)))
    near = copy_to(near_s, near_in, sibling)

    @pl.when(jnp.logical_not(settled))
    def _():
        side.start()

    swaps = []
    gain_sum = jnp.zeros((1, width), F32)
    for m in range(2):
        at = pl.ds(m * piece, piece)
        for k in range(1, half):
            hops[k, m].wait_recv()
        grad = mine[0, at, :].astype(F32)
        for k in range(1, half):
            grad = grad + from_line[k - 1, at, :].astype(F32)
        inputs = tokens_ref[at, :].astype(F32)
        r = row_scale(inputs)
        unit = inputs * r
        gain_sum = gain_sum + jnp.sum(grad * unit, axis=0, keepdims=True)
        scaled = grad * gain_ref[...]
        final_s[at, :] = (
            middle_ref[at, :] + r * (scaled - unit * jnp.mean(scaled * unit, axis=-1, keepdims=True))
        ).astype(BF16)
        there = place(p, 1 - c, span - 1 - t)
        swap = copy_to(final_s.at[at], rows_out.at[at] if m == 0 else pass_s, there if m == 0 else sibling)
        keep = pltpu.make_async_copy(final_s.at[at], rows_out.at[at], local_sems.at[(span + 1) * count + 1 + m])
        swaps.append((swap, keep))

        @pl.when(settled)
        def _():
            keep.start()
            if m == 0:
                side.wait_recv()
                far.start()

        @pl.when(jnp.logical_not(settled))
        def _():
            swap.start()

    gains_s[...] = gains_ref[...]
    gains_s[0:1, :] = gain_sum
    first_gains = [
        copy_to(gains_s, gains_one.at[k - 1], place(p, c ^ (k // span), t ^ (k % span))) for k in range(1, 2 * span)
    ]
    for copy in first_gains:
        copy.start()

    at = pl.ds(piece, piece)
    handed = swaps[1][0]
    passed = copy_to(pass_s, rows_out.at[at], place(p, c, span - 1 - t))

    @pl.when(settled)
    def _():
        handed.wait_recv()
        passed.start()

    for copy in first_gains:
        copy.wait_recv()
    total = gains_s[...]
    for k in range(1, 2 * span):
        total = total + gains_one[k - 1]
    gains_out[...] = total
    second_gains = [copy_to(gains_out, gains_two.at[k - 1], place(p ^ k, c, t)) for k in range(1, pairs)]
    for copy in second_gains:
        copy.start()

    for copy in second_gains:
        copy.wait()
    for copy in first_gains:
        copy.wait_send()
    whole = gains_out[...]
    for k in range(1, pairs):
        whole = whole + gains_two[k - 1]
    gains_out[...] = whole

    @pl.when(settled)
    def _():
        far.wait_recv()
        own = pl.ds(c * shard, shard)
        other = pl.ds((1 - c) * shard, shard)
        near_s[...] = (far_s[other, :].astype(F32) + far_in[other, :].astype(F32)).astype(BF16)
        near.start()
        far.wait_send()
        heads_out[...] = far_s[own, :].astype(F32) + far_in[own, :].astype(F32)
        near.wait_send()

    @pl.when(jnp.logical_not(settled))
    def _():
        side.wait_send()
        near.wait_recv()
        heads_out[...] = near_in[...].astype(F32)

    for copy in sides + list(hops.values()) + heads_copies:
        copy.wait_send()
    for copy in outputs:
        copy.wait()
    @pl.when(settled)
    def _():
        for swap, keep in swaps:
            keep.wait()
        passed.wait_send()

    @pl.when(jnp.logical_not(settled))
    def _():
        for swap, keep in swaps:
            swap.wait_send()
        swaps[0][0].wait_recv()
        passed.wait_recv()


def last_transfers(pairs, span, grads, grads_sorted, normed, weights, middle_grad, tokens, gain, gains, output):
    rows, width = tokens.shape
    half = span // 2
    shard = output.shape[1]
    cols = weights.shape[1]
    count = len(grads)
    any_ref = pl.BlockSpec(memory_space=pl.ANY)
    local_ref = pl.BlockSpec(memory_space=pltpu.VMEM)
    copies = span - 1 + half + 2 * (half - 1) + 2 * (pairs - 1) + 2 + 2 * span - 1 + 4
    return pl.pallas_call(
        functools.partial(last_kernel, pairs, span, count),
        in_specs=[any_ref] * (2 * count + 1) + [local_ref] * 5 + [any_ref],
        out_specs=[any_ref, local_ref, local_ref, any_ref],
        out_shape=[
            jax.ShapeDtypeStruct((rows, width), BF16),
            jax.ShapeDtypeStruct((shard, cols), F32),
            jax.ShapeDtypeStruct((8, width), F32),
            jax.ShapeDtypeStruct((span - 1, *output.shape[1:]), BF16),
        ],
        scratch_shapes=[
            pltpu.VMEM((span, rows, cols), BF16),
            pltpu.VMEM((span * rows, cols), BF16),
            pltpu.VMEM((span * rows, width), BF16),
            pltpu.VMEM((width, span * rows), BF16),
            pltpu.VMEM((half, rows, width), BF16),
            pltpu.VMEM((half, rows, width), BF16),
            pltpu.VMEM((half, rows, width), BF16),
            pltpu.VMEM((max(half - 1, 1), rows, width), BF16),
            pltpu.VMEM((width, cols), BF16),
            pltpu.VMEM((pairs - 1, 2 * shard, cols), BF16),
            pltpu.VMEM((2 * shard, cols), BF16),
            pltpu.VMEM((2 * shard, cols), BF16),
            pltpu.VMEM((shard, cols), BF16),
            pltpu.VMEM((shard, cols), BF16),
            pltpu.VMEM((rows, width), BF16),
            pltpu.VMEM((rows // 2, width), BF16),
            pltpu.VMEM((2 * shard, cols), BF16),
            pltpu.VMEM((2 * span - 1, 8, width), F32),
            pltpu.VMEM((pairs - 1, 8, width), F32),
            pltpu.VMEM((8, width), F32),
            pltpu.SemaphoreType.DMA((copies,)),
            pltpu.SemaphoreType.DMA((copies,)),
            pltpu.SemaphoreType.DMA(((span + 1) * count + 3,)),
        ],
        compiler_params=pltpu.CompilerParams(
            collective_id=3, has_side_effects=True, vmem_limit_bytes=VMEM_LIMIT
        ),
        name="last_transfers",
    )(*grads, *grads_sorted, normed, weights, middle_grad, tokens, gain, gains, output)


def local(
    tokens,
    lengths,
    row_order,
    attention_gain,
    query_gain,
    key_gain,
    query_weight,
    key_matrix,
    value_matrix,
    output_weight,
    feedforward_gain,
    gate_weight,
    up_weight,
    down_weight,
    cotangent,
):
    span = lax.axis_size("tensor")
    pairs = lax.axis_size("dp") // 2
    half = span // 2
    rows, width = tokens.shape
    group_rows = rows * span
    blocks = group_rows // BLOCK
    docs = lengths.shape[1]
    query_heads = query_weight.shape[1] // HEAD_SIZE
    key_heads = key_matrix.shape[1] // HEAD_SIZE
    head_columns = query_weight.shape[1]
    hidden_columns = gate_weight.shape[1]
    shard = query_weight.shape[0]

    dp, t = lax.axis_index("dp"), lax.axis_index("tensor")
    p, c = dp // 2, lax.rem(dp, 2)
    q = t // half
    settled = c == q

    def send(x, route):
        moves = []
        for pp in range(pairs):
            for cc in range(2):
                for tt in range(span):
                    to = route(pp, cc, tt)
                    if to is not None:
                        moves.append(((pp * 2 + cc) * span + tt, (to[0] * 2 + to[1]) * span + to[2]))
        return lax.ppermute(x, AXES, moves)

    def swap(x):
        moved = send(x, lambda pp, cc, tt: (pp, 1 - cc, span - 1 - tt) if cc != tt // half else None)
        return jnp.where(settled, x, moved)

    never = row_order[0, 0] < 0

    def behind(x, other):
        return jnp.where(never, other[0, 0].astype(x.dtype), x)

    def later(x, other):
        at = (0,) * x.ndim
        block = lax.slice(x, at, x.shape[:-2] and (1,) * (x.ndim - 2) + (8, 128) or (8, 128))
        return lax.dynamic_update_slice(x, jnp.where(never, other[0, 0].astype(x.dtype), block), at)

    def line(x, steps):
        return [send(x, lambda pp, cc, tt: (pp, cc, tt ^ r)) for r in steps]

    def gather_wide(pieces):
        cols = pieces[0].shape[1]
        out = by_rows(lax.all_gather(by_rows(jnp.concatenate(pieces, axis=0)), "dp", axis=0, tiled=True))
        return out.reshape(2 * pairs, len(pieces), shard, cols)

    def scatter_wide(grads):
        devices, count, _, cols = grads.shape
        out = by_rows(grads.reshape(devices * count * shard, cols))
        out = by_rows(lax.psum_scatter(out, "dp", scatter_dimension=0, tiled=True))
        return [out[r * shard : (r + 1) * shard] for r in range(count)]

    per_query, per_key = head_columns // key_heads, HEAD_SIZE
    heads_local = []
    for kv in range(key_heads):
        heads_local.append(query_weight[:, kv * per_query : (kv + 1) * per_query])
        heads_local.append(key_matrix[:, kv * per_key : (kv + 1) * per_key])
        heads_local.append(value_matrix[:, kv * per_key : (kv + 1) * per_key])
    heads_local = by_rows(jnp.concatenate(heads_local, axis=1))
    feed_local = by_rows(jnp.concatenate([gate_weight, up_weight, down_weight.T], axis=1))
    gains = jnp.concatenate([attention_gain, query_gain, key_gain, feedforward_gain])
    small, tiny = attention_gain.shape[0], query_gain.shape[0]
    few, lanes = gains.shape[0], -(-gains.shape[0] // 128) * 128
    gains = jnp.broadcast_to(jnp.pad(gains, (0, lanes - few))[None], (16, lanes))
    facts = jnp.concatenate([row_order[0], lengths[0]])
    fact_rows = -(-facts.shape[0] // 1024) * 8
    facts = jnp.pad(facts, (0, fact_rows * 128 - facts.shape[0])).reshape(fact_rows, 128)
    tokens_all, heads_weights, output_line, gains, facts_moved = first_transfers(
        pairs, span, tokens, heads_local, by_rows(output_weight.T), gains, facts
    )
    swapped = tokens_all[0]
    tokens_all = tokens_all.reshape(group_rows, width)
    own_weights = gather_wide([feed_local])
    output_weights = gather_wide([output_line[r] for r in range(span)])
    feed_line = line(behind(feed_local, swapped), range(1, span))

    gains = gains.reshape(2 * pairs, 16, lanes)[:, 0, :few].astype(F32)
    gain_one = gains[:, :small].reshape(1, width)
    gain_query = gains[:, small : small + tiny].reshape(1, HEAD_SIZE)
    gain_key = gains[:, small + tiny : small + 2 * tiny].reshape(1, HEAD_SIZE)
    gain_two = gains[:, small + 2 * tiny : small + 2 * tiny + small].reshape(1, width)
    facts = jnp.where(settled, facts, facts_moved).reshape(-1)[: group_rows + docs]
    order, length = facts[:group_rows].reshape(span, rows), facts[group_rows:]
    places = []
    for k in range(span):
        tt, cc = t ^ (k % half), c ^ (k // half)
        places.append(lax.dynamic_index_in_dim(order, jnp.where(cc == tt // half, tt, span - 1 - tt), 0, False))
    places = jnp.concatenate(places)
    inverse = jnp.argsort(places)
    before = jnp.arange(docs)[None, :] < jnp.arange(docs)[:, None]
    starts = jnp.sum(jnp.where(before, length[None, :], 0), axis=1).astype(jnp.int32)

    def start_of(place):
        return jnp.max(jnp.where(place[:, None] >= starts[None, :], starts[None, :], 0), axis=1)

    index = jnp.arange(blocks, dtype=jnp.int32) * BLOCK
    low = start_of(index) // BLOCK
    clear = (start_of(index + BLOCK - 1) + BLOCK - 1) // BLOCK
    info = jnp.concatenate([low, clear, starts]).astype(jnp.int32)
    index = jnp.arange(group_rows, dtype=jnp.int32)
    position = (index - start_of(index)).astype(F32)
    inverse_rate = THETA ** (-(jnp.arange(HEAD_SIZE // 2, dtype=F32) * 2.0 / HEAD_SIZE))
    angle = position[:, None] * inverse_rate[None, :]
    cosine, sine = jnp.cos(angle), jnp.sin(angle)
    cosine = jnp.concatenate([cosine, cosine], axis=1)
    sine = jnp.concatenate([-sine, sine], axis=1)

    tokens_sorted = jnp.take(tokens_all, inverse, axis=0, mode="clip")
    cot_own = swap(cotangent)
    normed, qkv, scales = project(
        tokens_sorted, gain_one, heads_weights, gain_query, gain_key, cosine, sine, query_heads, key_heads
    )

    line_weights = gather_wide([behind(piece, qkv) for piece in feed_line])

    attended, lse = attention_forward(info, qkv, query_heads, key_heads, docs)
    unsorted = [jnp.take(attended[kv], places, axis=0, mode="clip") for kv in range(key_heads)]

    hidden = gate_weight.shape[1]
    middle, normed_two, mixed = output_project(unsorted, output_weights, swapped, gain_two)
    out, normed_grad, line_grad = feed(normed_two, cot_own, line_weights)
    result, middle_grad, branch, gain_two_grad, own_grad = feed(
        normed_two, cot_own, own_weights, out, normed_grad, middle, gain_two
    )
    line_sum = scatter_wide(line_grad)

    *head_rows, output_grad = output_back(branch, mixed, output_weights, key_heads)
    layer_output = swap(result)

    head_grads, head_gains = [], 0.0
    for kv in range(key_heads):
        attended_grad = jnp.take(head_rows[kv], inverse, axis=0, mode="clip")
        if kv > 0:
            attended_grad = behind(attended_grad, grads)
        grads, gains_of = attention_backward(
            info,
            qkv,
            attended,
            attended_grad,
            lse,
            cosine,
            sine,
            scales,
            gain_query,
            gain_key,
            query_heads,
            key_heads,
            docs,
            kv,
        )
        if kv == 0:
            output_sum = scatter_wide(later(later(output_grad, line_sum[0]), grads))
            own_sum = scatter_wide(later(own_grad, grads))
            line_in = [
                send(piece, lambda pp, cc, tt: (pp, cc, tt ^ r)) for r, piece in enumerate(line_sum, start=1)
            ]
        head_grads.append(grads)
        head_gains = head_gains + gains_of
    qkv_rows = [jnp.take(grads, places, axis=0, mode="clip") for grads in head_grads]
    gain_rows = jnp.concatenate(
        [
            jnp.zeros((1, width), F32),
            gain_two_grad[:1],
            jnp.pad(head_gains[:2].reshape(1, 2 * HEAD_SIZE), ((0, 0), (0, width - 2 * HEAD_SIZE))),
            jnp.zeros((5, width), F32),
        ]
    )
    input_grad, heads_sum, gain_sums, output_in = last_transfers(
        pairs,
        span,
        qkv_rows,
        head_grads,
        normed,
        heads_weights,
        middle_grad,
        swapped,
        gain_one,
        gain_rows,
        jnp.stack(output_sum),
    )

    def total(first, others):
        out = first.astype(F32)
        for other in others:
            out = out + other.astype(F32)
        return out

    wide_sum = total(own_sum[0], line_in)
    output_sum = total(output_sum[0], [output_in[k] for k in range(span - 1)])
    stride = per_query + 2 * per_key
    columns = lambda at, size: jnp.concatenate(
        [heads_sum[:, kv * stride + at : kv * stride + at + size] for kv in range(key_heads)], axis=1
    )
    cut = lambda row, at, size: lax.dynamic_slice(gain_sums[row], (at + dp * size,), (size,))
    return (
        layer_output,
        input_grad,
        cut(0, 0, small),
        cut(2, 0, tiny),
        cut(2, HEAD_SIZE, tiny),
        columns(0, per_query),
        columns(per_query, per_key),
        columns(per_query + per_key, per_key),
        output_sum.T,
        cut(1, 0, small),
        wide_sum[:, :hidden],
        wide_sum[:, hidden : 2 * hidden],
        wide_sum[:, 2 * hidden :].T,
    )


def solution(mesh):
    placed = (
        P(AXES, None),
        P("dp", None),
        P("dp", None),
        P("dp"),
        P("dp"),
        P("dp"),
        P("dp", "tensor"),
        P("dp", "tensor"),
        P("dp", "tensor"),
        P("tensor", "dp"),
        P("dp"),
        P("dp", "tensor"),
        P("dp", "tensor"),
        P("tensor", "dp"),
        P(AXES, None),
    )
    return jax.shard_map(
        local,
        mesh=mesh,
        in_specs=placed,
        out_specs=(
            P(AXES, None),
            P(AXES, None),
            P("dp"),
            P("dp"),
            P("dp"),
            P("dp", "tensor"),
            P("dp", "tensor"),
            P("dp", "tensor"),
            P("tensor", "dp"),
            P("dp"),
            P("dp", "tensor"),
            P("dp", "tensor"),
            P("tensor", "dp"),
        ),
        check_vma=False,
    )
```

```python
import functools

import jax
import jax.numpy as jnp
import numpy as np
from jax import lax
from jax.experimental.layout import Layout, with_layout_constraint
from jax.experimental import pallas as pl
from jax.experimental.pallas import tpu as pltpu
from jax.sharding import PartitionSpec as P

HEAD_SIZE = 128
EPSILON = 1e-06
THETA = 1000000.0
AXES = ("dp", "tensor")
ROWS = 256
PROJECTED = 512
BLOCK = 512
STEP = 512
SCALE = HEAD_SIZE ** (-0.5)
LOG2E = 1.4426950408889634
VMEM_LIMIT = 56 * 1024 * 1024
F32 = jnp.float32
BF16 = jnp.bfloat16


def dot_nn(left, right):
    return lax.dot_general(left, right, (((1,), (0,)), ((), ())), preferred_element_type=F32)


def dot_nt(left, right):
    return lax.dot_general(left, right, (((1,), (1,)), ((), ())), preferred_element_type=F32)


def dot_tn(left, right):
    return lax.dot_general(left, right, (((0,), (0,)), ((), ())), preferred_element_type=F32)


def by_rows(x):
    return with_layout_constraint(x, Layout(major_to_minor=tuple(range(x.ndim))))


def row_scale(rows):
    return lax.rsqrt(jnp.mean(rows * rows, axis=-1, keepdims=True) + EPSILON)


def rotate(rows, cosine, sine):
    return rows * cosine + pltpu.roll(rows, HEAD_SIZE // 2, 1) * sine


def unrotate(rows, cosine, sine):
    return rows * cosine - pltpu.roll(rows, HEAD_SIZE // 2, 1) * sine


CHUNKS = 4


def first_kernel(
    pairs,
    span,
    tokens_ref,
    heads_ref,
    output_ref,
    gains_ref,
    facts_ref,
    tokens_out,
    heads_out,
    output_out,
    gains_out,
    facts_out,
    send_sems,
    recv_sems,
    local_sems,
):
    half = span // 2
    dp, t = lax.axis_index("dp"), lax.axis_index("tensor")
    p, c = dp // 2, lax.rem(dp, 2)
    q = t // half
    settled = c == q
    rows = tokens_ref.shape[0]
    piece = rows // CHUNKS
    shard = heads_ref.shape[0]
    small = gains_ref.shape[0]
    place = lambda pp, cc, tt: (pp * 2 + cc, tt)

    barrier = pltpu.get_barrier_semaphore()
    greeted = 0
    for k in range(1, 2 * span):
        pl.semaphore_signal(
            barrier,
            device_id=place(p, c ^ (k // span), t ^ (k % span)),
            device_id_type=pl.DeviceIdType.MESH,
        )
        greeted += 1
    for k in range(1, pairs):
        for cc in range(2):
            pl.semaphore_signal(
                barrier, device_id=place(p ^ k, c ^ cc, t), device_id_type=pl.DeviceIdType.MESH
            )
            greeted += 1
    pl.semaphore_wait(barrier, greeted)

    used = [0]

    def number(count=1):
        used[0] += count
        return used[0] - count

    def remote(src, dst, sem, to, arrival=None):
        return pltpu.make_async_remote_copy(
            src_ref=src,
            dst_ref=dst,
            send_sem=send_sems.at[sem],
            recv_sem=recv_sems.at[sem if arrival is None else arrival],
            device_id=to,
            device_id_type=pl.DeviceIdType.MESH,
        )

    def rows_of(i):
        return pl.ds(i * piece, piece)

    swap_sem = number(CHUNKS)
    line_sems = [[number() for _ in range(CHUNKS)] for _ in range(half)]
    side_sems = [[number() for _ in range(CHUNKS)] for _ in range(half)]
    near_sem, far_sem = number(), number(2)
    pair_sems = [number() for _ in range(pairs)]
    output_sems = [number() for _ in range(span)]
    gain_sems = [number() for _ in range(2 * pairs)]
    fact_sem = number()

    sibling = place(p, 1 - c, t)
    partner = place(p, 1 - c, span - 1 - t)
    swaps = [
        remote(tokens_ref.at[rows_of(i)], tokens_out.at[0, rows_of(i)], swap_sem + i, partner) for i in range(CHUNKS)
    ]
    own_rows = pl.ds(dp * shard, shard)
    far = lax.rem(t + half, span)
    near_copy = remote(heads_ref, heads_out.at[own_rows], near_sem, sibling)
    far_copy = remote(heads_ref, heads_out.at[own_rows], far_sem + c, place(p, q, far))
    local_tokens = pltpu.make_async_copy(tokens_ref, tokens_out.at[0], local_sems.at[0])
    local_heads = pltpu.make_async_copy(heads_ref, heads_out.at[own_rows], local_sems.at[1])
    local_output = pltpu.make_async_copy(output_ref, output_out.at[0], local_sems.at[2])
    local_gains = pltpu.make_async_copy(gains_ref, gains_out.at[pl.ds(dp * small, small)], local_sems.at[3])

    fact_copy = remote(facts_ref, facts_out, fact_sem, sibling)
    fact_copy.start()
    far_copy.start()

    @pl.when(settled)
    def _():
        local_heads.start()
        local_tokens.start()

    @pl.when(jnp.logical_not(settled))
    def _():
        near_copy.start()
        for copy in swaps:
            copy.start()

    gain_copies = []
    for k in range(1, 2 * pairs):
        to = (p ^ (k // 2), c ^ (k % 2))
        gain_copies.append(
            remote(gains_ref, gains_out.at[pl.ds(dp * small, small)], gain_sems[k], place(to[0], to[1], t))
        )
    local_gains.start()
    local_output.start()
    for copy in gain_copies:
        copy.start()

    def spread(i, source):
        copies = [remote(source, tokens_out.at[half, rows_of(i)], side_sems[0][i], sibling)]
        for k in range(1, half):
            copies.append(remote(source, tokens_out.at[k, rows_of(i)], line_sems[k][i], place(p, c, t ^ k)))
        return copies

    @pl.when(settled)
    def _():
        for i in range(CHUNKS):
            for copy in spread(i, tokens_ref.at[rows_of(i)]):
                copy.start()

    output_copies = [
        remote(output_ref, output_out.at[r], output_sems[r], place(p, c, t ^ r)) for r in range(1, span)
    ]

    @pl.when(settled)
    def _():
        local_heads.wait()
        near_copy.wait_recv()

    @pl.when(jnp.logical_not(settled))
    def _():
        near_copy.wait_send()
        for cc in range(2):
            remote(heads_ref, heads_out.at[own_rows], far_sem, sibling, far_sem + cc).wait_recv()

    both = heads_out.at[pl.ds(p * 2 * shard, 2 * shard)]
    pair_copies = [remote(both, both, pair_sems[k], place(p ^ k, c, t)) for k in range(1, pairs)]
    for copy in pair_copies:
        copy.start()

    @pl.when(jnp.logical_not(settled))
    def _():
        for i in range(CHUNKS):
            swaps[i].wait_recv()
            for copy in spread(i, tokens_out.at[0, rows_of(i)]):
                copy.start()

    for copy in output_copies:
        copy.start()

    forwards = []
    for i in range(CHUNKS):
        for k in range(1, half):
            block = tokens_out.at[k, rows_of(i)]
            remote(block, block, line_sems[k][i], sibling).wait_recv()
            copy = remote(block, tokens_out.at[half + k, rows_of(i)], side_sems[k][i], sibling)
            copy.start()
            forwards.append(copy)

    far_copy.wait_send()
    fact_copy.wait()
    local_output.wait()
    local_gains.wait()

    @pl.when(settled)
    def _():
        local_tokens.wait()

    @pl.when(jnp.logical_not(settled))
    def _():
        for copy in swaps:
            copy.wait_send()

    for i in range(CHUNKS):
        for index, copy in enumerate(spread(i, tokens_out.at[0, rows_of(i)])):
            copy.wait_send()
            if index == 0:
                copy.wait_recv()
    for copy in forwards + pair_copies + output_copies + gain_copies:
        copy.wait()


def first_transfers(pairs, span, tokens, heads, output, gains, facts):
    rows, width = tokens.shape
    shard = heads.shape[0]
    half = span // 2
    copies = CHUNKS * (1 + 2 * half) + 3 + pairs + span + 2 * pairs + 1
    any_ref = pl.BlockSpec(memory_space=pl.ANY)
    return pl.pallas_call(
        functools.partial(first_kernel, pairs, span),
        in_specs=[any_ref] * 5,
        out_specs=[any_ref] * 5,
        out_shape=[
            jax.ShapeDtypeStruct((span, rows, width), tokens.dtype),
            jax.ShapeDtypeStruct((2 * pairs * shard, heads.shape[1]), heads.dtype),
            jax.ShapeDtypeStruct((span, *output.shape), output.dtype),
            jax.ShapeDtypeStruct((2 * pairs * gains.shape[0], gains.shape[1]), gains.dtype),
            jax.ShapeDtypeStruct(facts.shape, facts.dtype),
        ],
        scratch_shapes=[
            pltpu.SemaphoreType.DMA((copies,)),
            pltpu.SemaphoreType.DMA((copies,)),
            pltpu.SemaphoreType.DMA((4,)),
        ],
        compiler_params=pltpu.CompilerParams(collective_id=0, has_side_effects=True),
        cost_estimate=pl.CostEstimate(flops=0, bytes_accessed=150_000_000, transcendentals=0),
        name="first_transfers",
    )(tokens, heads, output, gains, facts)


def sorting(places, first, count):
    index = first + lax.broadcasted_iota(jnp.int32, (count, places.shape[1]), 0)
    return jnp.where(places == index, 1.0, 0.0).astype(BF16)


def project_kernel(
    query_heads, key_heads, x_ref, places_ref, gain_ref, w_ref, gq_ref, gk_ref, cos_ref, sin_ref, normed_ref, qkv_ref, scale_ref
):
    x = dot_nn(sorting(places_ref[...], pl.program_id(0) * PROJECTED, PROJECTED), x_ref[...])
    normed = (x * row_scale(x) * gain_ref[...]).astype(BF16)
    normed_ref[...] = normed
    raw = dot_nn(normed, w_ref[...])
    cosine, sine = cos_ref[...], sin_ref[...]
    lane = lax.broadcasted_iota(jnp.int32, (x.shape[0], HEAD_SIZE), 1)
    scales = jnp.zeros((x.shape[0], HEAD_SIZE), F32)
    group = query_heads // key_heads
    for at in range(query_heads + 2 * key_heads):
        kv, kind = at // (group + 2), at % (group + 2)
        span = slice(at * HEAD_SIZE, (at + 1) * HEAD_SIZE)
        u = raw[:, span]
        if kind == group + 1:
            qkv_ref[:, span] = u.astype(BF16)
            continue
        r = row_scale(u)
        gain = gq_ref[...] if kind < group else gk_ref[...]
        qkv_ref[:, span] = rotate(u * r * gain, cosine, sine).astype(BF16)
        scales = jnp.where(lane == kind, r, scales) if kind else jnp.broadcast_to(r, scales.shape)
        if kind == group:
            scale_ref[kv] = scales


def project(x, places, gain, weights, gain_query, gain_key, cosine, sine, query_heads, key_heads):
    rows, width = x.shape
    wide = weights.shape[1]
    whole = lambda shape: pl.BlockSpec(shape, lambda i: (0, 0))
    block = lambda cols: pl.BlockSpec((PROJECTED, cols), lambda i: (i, 0))
    return pl.pallas_call(
        functools.partial(project_kernel, query_heads, key_heads),
        grid=(rows // PROJECTED,),
        in_specs=[
            pl.BlockSpec((rows, width), lambda i: (0, 0), pipeline_mode=pl.Buffered(1)),
            whole((1, rows)),
            whole((1, width)),
            whole((width, wide)),
            whole((1, HEAD_SIZE)),
            whole((1, HEAD_SIZE)),
            block(HEAD_SIZE),
            block(HEAD_SIZE),
        ],
        out_specs=[block(width), block(wide), pl.BlockSpec((key_heads, PROJECTED, HEAD_SIZE), lambda i: (0, i, 0))],
        out_shape=[
            jax.ShapeDtypeStruct((rows, width), BF16),
            jax.ShapeDtypeStruct((rows, wide), BF16),
            jax.ShapeDtypeStruct((key_heads, rows, HEAD_SIZE), F32),
        ],
        compiler_params=pltpu.CompilerParams(vmem_limit_bytes=VMEM_LIMIT),
        name="project",
    )(x, places, gain, weights, gain_query, gain_key, cosine, sine)


def first_place(info_ref, blocks, docs, places):
    start = jnp.zeros_like(places)
    for doc in range(docs):
        begin = info_ref[2 * blocks + doc]
        start = jnp.maximum(start, jnp.where(places >= begin, begin, 0))
    return start


def across(values, terms):
    ones = jnp.ones((8, HEAD_SIZE), BF16)
    total = None
    for _ in range(terms):
        part = values.astype(BF16)
        values = values - part.astype(F32)
        total = dot_nt(ones, part) if total is None else total + dot_nt(ones, part)
    return total


def keep_padded(pairs):
    for ref, kept in pairs:
        rows = ref.shape[0]
        kept[:rows, : ref.shape[1]] = ref[...]
        kept[rows:, : ref.shape[1]] = jnp.zeros((kept.shape[0] - rows, ref.shape[1]), BF16)


def forward_kernel(group, blocks, docs, info_ref, q_ref, k_ref, v_ref, o_ref, lse_ref, keys_s, wide_s, acc_ref):
    i = pl.program_id(1)

    @pl.when(i == 0)
    def _():
        keep_padded(((k_ref, keys_s), (v_ref, wide_s)))
        wide_s[:, HEAD_SIZE:] = jnp.ones((wide_s.shape[0], HEAD_SIZE), BF16)

    acc_ref[...] = jnp.zeros_like(acc_ref)
    places = i * BLOCK + lax.broadcasted_iota(jnp.int32, (BLOCK, 1), 0)
    start = first_place(info_ref, blocks, docs, places)
    low = info_ref[i]

    def step(m, carry):
        base = (low + m * (STEP // BLOCK)) * BLOCK
        rows = pl.ds(pl.multiple_of(base, BLOCK), STEP)
        keys, values = keys_s[rows, :], wide_s[rows, :]
        other = base + lax.broadcasted_iota(jnp.int32, (BLOCK, STEP), 1)
        keep = (other <= places) & (other >= start)
        scores = [dot_nt(q_ref[:, h * HEAD_SIZE : (h + 1) * HEAD_SIZE], keys) for h in range(group)]
        for h in range(group):
            weights = jnp.where(keep, jnp.exp2(scores[h] * (SCALE * LOG2E)), 0.0)
            acc_ref[h * BLOCK : (h + 1) * BLOCK, :] += dot_nn(weights.astype(BF16), values)
        return carry

    lax.fori_loop(0, (i - low) // (STEP // BLOCK) + 1, step, 0)
    total = acc_ref[:, HEAD_SIZE:]
    out = (acc_ref[:, :HEAD_SIZE] / total).astype(BF16)
    for h in range(group):
        o_ref[:, h * HEAD_SIZE : (h + 1) * HEAD_SIZE] = out[h * BLOCK : (h + 1) * BLOCK]
    lse_ref[0, 0] = across(jnp.log2(total) * (1.0 / HEAD_SIZE), 3)


def head_specs(rows, group, first):
    wide = group * HEAD_SIZE
    return [
        pl.BlockSpec((BLOCK, wide), lambda h, i, s: (i, (first + h) * (group + 2) // group)),
        pl.BlockSpec((rows, HEAD_SIZE), lambda h, i, s: (0, (first + h) * (group + 2) + group)),
        pl.BlockSpec((rows, HEAD_SIZE), lambda h, i, s: (0, (first + h) * (group + 2) + group + 1)),
    ]


def attention_forward(info, qkv, query_heads, key_heads, docs):
    rows = qkv.shape[0]
    blocks = rows // BLOCK
    group = query_heads // key_heads
    wide = group * HEAD_SIZE
    return pl.pallas_call(
        functools.partial(forward_kernel, group, blocks, docs),
        grid_spec=pltpu.PrefetchScalarGridSpec(
            num_scalar_prefetch=1,
            grid=(key_heads, blocks),
            in_specs=head_specs(rows, group, 0),
            out_specs=[
                pl.BlockSpec((BLOCK, wide), lambda h, i, s: (i, h)),
                pl.BlockSpec((1, 1, 8, group * BLOCK), lambda h, i, s: (h, i, 0, 0)),
            ],
            scratch_shapes=[
                pltpu.VMEM((rows + STEP, HEAD_SIZE), BF16),
                pltpu.VMEM((rows + STEP, 2 * HEAD_SIZE), BF16),
                pltpu.VMEM((group * BLOCK, 2 * HEAD_SIZE), F32),
            ],
        ),
        out_shape=[
            jax.ShapeDtypeStruct((rows, key_heads * wide), BF16),
            jax.ShapeDtypeStruct((key_heads, blocks, 8, group * BLOCK), F32),
        ],
        compiler_params=pltpu.CompilerParams(vmem_limit_bytes=VMEM_LIMIT),
        cost_estimate=pl.CostEstimate(flops=0, bytes_accessed=100_000_000, transcendentals=0),
        name="attention_forward",
    )(info, qkv, qkv, qkv)


def backward_kernel(
    group,
    blocks,
    docs,
    info_ref,
    q_ref,
    k_ref,
    v_ref,
    o_ref,
    do_ref,
    lse_ref,
    cos_ref,
    sin_ref,
    scale_ref,
    gq_ref,
    gk_ref,
    grad_ref,
    dgain_ref,
    dk_acc,
    dv_acc,
    dq_acc,
    keys_s,
    values_s,
):
    i = pl.program_id(1)
    rows_all = k_ref.shape[0]

    @pl.when(i == 0)
    def _():
        dk_acc[...] = jnp.zeros_like(dk_acc)
        dv_acc[...] = jnp.zeros_like(dv_acc)
        keep_padded(((k_ref, keys_s), (v_ref, values_s)))

    @pl.when(i == 0)
    def _():
        dgain_ref[...] = jnp.zeros_like(dgain_ref)

    def stacked(value):
        return jnp.concatenate([value[:, h * HEAD_SIZE : (h + 1) * HEAD_SIZE] for h in range(group)], axis=0)

    queries, grads = stacked(q_ref[...]), stacked(do_ref[...])
    delta = across(stacked(o_ref[...]).astype(F32) * grads.astype(F32), 2)[:1]
    lse = lse_ref[0, 0, :1]
    dq_acc[...] = jnp.zeros_like(dq_acc)
    places = i * BLOCK + lax.rem(lax.broadcasted_iota(jnp.int32, (1, group * BLOCK), 1), BLOCK)
    start = first_place(info_ref, blocks, docs, places)
    low = info_ref[i]

    def step(m, carry):
        base = (low + m * (STEP // BLOCK)) * BLOCK
        rows = pl.ds(pl.multiple_of(base, BLOCK), STEP)
        keys, values = keys_s[rows, :], values_s[rows, :]
        other = base + lax.broadcasted_iota(jnp.int32, (STEP, group * BLOCK), 0)
        keep = (other <= places) & (other >= start)
        probs = jnp.where(keep, jnp.exp2(dot_nt(keys, queries) * (SCALE * LOG2E) - lse), 0.0)
        score_grad = (probs * (dot_nt(values, grads) - delta)).astype(BF16)
        dv_acc[rows, :] += dot_nn(probs.astype(BF16), grads)
        dk_acc[rows, :] += dot_nn(score_grad, queries)
        dq_acc[...] += dot_tn(score_grad, keys)
        return carry

    lax.fori_loop(0, (i - low) // (STEP // BLOCK) + 1, step, 0)

    def raw_grad(grad, rotated, rows, kind, gain):
        cosine, sine = cos_ref[rows, :], sin_ref[rows, :]
        r = scale_ref[0, rows, kind : kind + 1]
        unit = unrotate(rotated.astype(F32), cosine, sine) * (1.0 / gain)
        back = unrotate(grad * SCALE, cosine, sine)
        scaled = back * gain
        raw = r * (scaled - unit * jnp.mean(scaled * unit, axis=1, keepdims=True))
        return raw.astype(BF16), jnp.sum(back * unit, axis=0, keepdims=True)

    here = pl.ds(pl.multiple_of(i * BLOCK, BLOCK), BLOCK)
    for h in range(group):
        span = slice(h * HEAD_SIZE, (h + 1) * HEAD_SIZE)
        raw, gain_grad = raw_grad(dq_acc[h * BLOCK : (h + 1) * BLOCK, :], q_ref[:, span], here, h, gq_ref[...])
        grad_ref[here, span] = raw
        dgain_ref[0:1, :] += gain_grad

    @pl.when(i == blocks - 1)
    def _():
        grad_ref[:, (group + 1) * HEAD_SIZE :] = dv_acc[:rows_all, :].astype(BF16)

        def finish(b, carry):
            rows = pl.ds(pl.multiple_of(b * BLOCK, BLOCK), BLOCK)
            raw, gain_grad = raw_grad(dk_acc[rows, :], k_ref[rows, :], rows, group, gk_ref[...])
            grad_ref[rows, group * HEAD_SIZE : (group + 1) * HEAD_SIZE] = raw
            dgain_ref[1:2, :] += gain_grad
            return carry

        lax.fori_loop(0, blocks, finish, 0)


def attention_backward(
    info, qkv, attended, grads, lse, cosine, sine, scales, gain_query, gain_key, query_heads, key_heads, docs, kv
):
    rows = qkv.shape[0]
    blocks = rows // BLOCK
    group = query_heads // key_heads
    wide = group * HEAD_SIZE
    own = pl.BlockSpec((BLOCK, wide), lambda h, i, s: (i, kv))
    whole = lambda shape: pl.BlockSpec(shape, lambda h, i, s: (0, 0), pipeline_mode=pl.Buffered(1))
    return pl.pallas_call(
        functools.partial(backward_kernel, group, blocks, docs),
        grid_spec=pltpu.PrefetchScalarGridSpec(
            num_scalar_prefetch=1,
            grid=(1, blocks),
            in_specs=[
                *head_specs(rows, group, kv),
                own,
                own,
                pl.BlockSpec((1, 1, 8, group * BLOCK), lambda h, i, s: (kv, i, 0, 0)),
                whole((rows, HEAD_SIZE)),
                whole((rows, HEAD_SIZE)),
                pl.BlockSpec((1, rows, HEAD_SIZE), lambda h, i, s: (kv, 0, 0), pipeline_mode=pl.Buffered(1)),
                whole((1, HEAD_SIZE)),
                whole((1, HEAD_SIZE)),
            ],
            out_specs=[
                whole((rows, wide + 2 * HEAD_SIZE)),
                pl.BlockSpec((8, HEAD_SIZE), lambda h, i, s: (0, 0)),
            ],
            scratch_shapes=[
                pltpu.VMEM((rows + STEP, HEAD_SIZE), F32),
                pltpu.VMEM((rows + STEP, HEAD_SIZE), F32),
                pltpu.VMEM((group * BLOCK, HEAD_SIZE), F32),
                pltpu.VMEM((rows + STEP, HEAD_SIZE), BF16),
                pltpu.VMEM((rows + STEP, HEAD_SIZE), BF16),
            ],
        ),
        out_shape=[
            jax.ShapeDtypeStruct((rows, wide + 2 * HEAD_SIZE), BF16),
            jax.ShapeDtypeStruct((8, HEAD_SIZE), F32),
        ],
        compiler_params=pltpu.CompilerParams(vmem_limit_bytes=VMEM_LIMIT),
        cost_estimate=pl.CostEstimate(flops=0, bytes_accessed=100_000_000, transcendentals=0),
        name="attention_backward",
    )(info, qkv, qkv, qkv, attended, grads, lse, cosine, sine, scales, gain_query, gain_key)


def wide_block(ref):
    value = ref[...]
    return value.reshape(value.shape[0] * value.shape[2], value.shape[3])


def group_places(span):
    half = span // 2
    dp, t = lax.axis_index("dp"), lax.axis_index("tensor")
    p, c = dp // 2, lax.rem(dp, 2)
    aside = jnp.where(c == t // half, 0, 1)

    def place(k):
        return (p * 2 + (c ^ (k // half)), t ^ (k % half))

    def chunk(k):
        return ((k // half) ^ aside) * half + k % half

    return place, chunk


def group_barrier(span, place, *others):
    barrier = pltpu.get_barrier_semaphore()
    for to in [place(k) for k in range(1, span)] + list(others):
        pl.semaphore_signal(barrier, device_id=to, device_id_type=pl.DeviceIdType.MESH)
    pl.semaphore_wait(barrier, span - 1 + len(others))


def remote_copy(src, dst, send_sem, recv_sem, to):
    return pltpu.make_async_remote_copy(
        src_ref=src,
        dst_ref=dst,
        send_sem=send_sem,
        recv_sem=recv_sem,
        device_id=to,
        device_id_type=pl.DeviceIdType.MESH,
    )


def arrival_order(span):
    half = span // 2
    return [0, half] + [k for k in range(1, span) if k != half]


def output_kernel(
    span,
    heads_ref,
    places_ref,
    w_hbm,
    tokens_ref,
    gain_ref,
    middle_ref,
    normed_ref,
    mixed_ref,
    w_ref,
    out_s,
    send_sems,
    recv_sems,
    local_sem,
):
    place, chunk = group_places(span)
    rows, width = tokens_ref.shape
    load = pltpu.make_async_copy(w_hbm, w_ref, local_sem)
    load.start()
    group_barrier(span, place)
    copies = {}
    index = lax.broadcasted_iota(jnp.int32, (rows, heads_ref.shape[0]), 1)
    for k in reversed(arrival_order(span)):
        picks = jnp.where(places_ref[k * rows : (k + 1) * rows, :] == index, 1.0, 0.0).astype(BF16)
        block = dot_nn(picks, heads_ref[...]).astype(BF16)
        if k:
            out_s[k] = block
            copies[k] = remote_copy(out_s.at[k], mixed_ref.at[k], send_sems.at[k], recv_sems.at[k], place(k))
            copies[k].start()
        else:
            mixed_ref[0] = block
    middle_ref[...] = tokens_ref[...].astype(F32)
    load.wait()
    for k in arrival_order(span):
        if k:
            copies[k].wait_recv()
        weights = w_ref[:, chunk(k)].reshape(width, w_ref.shape[3])
        middle_ref[...] += dot_nt(mixed_ref[k], weights)
    middle = middle_ref[...]
    normed_ref[...] = (middle * row_scale(middle) * gain_ref[...]).astype(BF16)
    for k in range(1, span):
        copies[k].wait_send()


def output_project(heads, places, weights, tokens, gain):
    devices, span, shard, cols = weights.shape
    rows, width = tokens.shape
    any_ref = pl.BlockSpec(memory_space=pl.ANY)
    local_ref = pl.BlockSpec(memory_space=pltpu.VMEM)
    return pl.pallas_call(
        functools.partial(output_kernel, span),
        in_specs=[local_ref] * 2 + [any_ref] + [local_ref] * 2,
        out_specs=[local_ref] * 3,
        out_shape=[
            jax.ShapeDtypeStruct((rows, width), F32),
            jax.ShapeDtypeStruct((rows, width), BF16),
            jax.ShapeDtypeStruct((span, rows, cols), BF16),
        ],
        scratch_shapes=[
            pltpu.VMEM(weights.shape, BF16),
            pltpu.VMEM((span, rows, cols), BF16),
            pltpu.SemaphoreType.DMA((span,)),
            pltpu.SemaphoreType.DMA((span,)),
            pltpu.SemaphoreType.DMA,
        ],
        compiler_params=pltpu.CompilerParams(
            collective_id=1, has_side_effects=True, vmem_limit_bytes=VMEM_LIMIT
        ),
        cost_estimate=pl.CostEstimate(flops=0, bytes_accessed=100_000_000, transcendentals=0),
        name="output_project",
    )(heads, places, weights, tokens, gain)


def output_back_kernel(
    span,
    b_ref,
    mixed_ref,
    places_ref,
    w_hbm,
    result_hbm,
    feed_hbm,
    out_ref,
    dw_hbm,
    result_out,
    w_ref,
    grad_s,
    in_s,
    dw_ref,
    bt_ref,
    send_sems,
    recv_sems,
    local_sems,
):
    place, chunk = group_places(span)
    rows, width = b_ref.shape
    cols = w_ref.shape[3]
    load = pltpu.make_async_copy(w_hbm, w_ref, local_sems.at[span])
    load.start()
    dp, t = lax.axis_index("dp"), lax.axis_index("tensor")
    p, c = dp // 2, lax.rem(dp, 2)
    settled = c == t // (span // 2)
    partner = (p * 2 + 1 - c, span - 1 - t)
    group_barrier(span, place, partner)
    load.wait()
    swap = remote_copy(result_hbm, result_out, send_sems.at[0], recv_sems.at[0], partner)
    keep = pltpu.make_async_copy(result_hbm, result_out, local_sems.at[span + 1])
    copies = {}
    for k in reversed(arrival_order(span)):
        block = dot_nn(b_ref[...], w_ref[:, chunk(k)].reshape(width, cols)).astype(BF16)
        if k:
            grad_s[k] = block
            copies[k] = remote_copy(grad_s.at[k], in_s.at[k], send_sems.at[k], recv_sems.at[k], place(k))
            copies[k].start()
        else:
            in_s[0] = block
    @pl.when(settled)
    def _():
        keep.start()

    @pl.when(jnp.logical_not(settled))
    def _():
        swap.start()

    bt_ref[...] = b_ref[...].T
    stores = []
    base = dw_hbm.shape[3] - span * cols
    for k in range(span):
        dw_ref[k] = dot_nn(bt_ref[...], mixed_ref[k]).astype(BF16).reshape(dw_ref.shape[1:])
        to = pl.ds(pl.multiple_of(base + chunk(k) * cols, 128), cols)
        stores.append(pltpu.make_async_copy(dw_ref.at[k], dw_hbm.at[:, 0, :, to], local_sems.at[k]))
        stores[-1].start()
    for k in arrival_order(span):
        if k:
            copies[k].wait_recv()

        def sort_step(m, carry, k=k):
            at = pl.ds(pl.multiple_of(m * rows, rows), rows)
            block = dot_nn(sorting(places_ref[k], m * rows, rows), in_s[k]).astype(BF16)
            if k:
                out_ref[at, :] += block
            else:
                out_ref[at, :] = block
            return carry

        lax.fori_loop(0, span, sort_step, 0)
    for copy in stores:
        copy.wait()
    for copy in copies.values():
        copy.wait_send()

    @pl.when(settled)
    def _():
        keep.wait()

    @pl.when(jnp.logical_not(settled))
    def _():
        swap.wait()


def output_back(branch, mixed, places, weights, result, feed_grads):
    devices, span, shard, cols = weights.shape
    rows, width = branch.shape
    any_ref = pl.BlockSpec(memory_space=pl.ANY)
    local_ref = pl.BlockSpec(memory_space=pltpu.VMEM)
    return pl.pallas_call(
        functools.partial(output_back_kernel, span),
        in_specs=[local_ref, local_ref, local_ref, any_ref, any_ref, any_ref],
        out_specs=[local_ref, any_ref, any_ref],
        input_output_aliases={5: 1},
        out_shape=[
            jax.ShapeDtypeStruct((span * rows, cols), BF16),
            jax.ShapeDtypeStruct(feed_grads.shape, BF16),
            jax.ShapeDtypeStruct(result.shape, BF16),
        ],
        scratch_shapes=[
            pltpu.VMEM(weights.shape, BF16),
            pltpu.VMEM((span, rows, cols), BF16),
            pltpu.VMEM((span, rows, cols), BF16),
            pltpu.VMEM((span, devices, shard, cols), BF16),
            pltpu.VMEM((width, rows), BF16),
            pltpu.SemaphoreType.DMA((span,)),
            pltpu.SemaphoreType.DMA((span,)),
            pltpu.SemaphoreType.DMA((span + 2,)),
        ],
        compiler_params=pltpu.CompilerParams(
            collective_id=2, has_side_effects=True, vmem_limit_bytes=VMEM_LIMIT
        ),
        cost_estimate=pl.CostEstimate(flops=0, bytes_accessed=100_000_000, transcendentals=0),
        name="output_back",
    )(branch, mixed, places, weights, result, feed_grads)


def feed_kernel(last, x_ref, c_ref, w_ref, *refs):
    if last:
        (out_in, ng_in, middle_ref, gain_ref, result_ref, grad_ref, branch_ref, dgain_ref, dw_ref, out_s, ng_s) = refs[:11]
        act_s, gg_s, ug_s, xt_s, ct_s = refs[11:]
    else:
        out_s, ng_s, dw_ref, act_s, gg_s, ug_s, xt_s, ct_s = refs
    j = pl.program_id(0)
    rows_all, width = x_ref.shape
    hidden = act_s.shape[1]
    devices, _, shard, _ = w_ref.shape
    chunk = rows_all

    @pl.when(j == 0)
    def _():
        xt_s[...] = x_ref[...].T
        ct_s[...] = c_ref[...].T
        out_s[...] = out_in[...] if last else jnp.zeros_like(out_s)
        ng_s[...] = ng_in[...] if last else jnp.zeros_like(ng_s)

    def part(k):
        return w_ref[:, 0, :, k * hidden : (k + 1) * hidden].reshape(width, hidden)

    def rows_step(m, carry):
        rows = pl.ds(pl.multiple_of(m * chunk, chunk), chunk)
        gate = dot_nn(x_ref[rows, :], part(0))
        upward = dot_nn(x_ref[rows, :], part(1))
        act_grad = dot_nn(c_ref[rows, :], part(2))
        sig = 1.0 / (1.0 + jnp.exp(-gate))
        silu = gate * sig
        act = (silu * upward).astype(BF16)
        up_grad = (act_grad * silu).astype(BF16)
        gate_grad = (act_grad * upward * sig * (1.0 + gate * (1.0 - sig))).astype(BF16)
        act_s[rows, :] = act
        ug_s[rows, :] = up_grad
        gg_s[rows, :] = gate_grad
        out_s[rows, :] += dot_nt(act, part(2))
        ng_s[rows, :] += dot_nt(gate_grad, part(0)) + dot_nt(up_grad, part(1))
        return carry

    lax.fori_loop(0, rows_all // chunk, rows_step, 0)

    group = ROWS // shard

    def grad_step(m, carry):
        rows = pl.ds(pl.multiple_of(m * ROWS, ROWS), ROWS)
        to = pl.ds(m * group, group)
        for k, left, right in ((0, xt_s, gg_s), (1, xt_s, ug_s), (2, ct_s, act_s)):
            value = dot_nn(left[rows, :], right[...]).astype(BF16)
            dw_ref[to, 0, :, k * hidden : (k + 1) * hidden] = value.reshape(group, shard, hidden)
        return carry

    lax.fori_loop(0, width // ROWS, grad_step, 0)

    if not last:
        return

    @pl.when(j == pl.num_programs(0) - 1)
    def _():
        middle = middle_ref[...]
        result_ref[...] = (middle + out_s[...]).astype(BF16)
        r = row_scale(middle)
        unit = middle * r
        dgain_ref[...] = jnp.broadcast_to(jnp.sum(ng_s[...] * unit, axis=0, keepdims=True), dgain_ref.shape)
        scaled = ng_s[...] * gain_ref[...]
        grad = c_ref[...].astype(F32) + r * (scaled - unit * jnp.mean(scaled * unit, axis=-1, keepdims=True))
        grad_ref[...] = grad
        branch_ref[...] = grad.astype(BF16)


def feed(x, cot, weights, *rest, room=0):
    rows, width = x.shape
    devices, span, shard, cols = weights.shape
    hidden = cols // 3
    last = len(rest) > 0
    whole = lambda shape: pl.BlockSpec(shape, lambda j: (0, 0), pipeline_mode=pl.Buffered(1))
    chunk = pl.BlockSpec((devices, 1, shard, cols), lambda j: (0, j, 0, 0))
    full = whole((rows, width))
    grads = jax.ShapeDtypeStruct((devices, span, shard, cols + room), BF16)
    shape = lambda kind: jax.ShapeDtypeStruct((rows, width), kind)
    sums = [pltpu.VMEM((rows, width), F32)] * 2 if last else []
    return pl.pallas_call(
        functools.partial(feed_kernel, last),
        grid=(span,),
        in_specs=[full, full, chunk] + ([full, full, full, whole((1, width))] if last else []),
        out_specs=[full, full, full, whole((8, width)), chunk] if last else [full, full, chunk],
        out_shape=[shape(BF16), shape(F32), shape(BF16), jax.ShapeDtypeStruct((8, width), F32), grads]
        if last
        else [shape(F32), shape(F32), grads],
        scratch_shapes=sums + [pltpu.VMEM((rows, hidden), BF16)] * 3 + [pltpu.VMEM((width, rows), BF16)] * 2,
        compiler_params=pltpu.CompilerParams(vmem_limit_bytes=VMEM_LIMIT),
        name="feed_forward",
    )(x, cot, weights, *rest)


def last_kernel(
    pairs,
    span,
    count,
    *refs,
):
    grads_hbm, sorted_hbm = refs[:count], refs[count : 2 * count]
    last_body(pairs, span, grads_hbm, sorted_hbm, *refs[2 * count :])


def last_body(
    pairs,
    span,
    grads_hbm,
    sorted_hbm,
    normed_hbm,
    w_ref,
    middle_ref,
    tokens_ref,
    gain_ref,
    gains_ref,
    output_ref,
    rows_out,
    heads_out,
    gains_out,
    output_out,
    grads,
    sorted_s,
    normed_s,
    turned,
    mine,
    theirs,
    from_sibling,
    from_line,
    heads_s,
    heads_in,
    far_in,
    far_s,
    near_in,
    near_s,
    final_s,
    pass_s,
    far_pass,
    wt_s,
    gains_one,
    gains_two,
    gains_s,
    send_sems,
    recv_sems,
    local_sems,
):
    half = span // 2
    dp, t = lax.axis_index("dp"), lax.axis_index("tensor")
    p, c = dp // 2, lax.rem(dp, 2)
    settled = c == t // half
    rows, width = middle_ref.shape
    shard = output_ref.shape[1]
    place = lambda pp, cc, tt: (pp * 2 + cc, tt)
    sibling = place(p, 1 - c, t)
    used = [0]

    def copy_to(src, dst, to):
        used[0] += 1
        at = used[0] - 1
        return remote_copy(src, dst, send_sems.at[at], recv_sems.at[at], to)

    count = len(grads_hbm)
    wide = grads_hbm[0].shape[1]

    def side_by_side(sources, rows_of, dst, sem):
        return [
            pltpu.make_async_copy(src.at[rows_of], dst.at[:, pl.ds(h * wide, wide)], local_sems.at[sem + h])
            for h, src in enumerate(sources)
        ]

    loads = [side_by_side(grads_hbm, pl.ds(k * rows, rows), grads.at[k], k * count) for k in range(span)]
    order = list(range(half + 1, span)) + list(range(1, half)) + [half, 0]
    for k in order:
        for load in loads[k]:
            load.start()
    more = [pltpu.make_async_copy(normed_hbm, normed_s, local_sems.at[span * count])]
    more += side_by_side(sorted_hbm, pl.ds(0, span * rows), sorted_s, span * count + 1)
    for load in more:
        load.start()

    barrier = pltpu.get_barrier_semaphore()
    greeted = 0
    for k in range(1, 2 * span):
        pl.semaphore_signal(
            barrier, device_id=place(p, c ^ (k // span), t ^ (k % span)), device_id_type=pl.DeviceIdType.MESH
        )
        greeted += 1
    for k in range(1, pairs):
        pl.semaphore_signal(barrier, device_id=place(p ^ k, c, t), device_id_type=pl.DeviceIdType.MESH)
        greeted += 1
    pl.semaphore_wait(barrier, greeted)

    wt_s[...] = w_ref[...].T
    outputs = [copy_to(output_ref.at[r], output_out.at[r - 1], place(p, c, t ^ r)) for r in range(1, span)]

    piece = rows // 2

    def multiply(k, dst, slot):
        def step(m, carry):
            at = pl.ds(pl.multiple_of(m * piece, piece), piece)
            dst[slot, at, :] = dot_nn(grads[k, at, :], wt_s[...]).astype(BF16)
            return carry

        lax.fori_loop(0, 2, step, 0)

    sides, hops = {}, {}
    away = list(range(1, half))

    def product_for_sibling(k):
        for load in loads[half + k]:
            load.wait()
        multiply(half + k, theirs, k)
        sides[k] = copy_to(theirs.at[k], from_sibling.at[k], sibling)
        sides[k].start()

    def own_sum(k):
        for load in loads[k]:
            load.wait()
        multiply(k, mine, k)
        sides[k].wait_recv()
        mine[k] = (mine[k].astype(F32) + from_sibling[k].astype(F32)).astype(BF16)

    for k in away:
        product_for_sibling(k)
    for k in away:
        own_sum(k)
        for m in range(2):
            at = pl.ds(m * piece, piece)
            hops[k, m] = copy_to(mine.at[k, at], from_line.at[k - 1, at], place(p, c, t ^ k))
            hops[k, m].start()
    product_for_sibling(0)
    own_sum(0)
    for load in more:
        load.wait()
    turned[...] = normed_s[...].T
    block = 2 * shard

    def weights_step(m, carry):
        at = pl.ds(pl.multiple_of(m * block, block), block)
        heads_s[at, :] = dot_nn(turned[at, :], sorted_s[...]).astype(BF16)
        return carry

    lax.fori_loop(0, pairs, weights_step, 0)
    heads_copies = []
    for k in range(1, pairs):
        there = pl.ds((p ^ k) * block, block)
        heads_copies.append(copy_to(heads_s.at[there], heads_in.at[k - 1], place(p ^ k, c, t)))
        heads_copies[-1].start()

    for copy in outputs:
        copy.start()

    swaps = []
    gain_sum = jnp.zeros((1, width), F32)
    for m in range(2):
        at = pl.ds(m * piece, piece)
        for k in range(1, half):
            hops[k, m].wait_recv()
        grad = mine[0, at, :].astype(F32)
        for k in range(1, half):
            grad = grad + from_line[k - 1, at, :].astype(F32)
        inputs = tokens_ref[at, :].astype(F32)
        r = row_scale(inputs)
        unit = inputs * r
        gain_sum = gain_sum + jnp.sum(grad * unit, axis=0, keepdims=True)
        scaled = grad * gain_ref[...]
        final_s[at, :] = (
            middle_ref[at, :] + r * (scaled - unit * jnp.mean(scaled * unit, axis=-1, keepdims=True))
        ).astype(BF16)
        there = place(p, 1 - c, span - 1 - t)
        swap = copy_to(final_s.at[at], rows_out.at[at] if m == 0 else pass_s, there if m == 0 else sibling)
        keep = pltpu.make_async_copy(final_s.at[at], rows_out.at[at], local_sems.at[(span + 1) * count + 1 + m])
        swaps.append((swap, keep))

        @pl.when(settled)
        def _():
            keep.start()

        @pl.when(jnp.logical_not(settled))
        def _():
            swap.start()

    gains_s[...] = gains_ref[...]
    gains_s[0:1, :] = gain_sum
    first_gains = [
        copy_to(gains_s, gains_one.at[k - 1], place(p, c ^ (k // span), t ^ (k % span))) for k in range(1, 2 * span)
    ]
    for copy in first_gains:
        copy.start()

    at = pl.ds(piece, piece)
    handed = swaps[1][0]
    passed = copy_to(pass_s, rows_out.at[at], place(p, c, span - 1 - t))

    @pl.when(settled)
    def _():
        handed.wait_recv()
        passed.start()

    for copy in heads_copies:
        copy.wait_recv()
    summed = heads_s[pl.ds(p * block, block), :].astype(F32)
    for k in range(1, pairs):
        summed = summed + heads_in[k - 1].astype(F32)
    far_s[...] = summed.astype(BF16)
    side = copy_to(far_s, far_pass, sibling)
    far = copy_to(far_pass, far_in, place(p, 1 - c, lax.rem(t + half, span)))
    near = copy_to(near_s, near_in, sibling)

    @pl.when(jnp.logical_not(settled))
    def _():
        side.start()

    for copy in first_gains:
        copy.wait_recv()
    total = gains_s[...]
    for k in range(1, 2 * span):
        total = total + gains_one[k - 1]
    gains_out[...] = total
    @pl.when(settled)
    def _():
        side.wait_recv()
        far.start()

    second_gains = [copy_to(gains_out, gains_two.at[k - 1], place(p ^ k, c, t)) for k in range(1, pairs)]
    for copy in second_gains:
        copy.start()

    for copy in second_gains:
        copy.wait()
    for copy in first_gains:
        copy.wait_send()
    whole = gains_out[...]
    for k in range(1, pairs):
        whole = whole + gains_two[k - 1]
    gains_out[...] = whole

    @pl.when(settled)
    def _():
        far.wait_recv()
        own = pl.ds(c * shard, shard)
        other = pl.ds((1 - c) * shard, shard)
        near_s[...] = (far_s[other, :].astype(F32) + far_in[other, :].astype(F32)).astype(BF16)
        near.start()
        far.wait_send()
        heads_out[...] = far_s[own, :].astype(F32) + far_in[own, :].astype(F32)
        near.wait_send()

    @pl.when(jnp.logical_not(settled))
    def _():
        side.wait_send()
        near.wait_recv()
        heads_out[...] = near_in[...].astype(F32)

    for copy in list(sides.values()) + list(hops.values()) + heads_copies:
        copy.wait_send()
    for copy in outputs:
        copy.wait()
    @pl.when(settled)
    def _():
        for swap, keep in swaps:
            keep.wait()
        passed.wait_send()

    @pl.when(jnp.logical_not(settled))
    def _():
        for swap, keep in swaps:
            swap.wait_send()
        swaps[0][0].wait_recv()
        passed.wait_recv()


def last_transfers(pairs, span, grads, grads_sorted, normed, weights, middle_grad, tokens, gain, gains, output):
    rows, width = tokens.shape
    half = span // 2
    shard = output.shape[1]
    cols = weights.shape[1]
    count = len(grads)
    any_ref = pl.BlockSpec(memory_space=pl.ANY)
    local_ref = pl.BlockSpec(memory_space=pltpu.VMEM)
    copies = span - 1 + half + 2 * (half - 1) + 2 * (pairs - 1) + 2 + 2 * span - 1 + 4
    return pl.pallas_call(
        functools.partial(last_kernel, pairs, span, count),
        in_specs=[any_ref] * (2 * count + 1) + [local_ref] * 5 + [any_ref],
        out_specs=[any_ref, local_ref, local_ref, any_ref],
        out_shape=[
            jax.ShapeDtypeStruct((rows, width), BF16),
            jax.ShapeDtypeStruct((shard, cols), F32),
            jax.ShapeDtypeStruct((8, width), F32),
            jax.ShapeDtypeStruct((span - 1, *output.shape[1:]), BF16),
        ],
        scratch_shapes=[
            pltpu.VMEM((span, rows, cols), BF16),
            pltpu.VMEM((span * rows, cols), BF16),
            pltpu.VMEM((span * rows, width), BF16),
            pltpu.VMEM((width, span * rows), BF16),
            pltpu.VMEM((half, rows, width), BF16),
            pltpu.VMEM((half, rows, width), BF16),
            pltpu.VMEM((half, rows, width), BF16),
            pltpu.VMEM((max(half - 1, 1), rows, width), BF16),
            pltpu.VMEM((width, cols), BF16),
            pltpu.VMEM((pairs - 1, 2 * shard, cols), BF16),
            pltpu.VMEM((2 * shard, cols), BF16),
            pltpu.VMEM((2 * shard, cols), BF16),
            pltpu.VMEM((shard, cols), BF16),
            pltpu.VMEM((shard, cols), BF16),
            pltpu.VMEM((rows, width), BF16),
            pltpu.VMEM((rows // 2, width), BF16),
            pltpu.VMEM((2 * shard, cols), BF16),
            pltpu.VMEM((cols, width), BF16),
            pltpu.VMEM((2 * span - 1, 8, width), F32),
            pltpu.VMEM((pairs - 1, 8, width), F32),
            pltpu.VMEM((8, width), F32),
            pltpu.SemaphoreType.DMA((copies,)),
            pltpu.SemaphoreType.DMA((copies,)),
            pltpu.SemaphoreType.DMA(((span + 1) * count + 3,)),
        ],
        compiler_params=pltpu.CompilerParams(
            collective_id=3, has_side_effects=True, vmem_limit_bytes=VMEM_LIMIT
        ),
        name="last_transfers",
    )(*grads, *grads_sorted, normed, weights, middle_grad, tokens, gain, gains, output)


def local(
    tokens,
    lengths,
    row_order,
    attention_gain,
    query_gain,
    key_gain,
    query_weight,
    key_matrix,
    value_matrix,
    output_weight,
    feedforward_gain,
    gate_weight,
    up_weight,
    down_weight,
    cotangent,
):
    span = lax.axis_size("tensor")
    pairs = lax.axis_size("dp") // 2
    half = span // 2
    rows, width = tokens.shape
    group_rows = rows * span
    blocks = group_rows // BLOCK
    docs = lengths.shape[1]
    query_heads = query_weight.shape[1] // HEAD_SIZE
    key_heads = key_matrix.shape[1] // HEAD_SIZE
    head_columns = query_weight.shape[1]
    hidden_columns = gate_weight.shape[1]
    shard = query_weight.shape[0]

    dp, t = lax.axis_index("dp"), lax.axis_index("tensor")
    p, c = dp // 2, lax.rem(dp, 2)
    q = t // half
    settled = c == q

    def send(x, route):
        moves = []
        for pp in range(pairs):
            for cc in range(2):
                for tt in range(span):
                    to = route(pp, cc, tt)
                    if to is not None:
                        moves.append(((pp * 2 + cc) * span + tt, (to[0] * 2 + to[1]) * span + to[2]))
        return lax.ppermute(x, AXES, moves)

    def swap(x):
        moved = send(x, lambda pp, cc, tt: (pp, 1 - cc, span - 1 - tt) if cc != tt // half else None)
        return jnp.where(settled, x, moved)

    never = row_order[0, 0] < 0

    def behind(x, other):
        return jnp.where(never, other[0, 0].astype(x.dtype), x)

    def line(x, steps):
        return [send(x, lambda pp, cc, tt: (pp, cc, tt ^ r)) for r in steps]

    def gather_wide(pieces):
        cols = pieces[0].shape[1]
        out = by_rows(lax.all_gather(by_rows(jnp.concatenate(pieces, axis=0)), "dp", axis=0, tiled=True))
        return out.reshape(2 * pairs, len(pieces), shard, cols)

    def scatter_wide(grads):
        devices, count, _, cols = grads.shape
        out = by_rows(grads.reshape(devices * count * shard, cols))
        out = by_rows(lax.psum_scatter(out, "dp", scatter_dimension=0, tiled=True))
        return [out[r * shard : (r + 1) * shard] for r in range(count)]

    per_query, per_key = head_columns // key_heads, HEAD_SIZE
    heads_local = []
    for kv in range(key_heads):
        heads_local.append(query_weight[:, kv * per_query : (kv + 1) * per_query])
        heads_local.append(key_matrix[:, kv * per_key : (kv + 1) * per_key])
        heads_local.append(value_matrix[:, kv * per_key : (kv + 1) * per_key])
    heads_local = by_rows(jnp.concatenate(heads_local, axis=1))
    feed_local = by_rows(jnp.concatenate([gate_weight, up_weight, down_weight.T], axis=1))
    gains = jnp.concatenate([attention_gain, query_gain, key_gain, feedforward_gain])
    small, tiny = attention_gain.shape[0], query_gain.shape[0]
    few, lanes = gains.shape[0], -(-gains.shape[0] // 128) * 128
    gains = jnp.broadcast_to(jnp.pad(gains, (0, lanes - few))[None], (16, lanes))
    facts = jnp.concatenate([row_order[0], lengths[0]])
    fact_rows = -(-facts.shape[0] // 1024) * 8
    facts = jnp.pad(facts, (0, fact_rows * 128 - facts.shape[0])).reshape(fact_rows, 128)
    tokens_all, heads_weights, output_line, gains, facts_moved = first_transfers(
        pairs, span, tokens, heads_local, by_rows(output_weight.T), gains, facts
    )
    swapped = tokens_all[0]
    tokens_all = tokens_all.reshape(group_rows, width)
    own_weights = gather_wide([feed_local])
    output_weights = gather_wide([output_line[r] for r in range(span)])
    feed_line = line(behind(feed_local, swapped), range(1, span))

    gains = gains.reshape(2 * pairs, 16, lanes)[:, 0, :few].astype(F32)
    gain_one = gains[:, :small].reshape(1, width)
    gain_query = gains[:, small : small + tiny].reshape(1, HEAD_SIZE)
    gain_key = gains[:, small + tiny : small + 2 * tiny].reshape(1, HEAD_SIZE)
    gain_two = gains[:, small + 2 * tiny : small + 2 * tiny + small].reshape(1, width)
    facts = jnp.where(settled, facts, facts_moved).reshape(-1)[: group_rows + docs]
    order, length = facts[:group_rows].reshape(span, rows), facts[group_rows:]
    places = []
    for k in range(span):
        tt, cc = t ^ (k % half), c ^ (k // half)
        places.append(lax.dynamic_index_in_dim(order, jnp.where(cc == tt // half, tt, span - 1 - tt), 0, False))
    places = jnp.concatenate(places)
    before = jnp.arange(docs)[None, :] < jnp.arange(docs)[:, None]
    starts = jnp.sum(jnp.where(before, length[None, :], 0), axis=1).astype(jnp.int32)

    def start_of(place):
        return jnp.max(jnp.where(place[:, None] >= starts[None, :], starts[None, :], 0), axis=1)

    index = jnp.arange(blocks, dtype=jnp.int32) * BLOCK
    low = start_of(index) // BLOCK
    clear = (start_of(index + BLOCK - 1) + BLOCK - 1) // BLOCK
    info = jnp.concatenate([low, clear, starts]).astype(jnp.int32)
    rate = np.float32(THETA) ** (-(np.arange(HEAD_SIZE // 2, dtype=np.float32) * np.float32(2.0) / HEAD_SIZE))
    angle = np.arange(group_rows, dtype=np.float32)[:, None] * rate.astype(np.float32)[None, :]
    turn_c, turn_s = np.cos(angle), np.sin(angle)
    tables = np.concatenate([turn_c, turn_c, -turn_s, turn_s], axis=1).astype(np.float32)
    turned, index = jnp.asarray(tables), jnp.arange(group_rows, dtype=jnp.int32)[:, None]
    for doc in range(1, docs):
        moved = lax.dynamic_slice(jnp.asarray(np.concatenate([tables, tables])), (group_rows - starts[doc], 0), tables.shape)
        turned = jnp.where(index >= starts[doc], moved, turned)
    cosine, sine = turned[:, :HEAD_SIZE], turned[:, HEAD_SIZE:]

    cot_own = swap(cotangent)
    normed, qkv, scales = project(
        tokens_all, places[None], gain_one, heads_weights, gain_query, gain_key, cosine, sine, query_heads, key_heads
    )

    line_weights = gather_wide([behind(piece, qkv) for piece in feed_line])

    attended, lse = attention_forward(info, qkv, query_heads, key_heads, docs)

    hidden = gate_weight.shape[1]
    middle, normed_two, mixed = output_project(attended, places[:, None], output_weights, swapped, gain_two)
    out, normed_grad, line_grad = feed(normed_two, cot_own, line_weights)
    result, middle_grad, branch, gain_two_grad, own_grad = feed(
        normed_two, cot_own, own_weights, out, normed_grad, middle, gain_two, room=span * head_columns
    )
    line_sum = scatter_wide(line_grad)

    attended_grad, own_grad, layer_output = output_back(
        branch, mixed, places.reshape(span, 1, rows), output_weights, result, own_grad
    )
    [both_sum] = scatter_wide(own_grad)
    own_sum = both_sum[:, : 3 * hidden]

    head_grads, head_gains = [], 0.0
    for kv in range(key_heads):
        if kv > 0:
            info = jnp.where(never, behind(line_sum[0], head_grads[0])[0, 0].astype(jnp.int32), info)
        grads, gains_of = attention_backward(
            info,
            qkv,
            attended,
            attended_grad,
            lse,
            cosine,
            sine,
            scales,
            gain_query,
            gain_key,
            query_heads,
            key_heads,
            docs,
            kv,
        )
        if kv == 0:
            line_in = [
                send(behind(piece, grads), lambda pp, cc, tt: (pp, cc, tt ^ r))
                for r, piece in enumerate(line_sum, start=1)
            ]
        head_grads.append(grads)
        head_gains = head_gains + gains_of
    arrived = sum(piece[0, 0].astype(jnp.int32) for piece in line_in)
    tied = jnp.where(never, arrived, places)
    qkv_rows = [
        jnp.take(grads, places if kv + 1 < key_heads else tied, axis=0, mode="clip")
        for kv, grads in enumerate(head_grads)
    ]
    output_sum = behind(both_sum, qkv_rows[-1])[:, 3 * hidden :]
    output_sum = output_sum.reshape(shard, span, head_columns).transpose(1, 0, 2)
    gain_rows = jnp.concatenate(
        [
            jnp.zeros((1, width), F32),
            gain_two_grad[:1],
            jnp.pad(head_gains[:2].reshape(1, 2 * HEAD_SIZE), ((0, 0), (0, width - 2 * HEAD_SIZE))),
            jnp.zeros((5, width), F32),
        ]
    )
    input_grad, heads_sum, gain_sums, output_in = last_transfers(
        pairs,
        span,
        qkv_rows,
        head_grads,
        normed,
        heads_weights,
        middle_grad,
        swapped,
        gain_one,
        gain_rows,
        output_sum,
    )

    def total(first, others):
        out = first.astype(F32)
        for other in others:
            out = out + other.astype(F32)
        return out

    wide_sum = total(behind(own_sum, gain_sums), [behind(piece, gain_sums) for piece in line_in])
    output_sum = total(output_sum[0], [output_in[k] for k in range(span - 1)])
    stride = per_query + 2 * per_key
    columns = lambda at, size: jnp.concatenate(
        [heads_sum[:, kv * stride + at : kv * stride + at + size] for kv in range(key_heads)], axis=1
    )
    cut = lambda row, at, size: lax.dynamic_slice(gain_sums[row], (at + dp * size,), (size,))
    return (
        layer_output,
        input_grad,
        cut(0, 0, small),
        cut(2, 0, tiny),
        cut(2, HEAD_SIZE, tiny),
        columns(0, per_query),
        columns(per_query, per_key),
        columns(per_query + per_key, per_key),
        output_sum.T,
        cut(1, 0, small),
        wide_sum[:, :hidden],
        wide_sum[:, hidden : 2 * hidden],
        wide_sum[:, 2 * hidden :].T,
    )


def solution(mesh):
    placed = (
        P(AXES, None),
        P("dp", None),
        P("dp", None),
        P("dp"),
        P("dp"),
        P("dp"),
        P("dp", "tensor"),
        P("dp", "tensor"),
        P("dp", "tensor"),
        P("tensor", "dp"),
        P("dp"),
        P("dp", "tensor"),
        P("dp", "tensor"),
        P("tensor", "dp"),
        P(AXES, None),
    )
    return jax.shard_map(
        local,
        mesh=mesh,
        in_specs=placed,
        out_specs=(
            P(AXES, None),
            P(AXES, None),
            P("dp"),
            P("dp"),
            P("dp"),
            P("dp", "tensor"),
            P("dp", "tensor"),
            P("dp", "tensor"),
            P("tensor", "dp"),
            P("dp"),
            P("dp", "tensor"),
            P("dp", "tensor"),
            P("tensor", "dp"),
        ),
        check_vma=False,
    )
```

```python
import functools

import jax
import jax.numpy as jnp
import numpy as np
from jax import lax
from jax.experimental.layout import Layout, with_layout_constraint
from jax.experimental import pallas as pl
from jax.experimental.pallas import tpu as pltpu
from jax.sharding import PartitionSpec as P

HEAD_SIZE = 128
EPSILON = 1e-06
THETA = 1000000.0
AXES = ("dp", "tensor")
ROWS = 256
PROJECTED = 512
BLOCK = 512
STEP = 512
SCALE = HEAD_SIZE ** (-0.5)
LOG2E = 1.4426950408889634
VMEM_LIMIT = 56 * 1024 * 1024
F32 = jnp.float32
BF16 = jnp.bfloat16


def dot_nn(left, right):
    return lax.dot_general(left, right, (((1,), (0,)), ((), ())), preferred_element_type=F32)


def dot_nt(left, right):
    return lax.dot_general(left, right, (((1,), (1,)), ((), ())), preferred_element_type=F32)


def dot_tn(left, right):
    return lax.dot_general(left, right, (((0,), (0,)), ((), ())), preferred_element_type=F32)


def by_rows(x):
    return with_layout_constraint(x, Layout(major_to_minor=tuple(range(x.ndim))))


def row_scale(rows):
    return lax.rsqrt(jnp.mean(rows * rows, axis=-1, keepdims=True) + EPSILON)


def rotate(rows, cosine, sine):
    return rows * cosine + pltpu.roll(rows, HEAD_SIZE // 2, 1) * sine


def unrotate(rows, cosine, sine):
    return rows * cosine - pltpu.roll(rows, HEAD_SIZE // 2, 1) * sine


CHUNKS = 4


def first_kernel(
    pairs,
    span,
    tokens_ref,
    heads_ref,
    output_ref,
    gains_ref,
    facts_ref,
    tokens_out,
    heads_out,
    output_out,
    gains_out,
    facts_out,
    send_sems,
    recv_sems,
    local_sems,
):
    half = span // 2
    dp, t = lax.axis_index("dp"), lax.axis_index("tensor")
    p, c = dp // 2, lax.rem(dp, 2)
    q = t // half
    settled = c == q
    rows = tokens_ref.shape[0]
    piece = rows // CHUNKS
    shard = heads_ref.shape[0]
    small = gains_ref.shape[0]
    place = lambda pp, cc, tt: (pp * 2 + cc, tt)

    barrier = pltpu.get_barrier_semaphore()
    greeted = 0
    for k in range(1, 2 * span):
        pl.semaphore_signal(
            barrier,
            device_id=place(p, c ^ (k // span), t ^ (k % span)),
            device_id_type=pl.DeviceIdType.MESH,
        )
        greeted += 1
    for k in range(1, pairs):
        for cc in range(2):
            pl.semaphore_signal(
                barrier, device_id=place(p ^ k, c ^ cc, t), device_id_type=pl.DeviceIdType.MESH
            )
            greeted += 1
    pl.semaphore_wait(barrier, greeted)

    used = [0]

    def number(count=1):
        used[0] += count
        return used[0] - count

    def remote(src, dst, sem, to, arrival=None):
        return pltpu.make_async_remote_copy(
            src_ref=src,
            dst_ref=dst,
            send_sem=send_sems.at[sem],
            recv_sem=recv_sems.at[sem if arrival is None else arrival],
            device_id=to,
            device_id_type=pl.DeviceIdType.MESH,
        )

    def rows_of(i):
        return pl.ds(i * piece, piece)

    swap_sem = number(CHUNKS)
    line_sems = [[number() for _ in range(CHUNKS)] for _ in range(half)]
    side_sems = [[number() for _ in range(CHUNKS)] for _ in range(half)]
    near_sem, far_sem = number(), number(2)
    pair_sems = [number() for _ in range(pairs)]
    output_sems = [number() for _ in range(span)]
    gain_sems = [number() for _ in range(2 * pairs)]
    fact_sem = number()

    sibling = place(p, 1 - c, t)
    partner = place(p, 1 - c, span - 1 - t)
    swaps = [
        remote(tokens_ref.at[rows_of(i)], tokens_out.at[0, rows_of(i)], swap_sem + i, partner) for i in range(CHUNKS)
    ]
    own_rows = pl.ds(dp * shard, shard)
    far = lax.rem(t + half, span)
    near_copy = remote(heads_ref, heads_out.at[own_rows], near_sem, sibling)
    far_copy = remote(heads_ref, heads_out.at[own_rows], far_sem + c, place(p, q, far))
    local_tokens = pltpu.make_async_copy(tokens_ref, tokens_out.at[0], local_sems.at[0])
    local_heads = pltpu.make_async_copy(heads_ref, heads_out.at[own_rows], local_sems.at[1])
    local_output = pltpu.make_async_copy(output_ref, output_out.at[0], local_sems.at[2])
    local_gains = pltpu.make_async_copy(gains_ref, gains_out.at[pl.ds(dp * small, small)], local_sems.at[3])

    fact_copy = remote(facts_ref, facts_out, fact_sem, sibling)
    fact_copy.start()
    far_copy.start()

    @pl.when(settled)
    def _():
        local_heads.start()
        local_tokens.start()

    @pl.when(jnp.logical_not(settled))
    def _():
        near_copy.start()
        for copy in swaps:
            copy.start()

    gain_copies = []
    for k in range(1, 2 * pairs):
        to = (p ^ (k // 2), c ^ (k % 2))
        gain_copies.append(
            remote(gains_ref, gains_out.at[pl.ds(dp * small, small)], gain_sems[k], place(to[0], to[1], t))
        )
    local_gains.start()
    local_output.start()
    for copy in gain_copies:
        copy.start()

    def spread(i, source):
        copies = [remote(source, tokens_out.at[half, rows_of(i)], side_sems[0][i], sibling)]
        for k in range(1, half):
            copies.append(remote(source, tokens_out.at[k, rows_of(i)], line_sems[k][i], place(p, c, t ^ k)))
        return copies

    @pl.when(settled)
    def _():
        for i in range(CHUNKS):
            for copy in spread(i, tokens_ref.at[rows_of(i)]):
                copy.start()

    output_copies = [
        remote(output_ref, output_out.at[r], output_sems[r], place(p, c, t ^ r)) for r in range(1, span)
    ]

    @pl.when(settled)
    def _():
        local_heads.wait()
        near_copy.wait_recv()

    @pl.when(jnp.logical_not(settled))
    def _():
        near_copy.wait_send()
        for cc in range(2):
            remote(heads_ref, heads_out.at[own_rows], far_sem, sibling, far_sem + cc).wait_recv()

    both = heads_out.at[pl.ds(p * 2 * shard, 2 * shard)]
    pair_copies = [remote(both, both, pair_sems[k], place(p ^ k, c, t)) for k in range(1, pairs)]
    for copy in pair_copies:
        copy.start()

    @pl.when(jnp.logical_not(settled))
    def _():
        for i in range(CHUNKS):
            swaps[i].wait_recv()
            for copy in spread(i, tokens_out.at[0, rows_of(i)]):
                copy.start()

    for copy in output_copies:
        copy.start()

    forwards = []
    for i in range(CHUNKS):
        for k in range(1, half):
            block = tokens_out.at[k, rows_of(i)]
            remote(block, block, line_sems[k][i], sibling).wait_recv()
            copy = remote(block, tokens_out.at[half + k, rows_of(i)], side_sems[k][i], sibling)
            copy.start()
            forwards.append(copy)

    far_copy.wait_send()
    fact_copy.wait()
    local_output.wait()
    local_gains.wait()

    @pl.when(settled)
    def _():
        local_tokens.wait()

    @pl.when(jnp.logical_not(settled))
    def _():
        for copy in swaps:
            copy.wait_send()

    for i in range(CHUNKS):
        for index, copy in enumerate(spread(i, tokens_out.at[0, rows_of(i)])):
            copy.wait_send()
            if index == 0:
                copy.wait_recv()
    for copy in forwards + pair_copies + output_copies + gain_copies:
        copy.wait()


def first_transfers(pairs, span, tokens, heads, output, gains, facts):
    rows, width = tokens.shape
    shard = heads.shape[0]
    half = span // 2
    copies = CHUNKS * (1 + 2 * half) + 3 + pairs + span + 2 * pairs + 1
    any_ref = pl.BlockSpec(memory_space=pl.ANY)
    return pl.pallas_call(
        functools.partial(first_kernel, pairs, span),
        in_specs=[any_ref] * 5,
        out_specs=[any_ref] * 5,
        out_shape=[
            jax.ShapeDtypeStruct((span, rows, width), tokens.dtype),
            jax.ShapeDtypeStruct((2 * pairs * shard, heads.shape[1]), heads.dtype),
            jax.ShapeDtypeStruct((span, *output.shape), output.dtype),
            jax.ShapeDtypeStruct((2 * pairs * gains.shape[0], gains.shape[1]), gains.dtype),
            jax.ShapeDtypeStruct(facts.shape, facts.dtype),
        ],
        scratch_shapes=[
            pltpu.SemaphoreType.DMA((copies,)),
            pltpu.SemaphoreType.DMA((copies,)),
            pltpu.SemaphoreType.DMA((4,)),
        ],
        compiler_params=pltpu.CompilerParams(collective_id=0, has_side_effects=True),
        cost_estimate=pl.CostEstimate(flops=0, bytes_accessed=150_000_000, transcendentals=0),
        name="first_transfers",
    )(tokens, heads, output, gains, facts)


def sorting(places, first, count):
    index = first + lax.broadcasted_iota(jnp.int32, (count, places.shape[1]), 0)
    return jnp.where(places == index, 1.0, 0.0).astype(BF16)


def project_kernel(
    query_heads, key_heads, x_ref, places_ref, gain_ref, w_ref, gq_ref, gk_ref, cos_ref, sin_ref, normed_ref, qkv_ref, scale_ref
):
    x = dot_nn(sorting(places_ref[...], pl.program_id(0) * PROJECTED, PROJECTED), x_ref[...])
    normed = (x * row_scale(x) * gain_ref[...]).astype(BF16)
    normed_ref[...] = normed
    raw = dot_nn(normed, w_ref[...])
    cosine, sine = cos_ref[...], sin_ref[...]
    lane = lax.broadcasted_iota(jnp.int32, (x.shape[0], HEAD_SIZE), 1)
    scales = jnp.zeros((x.shape[0], HEAD_SIZE), F32)
    group = query_heads // key_heads
    for at in range(query_heads + 2 * key_heads):
        kv, kind = at // (group + 2), at % (group + 2)
        span = slice(at * HEAD_SIZE, (at + 1) * HEAD_SIZE)
        u = raw[:, span]
        if kind == group + 1:
            qkv_ref[:, span] = u.astype(BF16)
            continue
        r = row_scale(u)
        gain = gq_ref[...] if kind < group else gk_ref[...]
        qkv_ref[:, span] = rotate(u * r * gain, cosine, sine).astype(BF16)
        scales = jnp.where(lane == kind, r, scales) if kind else jnp.broadcast_to(r, scales.shape)
        if kind == group:
            scale_ref[kv] = scales


def project(x, places, gain, weights, gain_query, gain_key, cosine, sine, query_heads, key_heads):
    rows, width = x.shape
    wide = weights.shape[1]
    whole = lambda shape: pl.BlockSpec(shape, lambda i: (0, 0))
    block = lambda cols: pl.BlockSpec((PROJECTED, cols), lambda i: (i, 0))
    return pl.pallas_call(
        functools.partial(project_kernel, query_heads, key_heads),
        grid=(rows // PROJECTED,),
        in_specs=[
            pl.BlockSpec((rows, width), lambda i: (0, 0), pipeline_mode=pl.Buffered(1)),
            whole((1, rows)),
            whole((1, width)),
            whole((width, wide)),
            whole((1, HEAD_SIZE)),
            whole((1, HEAD_SIZE)),
            block(HEAD_SIZE),
            block(HEAD_SIZE),
        ],
        out_specs=[block(width), block(wide), pl.BlockSpec((key_heads, PROJECTED, HEAD_SIZE), lambda i: (0, i, 0))],
        out_shape=[
            jax.ShapeDtypeStruct((rows, width), BF16),
            jax.ShapeDtypeStruct((rows, wide), BF16),
            jax.ShapeDtypeStruct((key_heads, rows, HEAD_SIZE), F32),
        ],
        compiler_params=pltpu.CompilerParams(vmem_limit_bytes=VMEM_LIMIT),
        name="project",
    )(x, places, gain, weights, gain_query, gain_key, cosine, sine)


def first_place(info_ref, blocks, docs, places):
    start = jnp.zeros_like(places)
    for doc in range(docs):
        begin = info_ref[2 * blocks + doc]
        start = jnp.maximum(start, jnp.where(places >= begin, begin, 0))
    return start


def across(values, terms):
    ones = jnp.ones((8, HEAD_SIZE), BF16)
    total = None
    for _ in range(terms):
        part = values.astype(BF16)
        values = values - part.astype(F32)
        total = dot_nt(ones, part) if total is None else total + dot_nt(ones, part)
    return total


def keep_padded(pairs):
    for ref, kept in pairs:
        rows = ref.shape[0]
        kept[:rows, : ref.shape[1]] = ref[...]
        kept[rows:, : ref.shape[1]] = jnp.zeros((kept.shape[0] - rows, ref.shape[1]), BF16)


def forward_kernel(group, blocks, docs, info_ref, q_ref, k_ref, v_ref, o_ref, lse_ref, keys_s, wide_s, acc_ref):
    i = pl.program_id(1)

    @pl.when(i == 0)
    def _():
        keep_padded(((k_ref, keys_s), (v_ref, wide_s)))
        wide_s[:, HEAD_SIZE:] = jnp.ones((wide_s.shape[0], HEAD_SIZE), BF16)

    acc_ref[...] = jnp.zeros_like(acc_ref)
    places = i * BLOCK + lax.broadcasted_iota(jnp.int32, (BLOCK, 1), 0)
    start = first_place(info_ref, blocks, docs, places)
    low = info_ref[i]

    def step(m, carry):
        base = (low + m * (STEP // BLOCK)) * BLOCK
        rows = pl.ds(pl.multiple_of(base, BLOCK), STEP)
        keys, values = keys_s[rows, :], wide_s[rows, :]
        other = base + lax.broadcasted_iota(jnp.int32, (BLOCK, STEP), 1)
        keep = (other <= places) & (other >= start)
        scores = [dot_nt(q_ref[:, h * HEAD_SIZE : (h + 1) * HEAD_SIZE], keys) for h in range(group)]
        for h in range(group):
            weights = jnp.where(keep, jnp.exp2(scores[h] * (SCALE * LOG2E)), 0.0)
            acc_ref[h * BLOCK : (h + 1) * BLOCK, :] += dot_nn(weights.astype(BF16), values)
        return carry

    lax.fori_loop(0, (i - low) // (STEP // BLOCK) + 1, step, 0)
    total = acc_ref[:, HEAD_SIZE:]
    out = (acc_ref[:, :HEAD_SIZE] / total).astype(BF16)
    for h in range(group):
        o_ref[:, h * HEAD_SIZE : (h + 1) * HEAD_SIZE] = out[h * BLOCK : (h + 1) * BLOCK]
    lse_ref[0, 0] = across(jnp.log2(total) * (1.0 / HEAD_SIZE), 3)


def head_specs(rows, group, first):
    wide = group * HEAD_SIZE
    return [
        pl.BlockSpec((BLOCK, wide), lambda h, i, s: (i, (first + h) * (group + 2) // group)),
        pl.BlockSpec((rows, HEAD_SIZE), lambda h, i, s: (0, (first + h) * (group + 2) + group)),
        pl.BlockSpec((rows, HEAD_SIZE), lambda h, i, s: (0, (first + h) * (group + 2) + group + 1)),
    ]


def attention_forward(info, qkv, query_heads, key_heads, docs):
    rows = qkv.shape[0]
    blocks = rows // BLOCK
    group = query_heads // key_heads
    wide = group * HEAD_SIZE
    return pl.pallas_call(
        functools.partial(forward_kernel, group, blocks, docs),
        grid_spec=pltpu.PrefetchScalarGridSpec(
            num_scalar_prefetch=1,
            grid=(key_heads, blocks),
            in_specs=head_specs(rows, group, 0),
            out_specs=[
                pl.BlockSpec((BLOCK, wide), lambda h, i, s: (i, h)),
                pl.BlockSpec((1, 1, 8, group * BLOCK), lambda h, i, s: (h, i, 0, 0)),
            ],
            scratch_shapes=[
                pltpu.VMEM((rows + STEP, HEAD_SIZE), BF16),
                pltpu.VMEM((rows + STEP, 2 * HEAD_SIZE), BF16),
                pltpu.VMEM((group * BLOCK, 2 * HEAD_SIZE), F32),
            ],
        ),
        out_shape=[
            jax.ShapeDtypeStruct((rows, key_heads * wide), BF16),
            jax.ShapeDtypeStruct((key_heads, blocks, 8, group * BLOCK), F32),
        ],
        compiler_params=pltpu.CompilerParams(vmem_limit_bytes=VMEM_LIMIT),
        cost_estimate=pl.CostEstimate(flops=0, bytes_accessed=100_000_000, transcendentals=0),
        name="attention_forward",
    )(info, qkv, qkv, qkv)


def backward_kernel(
    group,
    blocks,
    docs,
    info_ref,
    q_ref,
    k_ref,
    v_ref,
    o_ref,
    do_ref,
    lse_ref,
    cos_ref,
    sin_ref,
    scale_ref,
    gq_ref,
    gk_ref,
    grad_ref,
    dgain_ref,
    dk_acc,
    dv_acc,
    dq_acc,
    keys_s,
    values_s,
):
    i = pl.program_id(1)
    rows_all = k_ref.shape[0]

    @pl.when(i == 0)
    def _():
        dk_acc[...] = jnp.zeros_like(dk_acc)
        dv_acc[...] = jnp.zeros_like(dv_acc)
        keep_padded(((k_ref, keys_s), (v_ref, values_s)))

    @pl.when(i == 0)
    def _():
        dgain_ref[...] = jnp.zeros_like(dgain_ref)

    def stacked(value):
        return jnp.concatenate([value[:, h * HEAD_SIZE : (h + 1) * HEAD_SIZE] for h in range(group)], axis=0)

    queries, grads = stacked(q_ref[...]), stacked(do_ref[...])
    delta = across(stacked(o_ref[...]).astype(F32) * grads.astype(F32), 2)[:1]
    lse = lse_ref[0, 0, :1]
    dq_acc[...] = jnp.zeros_like(dq_acc)
    places = i * BLOCK + lax.rem(lax.broadcasted_iota(jnp.int32, (1, group * BLOCK), 1), BLOCK)
    start = first_place(info_ref, blocks, docs, places)
    low = info_ref[i]

    def step(m, carry):
        base = (low + m * (STEP // BLOCK)) * BLOCK
        rows = pl.ds(pl.multiple_of(base, BLOCK), STEP)
        keys, values = keys_s[rows, :], values_s[rows, :]
        other = base + lax.broadcasted_iota(jnp.int32, (STEP, group * BLOCK), 0)
        keep = (other <= places) & (other >= start)
        probs = jnp.where(keep, jnp.exp2(dot_nt(keys, queries) * (SCALE * LOG2E) - lse), 0.0)
        score_grad = (probs * (dot_nt(values, grads) - delta)).astype(BF16)
        dv_acc[rows, :] += dot_nn(probs.astype(BF16), grads)
        dk_acc[rows, :] += dot_nn(score_grad, queries)
        dq_acc[...] += dot_tn(score_grad, keys)
        return carry

    lax.fori_loop(0, (i - low) // (STEP // BLOCK) + 1, step, 0)

    def raw_grad(grad, rotated, rows, kind, gain):
        cosine, sine = cos_ref[rows, :], sin_ref[rows, :]
        r = scale_ref[0, rows, kind : kind + 1]
        unit = unrotate(rotated.astype(F32), cosine, sine) * (1.0 / gain)
        back = unrotate(grad * SCALE, cosine, sine)
        scaled = back * gain
        raw = r * (scaled - unit * jnp.mean(scaled * unit, axis=1, keepdims=True))
        return raw.astype(BF16), jnp.sum(back * unit, axis=0, keepdims=True)

    here = pl.ds(pl.multiple_of(i * BLOCK, BLOCK), BLOCK)
    for h in range(group):
        span = slice(h * HEAD_SIZE, (h + 1) * HEAD_SIZE)
        raw, gain_grad = raw_grad(dq_acc[h * BLOCK : (h + 1) * BLOCK, :], q_ref[:, span], here, h, gq_ref[...])
        grad_ref[here, span] = raw
        dgain_ref[0:1, :] += gain_grad

    @pl.when(i == blocks - 1)
    def _():
        grad_ref[:, (group + 1) * HEAD_SIZE :] = dv_acc[:rows_all, :].astype(BF16)

        def finish(b, carry):
            rows = pl.ds(pl.multiple_of(b * BLOCK, BLOCK), BLOCK)
            raw, gain_grad = raw_grad(dk_acc[rows, :], k_ref[rows, :], rows, group, gk_ref[...])
            grad_ref[rows, group * HEAD_SIZE : (group + 1) * HEAD_SIZE] = raw
            dgain_ref[1:2, :] += gain_grad
            return carry

        lax.fori_loop(0, blocks, finish, 0)


def attention_backward(
    info, qkv, attended, grads, lse, cosine, sine, scales, gain_query, gain_key, query_heads, key_heads, docs, kv
):
    rows = qkv.shape[0]
    blocks = rows // BLOCK
    group = query_heads // key_heads
    wide = group * HEAD_SIZE
    own = pl.BlockSpec((BLOCK, wide), lambda h, i, s: (i, kv))
    whole = lambda shape: pl.BlockSpec(shape, lambda h, i, s: (0, 0), pipeline_mode=pl.Buffered(1))
    return pl.pallas_call(
        functools.partial(backward_kernel, group, blocks, docs),
        grid_spec=pltpu.PrefetchScalarGridSpec(
            num_scalar_prefetch=1,
            grid=(1, blocks),
            in_specs=[
                *head_specs(rows, group, kv),
                own,
                own,
                pl.BlockSpec((1, 1, 8, group * BLOCK), lambda h, i, s: (kv, i, 0, 0)),
                whole((rows, HEAD_SIZE)),
                whole((rows, HEAD_SIZE)),
                pl.BlockSpec((1, rows, HEAD_SIZE), lambda h, i, s: (kv, 0, 0), pipeline_mode=pl.Buffered(1)),
                whole((1, HEAD_SIZE)),
                whole((1, HEAD_SIZE)),
            ],
            out_specs=[
                whole((rows, wide + 2 * HEAD_SIZE)),
                pl.BlockSpec((8, HEAD_SIZE), lambda h, i, s: (0, 0)),
            ],
            scratch_shapes=[
                pltpu.VMEM((rows + STEP, HEAD_SIZE), F32),
                pltpu.VMEM((rows + STEP, HEAD_SIZE), F32),
                pltpu.VMEM((group * BLOCK, HEAD_SIZE), F32),
                pltpu.VMEM((rows + STEP, HEAD_SIZE), BF16),
                pltpu.VMEM((rows + STEP, HEAD_SIZE), BF16),
            ],
        ),
        out_shape=[
            jax.ShapeDtypeStruct((rows, wide + 2 * HEAD_SIZE), BF16),
            jax.ShapeDtypeStruct((8, HEAD_SIZE), F32),
        ],
        compiler_params=pltpu.CompilerParams(vmem_limit_bytes=VMEM_LIMIT),
        cost_estimate=pl.CostEstimate(flops=0, bytes_accessed=100_000_000, transcendentals=0),
        name="attention_backward",
    )(info, qkv, qkv, qkv, attended, grads, lse, cosine, sine, scales, gain_query, gain_key)


def wide_block(ref):
    value = ref[...]
    return value.reshape(value.shape[0] * value.shape[2], value.shape[3])


def group_places(span):
    half = span // 2
    dp, t = lax.axis_index("dp"), lax.axis_index("tensor")
    p, c = dp // 2, lax.rem(dp, 2)
    aside = jnp.where(c == t // half, 0, 1)

    def place(k):
        return (p * 2 + (c ^ (k // half)), t ^ (k % half))

    def chunk(k):
        return ((k // half) ^ aside) * half + k % half

    return place, chunk


def group_barrier(span, place, *others):
    barrier = pltpu.get_barrier_semaphore()
    for to in [place(k) for k in range(1, span)] + list(others):
        pl.semaphore_signal(barrier, device_id=to, device_id_type=pl.DeviceIdType.MESH)
    pl.semaphore_wait(barrier, span - 1 + len(others))


def remote_copy(src, dst, send_sem, recv_sem, to):
    return pltpu.make_async_remote_copy(
        src_ref=src,
        dst_ref=dst,
        send_sem=send_sem,
        recv_sem=recv_sem,
        device_id=to,
        device_id_type=pl.DeviceIdType.MESH,
    )


def arrival_order(span):
    half = span // 2
    return [0, half] + [k for k in range(1, span) if k != half]


def output_kernel(
    span,
    heads_ref,
    places_ref,
    w_hbm,
    tokens_ref,
    gain_ref,
    middle_ref,
    normed_ref,
    mixed_ref,
    w_ref,
    out_s,
    send_sems,
    recv_sems,
    local_sem,
):
    place, chunk = group_places(span)
    rows, width = tokens_ref.shape
    load = pltpu.make_async_copy(w_hbm, w_ref, local_sem)
    load.start()
    group_barrier(span, place)
    copies = {}
    index = lax.broadcasted_iota(jnp.int32, (rows, heads_ref.shape[0]), 1)
    for k in reversed(arrival_order(span)):
        picks = jnp.where(places_ref[k * rows : (k + 1) * rows, :] == index, 1.0, 0.0).astype(BF16)
        block = dot_nn(picks, heads_ref[...]).astype(BF16)
        if k:
            out_s[k] = block
            copies[k] = remote_copy(out_s.at[k], mixed_ref.at[k], send_sems.at[k], recv_sems.at[k], place(k))
            copies[k].start()
        else:
            mixed_ref[0] = block
    middle_ref[...] = tokens_ref[...].astype(F32)
    load.wait()
    for k in arrival_order(span):
        if k:
            copies[k].wait_recv()
        weights = w_ref[:, chunk(k)].reshape(width, w_ref.shape[3])
        middle_ref[...] += dot_nt(mixed_ref[k], weights)
    middle = middle_ref[...]
    normed_ref[...] = (middle * row_scale(middle) * gain_ref[...]).astype(BF16)
    for k in range(1, span):
        copies[k].wait_send()


def output_project(heads, places, weights, tokens, gain):
    devices, span, shard, cols = weights.shape
    rows, width = tokens.shape
    any_ref = pl.BlockSpec(memory_space=pl.ANY)
    local_ref = pl.BlockSpec(memory_space=pltpu.VMEM)
    return pl.pallas_call(
        functools.partial(output_kernel, span),
        in_specs=[local_ref] * 2 + [any_ref] + [local_ref] * 2,
        out_specs=[local_ref] * 3,
        out_shape=[
            jax.ShapeDtypeStruct((rows, width), F32),
            jax.ShapeDtypeStruct((rows, width), BF16),
            jax.ShapeDtypeStruct((span, rows, cols), BF16),
        ],
        scratch_shapes=[
            pltpu.VMEM(weights.shape, BF16),
            pltpu.VMEM((span, rows, cols), BF16),
            pltpu.SemaphoreType.DMA((span,)),
            pltpu.SemaphoreType.DMA((span,)),
            pltpu.SemaphoreType.DMA,
        ],
        compiler_params=pltpu.CompilerParams(
            collective_id=1, has_side_effects=True, vmem_limit_bytes=VMEM_LIMIT
        ),
        cost_estimate=pl.CostEstimate(flops=0, bytes_accessed=100_000_000, transcendentals=0),
        name="output_project",
    )(heads, places, weights, tokens, gain)


def output_back_kernel(
    span,
    b_ref,
    mixed_ref,
    places_ref,
    w_hbm,
    feed_hbm,
    out_ref,
    dw_hbm,
    w_ref,
    grad_s,
    in_s,
    dw_ref,
    bt_ref,
    send_sems,
    recv_sems,
    local_sems,
):
    place, chunk = group_places(span)
    rows, width = b_ref.shape
    cols = w_ref.shape[3]
    load = pltpu.make_async_copy(w_hbm, w_ref, local_sems.at[span])
    load.start()
    group_barrier(span, place)
    load.wait()
    copies = {}
    for k in reversed(arrival_order(span)):
        block = dot_nn(b_ref[...], w_ref[:, chunk(k)].reshape(width, cols)).astype(BF16)
        if k:
            grad_s[k] = block
            copies[k] = remote_copy(grad_s.at[k], in_s.at[k], send_sems.at[k], recv_sems.at[k], place(k))
            copies[k].start()
        else:
            in_s[0] = block
    bt_ref[...] = b_ref[...].T
    stores = []
    base = dw_hbm.shape[3] - span * cols
    for k in range(span):
        dw_ref[k] = dot_nn(bt_ref[...], mixed_ref[k]).astype(BF16).reshape(dw_ref.shape[1:])
        to = pl.ds(pl.multiple_of(base + chunk(k) * cols, 128), cols)
        stores.append(pltpu.make_async_copy(dw_ref.at[k], dw_hbm.at[:, 0, :, to], local_sems.at[k]))
        stores[-1].start()
    for k in arrival_order(span):
        if k:
            copies[k].wait_recv()

        def sort_step(m, carry, k=k):
            at = pl.ds(pl.multiple_of(m * rows, rows), rows)
            block = dot_nn(sorting(places_ref[k], m * rows, rows), in_s[k]).astype(BF16)
            if k:
                out_ref[at, :] += block
            else:
                out_ref[at, :] = block
            return carry

        lax.fori_loop(0, span, sort_step, 0)
    for copy in stores:
        copy.wait()
    for copy in copies.values():
        copy.wait_send()


def output_back(branch, mixed, places, weights, feed_grads):
    devices, span, shard, cols = weights.shape
    rows, width = branch.shape
    any_ref = pl.BlockSpec(memory_space=pl.ANY)
    local_ref = pl.BlockSpec(memory_space=pltpu.VMEM)
    return pl.pallas_call(
        functools.partial(output_back_kernel, span),
        in_specs=[local_ref, local_ref, local_ref, any_ref, any_ref],
        out_specs=[local_ref, any_ref],
        input_output_aliases={4: 1},
        out_shape=[
            jax.ShapeDtypeStruct((span * rows, cols), BF16),
            jax.ShapeDtypeStruct(feed_grads.shape, BF16),
        ],
        scratch_shapes=[
            pltpu.VMEM(weights.shape, BF16),
            pltpu.VMEM((span, rows, cols), BF16),
            pltpu.VMEM((span, rows, cols), BF16),
            pltpu.VMEM((span, devices, shard, cols), BF16),
            pltpu.VMEM((width, rows), BF16),
            pltpu.SemaphoreType.DMA((span,)),
            pltpu.SemaphoreType.DMA((span,)),
            pltpu.SemaphoreType.DMA((span + 1,)),
        ],
        compiler_params=pltpu.CompilerParams(
            collective_id=2, has_side_effects=True, vmem_limit_bytes=VMEM_LIMIT
        ),
        cost_estimate=pl.CostEstimate(flops=0, bytes_accessed=100_000_000, transcendentals=0),
        name="output_back",
    )(branch, mixed, places, weights, feed_grads)


def feed_kernel(last, x_ref, c_ref, w_ref, *refs):
    if last:
        (out_in, ng_in, middle_ref, gain_ref, result_ref, grad_ref, branch_ref, dgain_ref, dw_ref, out_s, ng_s) = refs[:11]
        act_s, gg_s, ug_s, xt_s, ct_s = refs[11:]
    else:
        out_s, ng_s, dw_ref, act_s, gg_s, ug_s, xt_s, ct_s = refs
    j = pl.program_id(0)
    rows_all, width = x_ref.shape
    hidden = act_s.shape[1]
    devices, _, shard, _ = w_ref.shape
    chunk = rows_all

    @pl.when(j == 0)
    def _():
        xt_s[...] = x_ref[...].T
        ct_s[...] = c_ref[...].T
        out_s[...] = out_in[...] if last else jnp.zeros_like(out_s)
        ng_s[...] = ng_in[...] if last else jnp.zeros_like(ng_s)

    def part(k):
        return w_ref[:, 0, :, k * hidden : (k + 1) * hidden].reshape(width, hidden)

    def rows_step(m, carry):
        rows = pl.ds(pl.multiple_of(m * chunk, chunk), chunk)
        gate = dot_nn(x_ref[rows, :], part(0))
        upward = dot_nn(x_ref[rows, :], part(1))
        act_grad = dot_nn(c_ref[rows, :], part(2))
        sig = 1.0 / (1.0 + jnp.exp(-gate))
        silu = gate * sig
        act = (silu * upward).astype(BF16)
        up_grad = (act_grad * silu).astype(BF16)
        gate_grad = (act_grad * upward * sig * (1.0 + gate * (1.0 - sig))).astype(BF16)
        act_s[rows, :] = act
        ug_s[rows, :] = up_grad
        gg_s[rows, :] = gate_grad
        out_s[rows, :] += dot_nt(act, part(2))
        ng_s[rows, :] += dot_nt(gate_grad, part(0)) + dot_nt(up_grad, part(1))
        return carry

    lax.fori_loop(0, rows_all // chunk, rows_step, 0)

    group = ROWS // shard

    def grad_step(m, carry):
        rows = pl.ds(pl.multiple_of(m * ROWS, ROWS), ROWS)
        to = pl.ds(m * group, group)
        for k, left, right in ((0, xt_s, gg_s), (1, xt_s, ug_s), (2, ct_s, act_s)):
            value = dot_nn(left[rows, :], right[...]).astype(BF16)
            dw_ref[to, 0, :, k * hidden : (k + 1) * hidden] = value.reshape(group, shard, hidden)
        return carry

    lax.fori_loop(0, width // ROWS, grad_step, 0)

    if not last:
        return

    @pl.when(j == pl.num_programs(0) - 1)
    def _():
        middle = middle_ref[...]
        result_ref[...] = (middle + out_s[...]).astype(BF16)
        r = row_scale(middle)
        unit = middle * r
        dgain_ref[...] = jnp.broadcast_to(jnp.sum(ng_s[...] * unit, axis=0, keepdims=True), dgain_ref.shape)
        scaled = ng_s[...] * gain_ref[...]
        grad = c_ref[...].astype(F32) + r * (scaled - unit * jnp.mean(scaled * unit, axis=-1, keepdims=True))
        grad_ref[...] = grad
        branch_ref[...] = grad.astype(BF16)


def feed(x, cot, weights, *rest, room=0):
    rows, width = x.shape
    devices, span, shard, cols = weights.shape
    hidden = cols // 3
    last = len(rest) > 0
    whole = lambda shape: pl.BlockSpec(shape, lambda j: (0, 0), pipeline_mode=pl.Buffered(1))
    chunk = pl.BlockSpec((devices, 1, shard, cols), lambda j: (0, j, 0, 0))
    full = whole((rows, width))
    grads = jax.ShapeDtypeStruct((devices, span, shard, cols + room), BF16)
    shape = lambda kind: jax.ShapeDtypeStruct((rows, width), kind)
    sums = [pltpu.VMEM((rows, width), F32)] * 2 if last else []
    return pl.pallas_call(
        functools.partial(feed_kernel, last),
        grid=(span,),
        in_specs=[full, full, chunk] + ([full, full, full, whole((1, width))] if last else []),
        out_specs=[full, full, full, whole((8, width)), chunk] if last else [full, full, chunk],
        out_shape=[shape(BF16), shape(F32), shape(BF16), jax.ShapeDtypeStruct((8, width), F32), grads]
        if last
        else [shape(F32), shape(F32), grads],
        scratch_shapes=sums + [pltpu.VMEM((rows, hidden), BF16)] * 3 + [pltpu.VMEM((width, rows), BF16)] * 2,
        compiler_params=pltpu.CompilerParams(vmem_limit_bytes=VMEM_LIMIT),
        name="feed_forward",
    )(x, cot, weights, *rest)


def last_kernel(
    pairs,
    span,
    count,
    *refs,
):
    grads_hbm, sorted_hbm = refs[:count], refs[count : 2 * count]
    last_body(pairs, span, grads_hbm, sorted_hbm, *refs[2 * count :])


def last_body(
    pairs,
    span,
    grads_hbm,
    sorted_hbm,
    normed_hbm,
    w_ref,
    middle_ref,
    tokens_ref,
    gain_ref,
    gains_ref,
    output_ref,
    rows_out,
    heads_out,
    gains_out,
    output_out,
    grads,
    sorted_s,
    normed_s,
    turned,
    mine,
    theirs,
    from_sibling,
    from_line,
    heads_s,
    heads_in,
    far_in,
    far_s,
    near_in,
    near_s,
    final_s,
    pass_s,
    far_pass,
    wt_s,
    gains_one,
    gains_two,
    gains_s,
    send_sems,
    recv_sems,
    local_sems,
):
    half = span // 2
    dp, t = lax.axis_index("dp"), lax.axis_index("tensor")
    p, c = dp // 2, lax.rem(dp, 2)
    settled = c == t // half
    rows, width = middle_ref.shape
    shard, parts = output_ref.shape[0], output_out.shape[2]
    base = output_ref.shape[1] - span * parts
    place = lambda pp, cc, tt: (pp * 2 + cc, tt)
    sibling = place(p, 1 - c, t)
    used = [0]

    def copy_to(src, dst, to):
        used[0] += 1
        at = used[0] - 1
        return remote_copy(src, dst, send_sems.at[at], recv_sems.at[at], to)

    count = len(grads_hbm)
    wide = grads_hbm[0].shape[1]

    def side_by_side(sources, rows_of, dst, sem):
        return [
            pltpu.make_async_copy(src.at[rows_of], dst.at[:, pl.ds(h * wide, wide)], local_sems.at[sem + h])
            for h, src in enumerate(sources)
        ]

    loads = [side_by_side(grads_hbm, pl.ds(k * rows, rows), grads.at[k], k * count) for k in range(span)]
    order = list(range(half + 1, span)) + list(range(1, half)) + [half, 0]
    for k in order:
        for load in loads[k]:
            load.start()
    more = [pltpu.make_async_copy(normed_hbm, normed_s, local_sems.at[span * count])]
    more += side_by_side(sorted_hbm, pl.ds(0, span * rows), sorted_s, span * count + 1)
    for load in more:
        load.start()

    barrier = pltpu.get_barrier_semaphore()
    greeted = 0
    for k in range(1, 2 * span):
        pl.semaphore_signal(
            barrier, device_id=place(p, c ^ (k // span), t ^ (k % span)), device_id_type=pl.DeviceIdType.MESH
        )
        greeted += 1
    for k in range(1, pairs):
        pl.semaphore_signal(barrier, device_id=place(p ^ k, c, t), device_id_type=pl.DeviceIdType.MESH)
        greeted += 1
    pl.semaphore_wait(barrier, greeted)

    wt_s[...] = w_ref[...].T
    outputs = [
        copy_to(output_ref.at[:, pl.ds(base + r * parts, parts)], output_out.at[r - 1], place(p, c, t ^ r))
        for r in range(1, span)
    ]

    piece = rows // 2

    def multiply(k, dst, slot):
        def step(m, carry):
            at = pl.ds(pl.multiple_of(m * piece, piece), piece)
            dst[slot, at, :] = dot_nn(grads[k, at, :], wt_s[...]).astype(BF16)
            return carry

        lax.fori_loop(0, 2, step, 0)

    sides, hops = {}, {}
    away = list(range(1, half))

    def product_for_sibling(k):
        for load in loads[half + k]:
            load.wait()
        multiply(half + k, theirs, k)
        sides[k] = copy_to(theirs.at[k], from_sibling.at[k], sibling)
        sides[k].start()

    def own_sum(k):
        for load in loads[k]:
            load.wait()
        multiply(k, mine, k)
        sides[k].wait_recv()
        mine[k] = (mine[k].astype(F32) + from_sibling[k].astype(F32)).astype(BF16)

    for k in away:
        product_for_sibling(k)
    for k in away:
        own_sum(k)
        for m in range(2):
            at = pl.ds(m * piece, piece)
            hops[k, m] = copy_to(mine.at[k, at], from_line.at[k - 1, at], place(p, c, t ^ k))
            hops[k, m].start()
    product_for_sibling(0)
    own_sum(0)
    for load in more:
        load.wait()
    turned[...] = normed_s[...].T
    block = 2 * shard

    def weights_step(m, carry):
        at = pl.ds(pl.multiple_of(m * block, block), block)
        heads_s[at, :] = dot_nn(turned[at, :], sorted_s[...]).astype(BF16)
        return carry

    lax.fori_loop(0, pairs, weights_step, 0)
    heads_copies = []
    for k in range(1, pairs):
        there = pl.ds((p ^ k) * block, block)
        heads_copies.append(copy_to(heads_s.at[there], heads_in.at[k - 1], place(p ^ k, c, t)))
        heads_copies[-1].start()

    for copy in outputs:
        copy.start()

    swaps = []
    gain_sum = jnp.zeros((1, width), F32)
    for m in range(2):
        at = pl.ds(m * piece, piece)
        for k in range(1, half):
            hops[k, m].wait_recv()
        grad = mine[0, at, :].astype(F32)
        for k in range(1, half):
            grad = grad + from_line[k - 1, at, :].astype(F32)
        inputs = tokens_ref[at, :].astype(F32)
        r = row_scale(inputs)
        unit = inputs * r
        gain_sum = gain_sum + jnp.sum(grad * unit, axis=0, keepdims=True)
        scaled = grad * gain_ref[...]
        final_s[at, :] = (
            middle_ref[at, :] + r * (scaled - unit * jnp.mean(scaled * unit, axis=-1, keepdims=True))
        ).astype(BF16)
        there = place(p, 1 - c, span - 1 - t)
        swap = copy_to(final_s.at[at], rows_out.at[at] if m == 0 else pass_s, there if m == 0 else sibling)
        keep = pltpu.make_async_copy(final_s.at[at], rows_out.at[at], local_sems.at[(span + 1) * count + 1 + m])
        swaps.append((swap, keep))

        @pl.when(settled)
        def _():
            keep.start()

        @pl.when(jnp.logical_not(settled))
        def _():
            swap.start()

    gains_s[...] = gains_ref[...]
    gains_s[0:1, :] = gain_sum
    first_gains = [
        copy_to(gains_s, gains_one.at[k - 1], place(p, c ^ (k // span), t ^ (k % span))) for k in range(1, 2 * span)
    ]
    for copy in first_gains:
        copy.start()

    at = pl.ds(piece, piece)
    handed = swaps[1][0]
    passed = copy_to(pass_s, rows_out.at[at], place(p, c, span - 1 - t))

    @pl.when(settled)
    def _():
        handed.wait_recv()
        passed.start()

    for copy in heads_copies:
        copy.wait_recv()
    summed = heads_s[pl.ds(p * block, block), :].astype(F32)
    for k in range(1, pairs):
        summed = summed + heads_in[k - 1].astype(F32)
    far_s[...] = summed.astype(BF16)
    side = copy_to(far_s, far_pass, sibling)
    far = copy_to(far_pass, far_in, place(p, 1 - c, lax.rem(t + half, span)))
    near = copy_to(near_s, near_in, sibling)

    @pl.when(jnp.logical_not(settled))
    def _():
        side.start()

    for copy in first_gains:
        copy.wait_recv()
    total = gains_s[...]
    for k in range(1, 2 * span):
        total = total + gains_one[k - 1]
    gains_out[...] = total
    @pl.when(settled)
    def _():
        side.wait_recv()
        far.start()

    second_gains = [copy_to(gains_out, gains_two.at[k - 1], place(p ^ k, c, t)) for k in range(1, pairs)]
    for copy in second_gains:
        copy.start()

    for copy in second_gains:
        copy.wait()
    for copy in first_gains:
        copy.wait_send()
    whole = gains_out[...]
    for k in range(1, pairs):
        whole = whole + gains_two[k - 1]
    gains_out[...] = whole

    @pl.when(settled)
    def _():
        far.wait_recv()
        own = pl.ds(c * shard, shard)
        other = pl.ds((1 - c) * shard, shard)
        near_s[...] = (far_s[other, :].astype(F32) + far_in[other, :].astype(F32)).astype(BF16)
        near.start()
        far.wait_send()
        heads_out[...] = far_s[own, :].astype(F32) + far_in[own, :].astype(F32)
        near.wait_send()

    @pl.when(jnp.logical_not(settled))
    def _():
        side.wait_send()
        near.wait_recv()
        heads_out[...] = near_in[...].astype(F32)

    for copy in list(sides.values()) + list(hops.values()) + heads_copies:
        copy.wait_send()
    for copy in outputs:
        copy.wait()
    @pl.when(settled)
    def _():
        for swap, keep in swaps:
            keep.wait()
        passed.wait_send()

    @pl.when(jnp.logical_not(settled))
    def _():
        for swap, keep in swaps:
            swap.wait_send()
        swaps[0][0].wait_recv()
        passed.wait_recv()


def last_transfers(pairs, span, grads, grads_sorted, normed, weights, middle_grad, tokens, gain, gains, output, parts):
    rows, width = tokens.shape
    half = span // 2
    shard = output.shape[0]
    cols = weights.shape[1]
    count = len(grads)
    any_ref = pl.BlockSpec(memory_space=pl.ANY)
    local_ref = pl.BlockSpec(memory_space=pltpu.VMEM)
    copies = span - 1 + half + 2 * (half - 1) + 2 * (pairs - 1) + 2 + 2 * span - 1 + 4
    return pl.pallas_call(
        functools.partial(last_kernel, pairs, span, count),
        in_specs=[any_ref] * (2 * count + 1) + [local_ref] * 5 + [any_ref],
        out_specs=[any_ref, local_ref, local_ref, any_ref],
        out_shape=[
            jax.ShapeDtypeStruct((rows, width), BF16),
            jax.ShapeDtypeStruct((shard, cols), F32),
            jax.ShapeDtypeStruct((8, width), F32),
            jax.ShapeDtypeStruct((span - 1, shard, parts), BF16),
        ],
        scratch_shapes=[
            pltpu.VMEM((span, rows, cols), BF16),
            pltpu.VMEM((span * rows, cols), BF16),
            pltpu.VMEM((span * rows, width), BF16),
            pltpu.VMEM((width, span * rows), BF16),
            pltpu.VMEM((half, rows, width), BF16),
            pltpu.VMEM((half, rows, width), BF16),
            pltpu.VMEM((half, rows, width), BF16),
            pltpu.VMEM((max(half - 1, 1), rows, width), BF16),
            pltpu.VMEM((width, cols), BF16),
            pltpu.VMEM((pairs - 1, 2 * shard, cols), BF16),
            pltpu.VMEM((2 * shard, cols), BF16),
            pltpu.VMEM((2 * shard, cols), BF16),
            pltpu.VMEM((shard, cols), BF16),
            pltpu.VMEM((shard, cols), BF16),
            pltpu.VMEM((rows, width), BF16),
            pltpu.VMEM((rows // 2, width), BF16),
            pltpu.VMEM((2 * shard, cols), BF16),
            pltpu.VMEM((cols, width), BF16),
            pltpu.VMEM((2 * span - 1, 8, width), F32),
            pltpu.VMEM((pairs - 1, 8, width), F32),
            pltpu.VMEM((8, width), F32),
            pltpu.SemaphoreType.DMA((copies,)),
            pltpu.SemaphoreType.DMA((copies,)),
            pltpu.SemaphoreType.DMA(((span + 1) * count + 3,)),
        ],
        compiler_params=pltpu.CompilerParams(
            collective_id=3, has_side_effects=True, vmem_limit_bytes=VMEM_LIMIT
        ),
        name="last_transfers",
    )(*grads, *grads_sorted, normed, weights, middle_grad, tokens, gain, gains, output)


def finish_kernel(lines, span, key_heads, both_ref, *refs):
    line_refs = refs[:lines]
    output_ref, heads_ref, q_ref, k_ref, v_ref, o_ref, gate_ref, up_ref, down_ref = refs[lines:]
    hidden = gate_ref.shape[1]
    cols = o_ref.shape[0]

    def part(k):
        at = slice(k * hidden, (k + 1) * hidden)
        total = both_ref[:, at].astype(F32)
        for ref in line_refs:
            total = total + ref[:, at].astype(F32)
        return total

    gate_ref[...] = part(0)
    up_ref[...] = part(1)
    down_ref[...] = part(2).T
    total = both_ref[:, 3 * hidden : 3 * hidden + cols].astype(F32)
    for r in range(span - 1):
        total = total + output_ref[r].astype(F32)
    o_ref[...] = total.T
    query, key = q_ref.shape[1] // key_heads, k_ref.shape[1] // key_heads
    for kv in range(key_heads):
        at = kv * (query + 2 * key)
        q_ref[:, kv * query : (kv + 1) * query] = heads_ref[:, at : at + query]
        k_ref[:, kv * key : (kv + 1) * key] = heads_ref[:, at + query : at + query + key]
        v_ref[:, kv * key : (kv + 1) * key] = heads_ref[:, at + query + key : at + query + 2 * key]


def finish(both, lines, output, heads, shapes, span, key_heads):
    return pl.pallas_call(
        functools.partial(finish_kernel, len(lines), span, key_heads),
        out_shape=[jax.ShapeDtypeStruct(shape, F32) for shape in shapes],
        compiler_params=pltpu.CompilerParams(vmem_limit_bytes=VMEM_LIMIT),
        name="finish",
    )(both, *lines, output, heads)


def local(
    tokens,
    lengths,
    row_order,
    attention_gain,
    query_gain,
    key_gain,
    query_weight,
    key_matrix,
    value_matrix,
    output_weight,
    feedforward_gain,
    gate_weight,
    up_weight,
    down_weight,
    cotangent,
):
    span = lax.axis_size("tensor")
    pairs = lax.axis_size("dp") // 2
    half = span // 2
    rows, width = tokens.shape
    group_rows = rows * span
    blocks = group_rows // BLOCK
    docs = lengths.shape[1]
    query_heads = query_weight.shape[1] // HEAD_SIZE
    key_heads = key_matrix.shape[1] // HEAD_SIZE
    head_columns = query_weight.shape[1]
    hidden_columns = gate_weight.shape[1]
    shard = query_weight.shape[0]

    dp, t = lax.axis_index("dp"), lax.axis_index("tensor")
    p, c = dp // 2, lax.rem(dp, 2)
    q = t // half
    settled = c == q

    def send(x, route):
        moves = []
        for pp in range(pairs):
            for cc in range(2):
                for tt in range(span):
                    to = route(pp, cc, tt)
                    if to is not None:
                        moves.append(((pp * 2 + cc) * span + tt, (to[0] * 2 + to[1]) * span + to[2]))
        return lax.ppermute(x, AXES, moves)

    def swap(x):
        moved = send(x, lambda pp, cc, tt: (pp, 1 - cc, span - 1 - tt) if cc != tt // half else None)
        return jnp.where(settled, x, moved)

    never = row_order[0, 0] < 0

    def behind(x, other):
        return jnp.where(never, other[0, 0].astype(x.dtype), x)

    def line(x, steps):
        return [send(x, lambda pp, cc, tt: (pp, cc, tt ^ r)) for r in steps]

    def gather_wide(pieces):
        cols = pieces[0].shape[1]
        out = by_rows(lax.all_gather(by_rows(jnp.concatenate(pieces, axis=0)), "dp", axis=0, tiled=True))
        return out.reshape(2 * pairs, len(pieces), shard, cols)

    def scatter_wide(grads):
        devices, count, _, cols = grads.shape
        out = by_rows(grads.reshape(devices * count * shard, cols))
        out = by_rows(lax.psum_scatter(out, "dp", scatter_dimension=0, tiled=True))
        return [out[r * shard : (r + 1) * shard] for r in range(count)]

    per_query, per_key = head_columns // key_heads, HEAD_SIZE
    heads_local = []
    for kv in range(key_heads):
        heads_local.append(query_weight[:, kv * per_query : (kv + 1) * per_query])
        heads_local.append(key_matrix[:, kv * per_key : (kv + 1) * per_key])
        heads_local.append(value_matrix[:, kv * per_key : (kv + 1) * per_key])
    heads_local = by_rows(jnp.concatenate(heads_local, axis=1))
    feed_local = by_rows(jnp.concatenate([gate_weight, up_weight, down_weight.T], axis=1))
    gains = jnp.concatenate([attention_gain, query_gain, key_gain, feedforward_gain])
    small, tiny = attention_gain.shape[0], query_gain.shape[0]
    few, lanes = gains.shape[0], -(-gains.shape[0] // 128) * 128
    gains = jnp.broadcast_to(jnp.pad(gains, (0, lanes - few))[None], (16, lanes))
    facts = jnp.concatenate([row_order[0], lengths[0]])
    fact_rows = -(-facts.shape[0] // 1024) * 8
    facts = jnp.pad(facts, (0, fact_rows * 128 - facts.shape[0])).reshape(fact_rows, 128)
    tokens_all, heads_weights, output_line, gains, facts_moved = first_transfers(
        pairs, span, tokens, heads_local, by_rows(output_weight.T), gains, facts
    )
    swapped = tokens_all[0]
    tokens_all = tokens_all.reshape(group_rows, width)
    own_weights = gather_wide([feed_local])
    output_weights = gather_wide([output_line[r] for r in range(span)])
    feed_line = line(behind(feed_local, swapped), range(1, span))

    gains = gains.reshape(2 * pairs, 16, lanes)[:, 0, :few].astype(F32)
    gain_one = gains[:, :small].reshape(1, width)
    gain_query = gains[:, small : small + tiny].reshape(1, HEAD_SIZE)
    gain_key = gains[:, small + tiny : small + 2 * tiny].reshape(1, HEAD_SIZE)
    gain_two = gains[:, small + 2 * tiny : small + 2 * tiny + small].reshape(1, width)
    facts = jnp.where(settled, facts, facts_moved).reshape(-1)[: group_rows + docs]
    order, length = facts[:group_rows].reshape(span, rows), facts[group_rows:]
    places = []
    for k in range(span):
        tt, cc = t ^ (k % half), c ^ (k // half)
        places.append(lax.dynamic_index_in_dim(order, jnp.where(cc == tt // half, tt, span - 1 - tt), 0, False))
    places = jnp.concatenate(places)
    before = jnp.arange(docs)[None, :] < jnp.arange(docs)[:, None]
    starts = jnp.sum(jnp.where(before, length[None, :], 0), axis=1).astype(jnp.int32)

    def start_of(place):
        return jnp.max(jnp.where(place[:, None] >= starts[None, :], starts[None, :], 0), axis=1)

    index = jnp.arange(blocks, dtype=jnp.int32) * BLOCK
    low = start_of(index) // BLOCK
    clear = (start_of(index + BLOCK - 1) + BLOCK - 1) // BLOCK
    info = jnp.concatenate([low, clear, starts]).astype(jnp.int32)
    rate = np.float32(THETA) ** (-(np.arange(HEAD_SIZE // 2, dtype=np.float32) * np.float32(2.0) / HEAD_SIZE))
    angle = np.arange(group_rows, dtype=np.float32)[:, None] * rate.astype(np.float32)[None, :]
    turn_c, turn_s = np.cos(angle), np.sin(angle)
    tables = np.concatenate([turn_c, turn_c, -turn_s, turn_s], axis=1).astype(np.float32)
    turned, index = jnp.asarray(tables), jnp.arange(group_rows, dtype=jnp.int32)[:, None]
    for doc in range(1, docs):
        moved = lax.dynamic_slice(jnp.asarray(np.concatenate([tables, tables])), (group_rows - starts[doc], 0), tables.shape)
        turned = jnp.where(index >= starts[doc], moved, turned)
    cosine, sine = turned[:, :HEAD_SIZE], turned[:, HEAD_SIZE:]

    cot_own = swap(cotangent)
    normed, qkv, scales = project(
        tokens_all, places[None], gain_one, heads_weights, gain_query, gain_key, cosine, sine, query_heads, key_heads
    )

    line_weights = gather_wide([behind(piece, qkv) for piece in feed_line])

    attended, lse = attention_forward(info, qkv, query_heads, key_heads, docs)

    hidden = gate_weight.shape[1]
    middle, normed_two, mixed = output_project(attended, places[:, None], output_weights, swapped, gain_two)
    out, normed_grad, line_grad = feed(normed_two, cot_own, line_weights)
    result, middle_grad, branch, gain_two_grad, own_grad = feed(
        normed_two, cot_own, own_weights, out, normed_grad, middle, gain_two, room=span * head_columns
    )
    line_sum = scatter_wide(line_grad)

    attended_grad, own_grad = output_back(branch, mixed, places.reshape(span, 1, rows), output_weights, own_grad)
    layer_output = swap(behind(result, attended_grad))
    [both_sum] = scatter_wide(own_grad)

    head_grads, head_gains = [], 0.0
    for kv in range(key_heads):
        if kv > 0:
            info = jnp.where(never, behind(line_sum[0], head_grads[0])[0, 0].astype(jnp.int32) + layer_output[0, 0].astype(jnp.int32), info)
        grads, gains_of = attention_backward(
            info,
            qkv,
            attended,
            attended_grad,
            lse,
            cosine,
            sine,
            scales,
            gain_query,
            gain_key,
            query_heads,
            key_heads,
            docs,
            kv,
        )
        if kv == 0:
            line_in = [
                send(behind(piece, grads), lambda pp, cc, tt: (pp, cc, tt ^ r))
                for r, piece in enumerate(line_sum, start=1)
            ]
        head_grads.append(grads)
        head_gains = head_gains + gains_of
    arrived = sum(piece[0, 0].astype(jnp.int32) for piece in line_in)
    tied = jnp.where(never, arrived, places)
    qkv_rows = [
        jnp.take(grads, places if kv + 1 < key_heads else tied, axis=0, mode="clip")
        for kv, grads in enumerate(head_grads)
    ]
    gain_rows = jnp.concatenate(
        [
            jnp.zeros((1, width), F32),
            gain_two_grad[:1],
            jnp.pad(head_gains[:2].reshape(1, 2 * HEAD_SIZE), ((0, 0), (0, width - 2 * HEAD_SIZE))),
            jnp.zeros((5, width), F32),
        ]
    )
    input_grad, heads_sum, gain_sums, output_in = last_transfers(
        pairs,
        span,
        qkv_rows,
        head_grads,
        normed,
        heads_weights,
        middle_grad,
        swapped,
        gain_one,
        gain_rows,
        both_sum,
        head_columns,
    )

    weight_grads = finish(
        both_sum,
        line_in,
        output_in,
        heads_sum,
        [x.shape for x in (query_weight, key_matrix, value_matrix, output_weight, gate_weight, up_weight, down_weight)],
        span,
        key_heads,
    )
    cut = lambda row, at, size: lax.dynamic_slice(gain_sums[row], (at + dp * size,), (size,))
    return (
        layer_output,
        input_grad,
        cut(0, 0, small),
        cut(2, 0, tiny),
        cut(2, HEAD_SIZE, tiny),
        *weight_grads[:4],
        cut(1, 0, small),
        *weight_grads[4:],
    )


def solution(mesh):
    placed = (
        P(AXES, None),
        P("dp", None),
        P("dp", None),
        P("dp"),
        P("dp"),
        P("dp"),
        P("dp", "tensor"),
        P("dp", "tensor"),
        P("dp", "tensor"),
        P("tensor", "dp"),
        P("dp"),
        P("dp", "tensor"),
        P("dp", "tensor"),
        P("tensor", "dp"),
        P(AXES, None),
    )
    return jax.shard_map(
        local,
        mesh=mesh,
        in_specs=placed,
        out_specs=(
            P(AXES, None),
            P(AXES, None),
            P("dp"),
            P("dp"),
            P("dp"),
            P("dp", "tensor"),
            P("dp", "tensor"),
            P("dp", "tensor"),
            P("tensor", "dp"),
            P("dp"),
            P("dp", "tensor"),
            P("dp", "tensor"),
            P("tensor", "dp"),
        ),
        check_vma=False,
    )
```
